32 devices in a mesh: dp: 8 (over y, x, core), mp: 4 (over z).
Axes of the slice: x: 2, y: 2, z: 4, core: 2. Of those that a mesh axis runs over, the one named last changes fastest.
Arguments:
- tokens: bfloat16 [16, 1024, 1024], P('dp', 'mp'), may hold values from -6 to 6
- cotangent: bfloat16 [16, 1024, 1024], P('dp', 'mp'), may hold values from -6 to 6
- lengths: int32 [16], P('dp'), may hold values from 102 to 1024, as said below
- buckets: int32 [1024], replicated, may hold values from 0 to 31, as said below
- step_count: int32 [1], replicated, may hold values from 1 to 5
- qkv_weight: float32 [1024, 3, 1024], P(None, None, 'mp')
- out_weight: float32 [1024, 1024], P('mp')
- up_weight: float32 [1024, 4096], P(None, 'mp')
- down_weight: float32 [4096, 1024], P('mp')
- up_bias: float32 [4096], P('mp'), may hold values from -4 to 4
- rel_bias: float32 [32, 16], P(None, 'mp'), may hold values from -6 to 6
- norm_vectors: float32 [6, 1024], replicated
- qkv_moments: float32 [2, 1024, 3, 1024], P(None, 'dp', None, 'mp'), as said below
- out_moments: float32 [2, 1024, 1024], P(None, 'mp', 'dp'), as said below
- up_moments: float32 [2, 1024, 4096], P(None, 'dp', 'mp'), as said below
- down_moments: float32 [2, 4096, 1024], P(None, 'mp', 'dp'), as said below
- bias_moments: float32 [2, 4096], P(None, 'mp'), as said below
- rel_moments: float32 [2, 32, 16], P(None, None, 'mp'), as said below
- vector_moments: float32 [2, 6, 1024], replicated, as said below
Outputs:
- block_out: bfloat16 [16, 1024, 1024], P('dp', 'mp')
- input_grad: float32 [16, 1024, 1024], P('dp', 'mp')
- qkv_new: float32 [1024, 3, 1024], P('dp', None, 'mp')
- qkv_state: float32 [2, 1024, 3, 1024], P(None, 'dp', None, 'mp')
- out_new: float32 [1024, 1024], P('mp', 'dp')
- out_state: float32 [2, 1024, 1024], P(None, 'mp', 'dp')
- up_new: float32 [1024, 4096], P('dp', 'mp')
- up_state: float32 [2, 1024, 4096], P(None, 'dp', 'mp')
- down_new: float32 [4096, 1024], P('mp', 'dp')
- down_state: float32 [2, 4096, 1024], P(None, 'mp', 'dp')
- bias_new: float32 [4096], P('mp')
- bias_state: float32 [2, 4096], P(None, 'mp')
- rel_new: float32 [32, 16], P(None, 'mp')
- rel_state: float32 [2, 32, 16], P(None, None, 'mp')
- vector_new: float32 [6, 1024], replicated
- vector_state: float32 [2, 6, 1024], replicated
- norm_values: float32 [2, 12], replicated
The draws below stay inside these ranges and needn't reach their ends.
Inputs may be any that keep to these rules, and one draw needn't show every extreme that they name: `lengths`: some sequence has all 1024 positions valid. buckets never fall with the distance, are 0 at distance 0 and 31 at distance 1024 - 1. `qkv_moments`: index 1 of the first dimension holds positive second moments. `out_moments`: index 1 of the first dimension holds positive second moments. `up_moments`: index 1 of the first dimension holds positive second moments. `down_moments`: index 1 of the first dimension holds positive second moments. `bias_moments`: index 1 of the first dimension holds positive second moments. `rel_moments`: index 1 of the first dimension holds positive second moments. `vector_moments`: index 1 of the first dimension holds positive second moments.
All inputs are finite; a program needn't handle non-finite values.
Results may differ from the reference program's by a relative error of at most 0.017.
Values may be sent and summed in bfloat16 or wider, within the bound.
No kernel may reach another device: no remote copies, remote signals or barrier semaphores. Data moves between devices by JAX's collectives and lax.ppermute only.
A program may use at most 192 MiB of HBM per device.

```python
import math
import jax
import jax.numpy as jnp
from jax import lax

D = 1024
H = 16
HD = 64
FF = 4096
NB = 32
SEQ = 1024
BATCH = 16
N_MP = 4


def draw_lengths(key, part):
    drawn_len = jax.random.randint(key, (BATCH,), max(1, SEQ // 10), SEQ + 1)
    return drawn_len.at[0].set(SEQ).astype(jnp.int32)


def draw_buckets(key, part):
    steps_up = jax.random.randint(key, (SEQ,), 0, 2).at[0].set(0)
    climbed = jnp.minimum(jnp.cumsum(steps_up), NB - 1)
    return climbed.at[SEQ - 1].set(NB - 1).astype(jnp.int32)


def ramp_scale(count):
    spread = 3.0
    places = jnp.arange(count, dtype=jnp.float32) / max(count - 1, 1)
    return jnp.exp(math.log(spread) * (places - 0.5))


def ramped_normal(key, shape, fan_in, ramp_dim):
    values = jnp.clip(jax.random.normal(key, shape, jnp.float32), -6.0, 6.0) * fan_in ** (-0.5)
    ramp = ramp_scale(shape[ramp_dim])
    view = [1] * len(shape)
    view[ramp_dim] = shape[ramp_dim]
    return values * ramp.reshape(view)


def draw_qkv_weight(key, part):
    return ramped_normal(jax.random.fold_in(key, 31), (D, 3, H * HD), D, 0)


def draw_out_weight(key, part):
    return ramped_normal(jax.random.fold_in(key, 32), (H * HD, D), HD, 1)


def draw_up_weight(key, part):
    return ramped_normal(jax.random.fold_in(key, 33), (D, FF), D, 0)


def draw_down_weight(key, part):
    return ramped_normal(jax.random.fold_in(key, 34), (FF, D), FF, 1)


def draw_norm_vectors(key, part):
    gain_key, shift_key = jax.random.split(jax.random.fold_in(key, 11))
    gain_rows = 1.0 + 0.3 * jax.random.uniform(gain_key, (2, D), jnp.float32, -1.0, 1.0)
    shifts = 0.3 * jax.random.normal(shift_key, (4, D), jnp.float32)
    return jnp.stack([gain_rows[0], shifts[0], gain_rows[1], shifts[1], shifts[2], shifts[3]])


def token_root():
    return math.sqrt(BATCH * SEQ / 2.0)


def moment_pair(key, shape, grad_size):
    first_key, second_key = jax.random.split(key)
    first_vals = jax.random.normal(first_key, shape, jnp.float32) * (0.111 * grad_size)
    second_vals = jnp.exp(jax.random.uniform(second_key, shape, jnp.float32, 0.0, math.log(4.0))) * (0.001 * grad_size * grad_size)
    return jnp.stack([first_vals, second_vals])


def draw_qkv_moments(key, part):
    return moment_pair(jax.random.fold_in(key, 21), (D, 3, H * HD), 0.1 * token_root())


def draw_out_moments(key, part):
    return moment_pair(jax.random.fold_in(key, 22), (H * HD, D), 0.3 * token_root())


def draw_up_moments(key, part):
    return moment_pair(jax.random.fold_in(key, 23), (D, FF), 0.3 * token_root())


def draw_down_moments(key, part):
    return moment_pair(jax.random.fold_in(key, 24), (FF, D), 0.6 * token_root())


def draw_bias_moments(key, part):
    return moment_pair(jax.random.fold_in(key, 25), (FF,), 0.3 * token_root())


def draw_rel_moments(key, part):
    return moment_pair(jax.random.fold_in(key, 26), (NB, H), 0.0045 * math.sqrt(BATCH * SEQ))


def draw_vector_moments(key, part):
    return moment_pair(jax.random.fold_in(key, 27), (6, D), token_root())


def shard_levels(key, extent, shards, low, high):
    loudness = 1.0
    for axis_at, shards_of in shards:
        steps = jax.random.uniform(jax.random.fold_in(jax.random.fold_in(key, 6), axis_at), (shards_of,), jnp.float32, low / len(shards), high / len(shards))
        loudness = loudness * jnp.repeat(jnp.exp(steps), extent[axis_at] // shards_of).reshape((-1,) + (1,) * (len(extent) - 1 - axis_at))
    return loudness


def bell_draw(own_key, dims, deviation, reach, cuts=(), held_as=jnp.bfloat16):
    result = jax.random.normal(own_key, dims, jnp.float32) * deviation
    if len(cuts) > 0:
        result = shard_levels(own_key, dims, cuts, -0.22, 0.18) * result
    return jnp.clip(result, min=-reach, max=reach).astype(held_as)


def setup_inputs(seed: int = 0) -> dict:
    streams_of = jax.random.split(jax.random.key(seed), 20)
    tokens = bell_draw(streams_of[0], (BATCH, SEQ, D), 1.0, 6.0, ((0, 8), (1, 4)))
    cotangent = bell_draw(streams_of[1], (BATCH, SEQ, D), 1.0, 6.0, ((0, 8), (1, 4)))
    lengths = draw_lengths(jax.random.fold_in(streams_of[19], 71), 0)
    buckets = draw_buckets(jax.random.fold_in(streams_of[19], 71), 0)
    step_count = jax.random.randint(streams_of[4], (1,), 1, 6).astype(jnp.int32)
    qkv_weight = draw_qkv_weight(jax.random.fold_in(streams_of[19], 71), 0)
    out_weight = draw_out_weight(jax.random.fold_in(streams_of[19], 71), 0)
    up_weight = draw_up_weight(jax.random.fold_in(streams_of[19], 71), 0)
    down_weight = draw_down_weight(jax.random.fold_in(streams_of[19], 71), 0)
    up_bias = bell_draw(streams_of[9], (FF,), 0.3, 4.0, ((0, 4),), jnp.float32)
    rel_bias = bell_draw(streams_of[10], (NB, H), 1.0, 6.0, ((1, 4),), jnp.float32)
    norm_vectors = draw_norm_vectors(jax.random.fold_in(streams_of[19], 71), 0)
    qkv_moments = draw_qkv_moments(jax.random.fold_in(streams_of[19], 71), 0)
    out_moments = draw_out_moments(jax.random.fold_in(streams_of[19], 71), 0)
    up_moments = draw_up_moments(jax.random.fold_in(streams_of[19], 71), 0)
    down_moments = draw_down_moments(jax.random.fold_in(streams_of[19], 71), 0)
    bias_moments = draw_bias_moments(jax.random.fold_in(streams_of[19], 71), 0)
    rel_moments = draw_rel_moments(jax.random.fold_in(streams_of[19], 71), 0)
    vector_moments = draw_vector_moments(jax.random.fold_in(streams_of[19], 71), 0)
    return dict(tokens=tokens, cotangent=cotangent, lengths=lengths, buckets=buckets, step_count=step_count, qkv_weight=qkv_weight, out_weight=out_weight, up_weight=up_weight, down_weight=down_weight, up_bias=up_bias, rel_bias=rel_bias, norm_vectors=norm_vectors, qkv_moments=qkv_moments, out_moments=out_moments, up_moments=up_moments, down_moments=down_moments, bias_moments=bias_moments, rel_moments=rel_moments, vector_moments=vector_moments)


@jax.custom_vjp
def low(v):
    return lax.optimization_barrier(v.astype(jnp.bfloat16)).astype(jnp.float32)

@jax.custom_vjp
def low_back(v):
    return v

def low_keep(v):
    return (low(v), None)

def low_pass(kept, grad):
    return (grad,)

def back_keep(v):
    return (v, None)

def back_low(kept, grad):
    return (low(grad),)
low.defvjp(low_keep, low_pass)
low_back.defvjp(back_keep, back_low)
norm_eps = 1e-05
adam_eps = 1e-06
learn_rate = 0.25
weight_decay = 0.1

def layer_norm(values, gain_vec, shift_vec):
    center = values - lax.optimization_barrier(jnp.mean(values, axis=-1, keepdims=True))
    spread = lax.optimization_barrier(jnp.mean(center * center, axis=-1, keepdims=True))
    return center * lax.rsqrt(spread + norm_eps) * gain_vec + shift_vec

def seq_forward(params, inputs, length, buckets):
    qkv_weight, out_weight, up_weight, down_weight, up_bias, rel_bias, norm_vectors = params
    places = jnp.arange(SEQ, dtype=jnp.int32)
    row_mask = (places < length).astype(jnp.float32)[:, None]
    distance = places[:, None] - places[None, :]
    allowed = (distance >= 0) & (places[None, :] < length)
    bucket_grid = buckets[jnp.clip(distance, 0, SEQ - 1)]
    group_heads = H // N_MP
    group_width = group_heads * HD
    group_units = FF // N_MP
    score_scale = HD ** (-0.5)
    first_normed = low(layer_norm(inputs, norm_vectors[0], norm_vectors[1]))
    mixed_sum = jnp.zeros((SEQ, D), jnp.float32)
    for group_idx in range(N_MP):
        head_cols = slice(group_idx * group_width, (group_idx + 1) * group_width)
        head_ids = slice(group_idx * group_heads, (group_idx + 1) * group_heads)
        shared = low_back(first_normed)
        weight_group = low(qkv_weight[:, :, head_cols]).reshape(D, 3 * group_width)
        projected = low_back(low(jnp.dot(shared, weight_group, precision=lax.Precision.HIGHEST)))
        projected = projected.reshape(SEQ, 3, group_heads, HD)
        queries, key_vecs, value_vecs = (projected[:, 0], projected[:, 1], projected[:, 2])
        bias_grid = jnp.moveaxis(jnp.take(rel_bias[:, head_ids], bucket_grid, axis=0), 2, 0)
        scores = jnp.einsum('qhd,khd->hqk', queries, key_vecs, precision=lax.Precision.HIGHEST) * score_scale + bias_grid
        scores = jnp.where(allowed[None], low_back(scores), -1000000000.0)
        weights_soft = low(jax.nn.softmax(scores, axis=-1))
        context = jnp.einsum('hqk,khd->qhd', weights_soft, value_vecs, precision=lax.Precision.HIGHEST)
        context = low_back(low(context.reshape(SEQ, group_width)))
        partial_out = jnp.dot(context, low(out_weight[head_cols]), precision=lax.Precision.HIGHEST) * row_mask
        mixed_sum = mixed_sum + low(partial_out)
    branch = low_back((mixed_sum + norm_vectors[4]) * row_mask)
    middle = inputs + branch
    second_normed = low(layer_norm(middle, norm_vectors[2], norm_vectors[3]))
    fed_sum = jnp.zeros((SEQ, D), jnp.float32)
    for group_idx in range(N_MP):
        unit_cols = slice(group_idx * group_units, (group_idx + 1) * group_units)
        shared = low_back(second_normed)
        hidden_pre = jnp.dot(shared, low(up_weight[:, unit_cols]), precision=lax.Precision.HIGHEST) + up_bias[unit_cols]
        hidden_pre = low_back(hidden_pre)
        hidden_act = low(jax.nn.gelu(hidden_pre, approximate=False))
        partial_out = jnp.dot(hidden_act, low(down_weight[unit_cols]), precision=lax.Precision.HIGHEST) * row_mask
        fed_sum = fed_sum + low(partial_out)
    return middle + low_back((fed_sum + norm_vectors[5]) * row_mask)

def adjust(weight, moments, gradient, decay_rate, first_fix, second_fix):
    first_new = 0.9 * moments[0] + 0.1 * gradient
    second = 0.999 * moments[1] + 0.001 * gradient * gradient
    update = first_new / first_fix / (jnp.sqrt(second / second_fix) + adam_eps) + decay_rate * weight
    return (first_new, second, update)

def reference(tokens, cotangent, lengths, buckets, step_count, qkv_weight, out_weight, up_weight, down_weight, up_bias, rel_bias, norm_vectors, qkv_moments, out_moments, up_moments, down_moments, bias_moments, rel_moments, vector_moments):
    params = (qkv_weight, out_weight, up_weight, down_weight, up_bias, rel_bias, norm_vectors)

    def one_sequence(totals, bundle):
        inputs, incoming, length = bundle
        output, pullback = jax.vjp(lambda weights, values: seq_forward(weights, values, length, buckets), params, inputs.astype(jnp.float32))
        gradients, in_grad = pullback(incoming.astype(jnp.float32))
        return (jax.tree.map(jnp.add, totals, gradients), (output.astype(jnp.bfloat16), in_grad))
    totals, (block_out, input_grad) = lax.scan(one_sequence, jax.tree.map(jnp.zeros_like, params), (tokens, cotangent, lengths))
    steps_done = step_count[0].astype(jnp.float32)
    first_fix = 1.0 - jnp.power(jnp.float32(0.9), steps_done)
    second_fix = 1.0 - jnp.power(jnp.float32(0.999), steps_done)
    moments_all = (qkv_moments, out_moments, up_moments, down_moments, bias_moments, rel_moments, vector_moments)
    decays = (weight_decay, weight_decay, weight_decay, weight_decay, 0.0, 0.0, 0.0)
    results = [adjust(params[index], moments_all[index], totals[index], decays[index], first_fix, second_fix) for index in range(7)]
    weight_norms = [jnp.sqrt(jnp.sum(params[index] * params[index])) for index in range(6)]
    update_norms = [jnp.sqrt(jnp.sum(results[index][2] * results[index][2])) for index in range(6)]
    weight_norm = jnp.concatenate([jnp.stack(weight_norms), jnp.sqrt(lax.optimization_barrier(jnp.sum(norm_vectors * norm_vectors, axis=1)))])
    update_norm = jnp.concatenate([jnp.stack(update_norms), jnp.sqrt(lax.optimization_barrier(jnp.sum(results[6][2] * results[6][2], axis=1)))])
    trust_ratio = weight_norm / (update_norm + adam_eps)
    outputs = [block_out, input_grad]
    for index in range(6):
        outputs.append(params[index] - learn_rate * trust_ratio[index] * results[index][2])
        outputs.append(jnp.stack([results[index][0], results[index][1]]))
    outputs.append(norm_vectors - learn_rate * trust_ratio[6:][:, None] * results[6][2])
    outputs.append(jnp.stack([results[6][0], results[6][1]]))
    outputs.append(jnp.stack([weight_norm, update_norm]))
    return (outputs[0], outputs[1], outputs[2], outputs[3], outputs[4], outputs[5], outputs[6], outputs[7], outputs[8], outputs[9], outputs[10], outputs[11], outputs[12], outputs[13], outputs[14], outputs[15], outputs[16])
```

```python
import jax
import jax.numpy as jnp
from jax import lax
from jax.experimental import pallas as pl
from jax.experimental.pallas import tpu as pltpu
from jax.sharding import PartitionSpec as P

HD = 64
f32 = jnp.float32
bf16 = jnp.bfloat16

norm_eps = 1e-05
adam_eps = 1e-06
learn_rate = 0.25
weight_decay = 0.1
masked_score = -1000000000.0
score_scale = HD ** (-0.5)
kernel_bytes = 48 << 20

in_vmem = pl.BlockSpec(memory_space=pltpu.VMEM)
in_smem = pl.BlockSpec(memory_space=pltpu.SMEM)


def dot_nt(left, right):
    return lax.dot_general(left, right, (((1,), (1,)), ((), ())), preferred_element_type=f32)


def dot_nn(left, right):
    return lax.dot_general(left, right, (((1,), (0,)), ((), ())), preferred_element_type=f32)


def dot_tn(left, right):
    return lax.dot_general(left, right, (((0,), (0,)), ((), ())), preferred_element_type=f32)


def tile_of(rows):
    return min(256, rows)


def bias_tiles(line_ref, head, tiles, tile):
    causal = lax.broadcasted_iota(jnp.int32, (tile, tile), 0) <= lax.broadcasted_iota(
        jnp.int32, (tile, tile), 1
    )
    made = []
    for kk in range(tiles):
        line = line_ref[head : head + 1, kk * 2 * tile : (kk + 1) * 2 * tile]
        wide = jnp.broadcast_to(line, (tile, 2 * tile))
        made.append(pltpu.roll(wide, tile, 1, stride=1, stride_axis=0)[:, :tile])
    made[0] = jnp.where(causal, made[0], masked_score)
    return made


def scores_of(keys, query, toeplitz, block, tile, key_pos, length):
    count = (block + 1) * tile
    raw = dot_nt(keys[:count], query)
    raw = raw + jnp.concatenate([toeplitz[block - j] for j in range(block + 1)], axis=0)
    return jnp.where(key_pos[:count] < length, raw, masked_score)


def attend_kernel(heads, length_ref, qkv_ref, line_ref, ctx_ref, lse_ref):
    rows = qkv_ref.shape[0]
    tile = tile_of(rows)
    tiles = rows // tile
    width = heads * HD
    length = length_ref[0]
    key_pos = lax.broadcasted_iota(jnp.int32, (rows, tile), 0)
    for head in range(heads):
        toeplitz = bias_tiles(line_ref, head, tiles, tile)
        cols = slice(head * HD, (head + 1) * HD)
        keys = qkv_ref[:, width + head * HD : width + (head + 1) * HD]
        vals = qkv_ref[:, 2 * width + head * HD : 2 * width + (head + 1) * HD]
        for block in range(tiles):
            here = slice(block * tile, (block + 1) * tile)
            count = (block + 1) * tile
            query = qkv_ref[here, cols] * jnp.asarray(score_scale, bf16)
            raw = scores_of(keys, query, toeplitz, block, tile, key_pos, length)
            top = jnp.max(raw, axis=0, keepdims=True)
            grown = jnp.exp(raw - top)
            total = jnp.sum(grown, axis=0, keepdims=True)
            probs = (grown * (1.0 / total)).astype(bf16)
            ctx_ref[here, cols] = dot_tn(probs, vals[:count]).astype(bf16)
            lse_ref[head : head + 1, here] = top + jnp.log(total)


def attend_back_kernel(
    heads,
    length_ref,
    qkv_ref,
    line_ref,
    lse_ref,
    grad_ref,
    out_ref,
    dist_ref,
    key_acc,
    val_acc,
    diag_acc,
):
    rows = qkv_ref.shape[0]
    tile = tile_of(rows)
    tiles = rows // tile
    width = heads * HD
    length = length_ref[0]
    key_pos = lax.broadcasted_iota(jnp.int32, (rows, tile), 0)
    for head in range(heads):
        toeplitz = bias_tiles(line_ref, head, tiles, tile)
        cols = slice(head * HD, (head + 1) * HD)
        key_cols = slice(width + head * HD, width + (head + 1) * HD)
        val_cols = slice(2 * width + head * HD, 2 * width + (head + 1) * HD)
        keys = qkv_ref[:, key_cols]
        vals = qkv_ref[:, val_cols]
        key_acc[...] = jnp.zeros_like(key_acc)
        val_acc[...] = jnp.zeros_like(val_acc)
        diag_acc[...] = jnp.zeros_like(diag_acc)
        for block in range(tiles):
            here = slice(block * tile, (block + 1) * tile)
            count = (block + 1) * tile
            query = qkv_ref[here, cols] * jnp.asarray(score_scale, bf16)
            grad = grad_ref[here, cols]
            raw = scores_of(keys, query, toeplitz, block, tile, key_pos, length)
            probs = jnp.exp(raw - lse_ref[head : head + 1, here])
            pgrad = dot_nt(vals[:count], grad)
            drop = jnp.sum(probs * pgrad, axis=0, keepdims=True)
            sgrad = (probs * (pgrad - drop)).astype(bf16)
            val_acc[:count] += dot_nn(probs.astype(bf16), grad)
            key_acc[:count] += dot_nn(sgrad, query)
            out_ref[here, cols] = (dot_tn(sgrad, keys[:count]) * score_scale).astype(bf16)
            wide = sgrad.astype(f32)
            for j in range(block + 1):
                diag_acc[block - j] += wide[j * tile : (j + 1) * tile]
        out_ref[:, key_cols] = key_acc[...].astype(bf16)
        out_ref[:, val_cols] = val_acc[...].astype(bf16)
        for kk in range(tiles):
            held = jnp.concatenate([diag_acc[kk], jnp.zeros((tile, tile), f32)], axis=1)
            half = tile // 2
            while half >= 1:
                held = held[:half] + pltpu.roll(held[half : 2 * half], 2 * tile - half, 1)
                half //= 2
            dist_ref[head : head + 1, kk * 2 * tile : (kk + 1) * 2 * tile] = pltpu.roll(held, tile, 1)


def attend(length, qkv, line, heads):
    rows = qkv.shape[0]
    return pl.pallas_call(
        lambda *refs: attend_kernel(heads, *refs),
        out_shape=(
            jax.ShapeDtypeStruct((rows, heads * HD), bf16),
            jax.ShapeDtypeStruct((heads, rows), f32),
        ),
        in_specs=[in_smem, in_vmem, in_vmem],
        out_specs=(in_vmem, in_vmem),
        compiler_params=pltpu.CompilerParams(vmem_limit_bytes=kernel_bytes),
        cost_estimate=pl.CostEstimate(
            flops=heads * rows * rows * HD * 32,
            bytes_accessed=4 << 20,
            transcendentals=heads * rows * rows,
        ),
        name="attend",
    )(length, qkv, line)


def attend_back(length, qkv, line, lse, grad, heads):
    rows = qkv.shape[0]
    tile = tile_of(rows)
    return pl.pallas_call(
        lambda *refs: attend_back_kernel(heads, *refs),
        out_shape=(
            jax.ShapeDtypeStruct((rows, 3 * heads * HD), bf16),
            jax.ShapeDtypeStruct((heads, 2 * rows), f32),
        ),
        in_specs=[in_smem, in_vmem, in_vmem, in_vmem, in_vmem],
        out_specs=(in_vmem, in_vmem),
        scratch_shapes=[
            pltpu.VMEM((rows, HD), f32),
            pltpu.VMEM((rows, HD), f32),
            pltpu.VMEM((rows // tile, tile, tile), f32),
        ],
        compiler_params=pltpu.CompilerParams(vmem_limit_bytes=kernel_bytes),
        cost_estimate=pl.CostEstimate(
            flops=heads * rows * rows * HD * 64,
            bytes_accessed=4 << 20,
            transcendentals=heads * rows * rows,
        ),
        name="attend_back",
    )(length, qkv, line, lse, grad)


class Places:
    def __init__(self, per):
        self.per = per
        self.dp_n = lax.axis_size("dp")
        self.mp_n = lax.axis_size("mp")
        self.q_n = self.dp_n // 2
        self.slots = 2 * per
        self.t_n = self.mp_n // self.slots
        assert self.dp_n % 2 == 0 and self.mp_n % self.slots == 0
        dp_i = lax.axis_index("dp")
        mp_i = lax.axis_index("mp")
        self.dp_i, self.mp_i = dp_i, mp_i
        self.q, self.c = dp_i // 2, lax.rem(dp_i, 2)
        self.s, self.t = mp_i // self.t_n, lax.rem(mp_i, self.t_n)
        self.home = self.s // per
        self.at_home = self.c == self.home
        self.q_bits = []
        while (1 << len(self.q_bits)) < self.q_n:
            self.q_bits.append(1 << len(self.q_bits))
        assert (1 << len(self.q_bits)) == self.q_n

    def move(self, values, target):
        pairs = []
        for q in range(self.q_n):
            for c in range(2):
                for s in range(self.slots):
                    for t in range(self.t_n):
                        found = target(q, c, s, t)
                        if found is not None:
                            nq, nc, ns, nt = found
                            pairs.append(
                                (
                                    (q * 2 + c) * self.mp_n + s * self.t_n + t,
                                    (nq * 2 + nc) * self.mp_n + ns * self.t_n + nt,
                                )
                            )
        return lax.ppermute(values, ("dp", "mp"), pairs)

    def to_core(self, values):
        return self.move(values, lambda q, c, s, t: (q, 1 - c, s, t))

    def to_slot(self, values, step):
        return self.move(values, lambda q, c, s, t: (q, c, (s + step) % self.slots, t))

    def to_chip(self, values, bit):
        return self.move(values, lambda q, c, s, t: (q ^ bit, c, s, t))

    def to_team(self, values, step):
        return self.move(values, lambda q, c, s, t: (q, c, s, (t + step) % self.t_n))

    def relative(self, values, dim):
        size = values.shape[dim] // self.q_n
        return jnp.concatenate(
            [
                lax.dynamic_slice_in_dim(values, (self.q ^ k) * size, size, dim)
                for k in range(self.q_n)
            ],
            axis=dim,
        )

    def block_at(self, step):
        return lax.rem(self.s + step, self.slots) * self.t_n + self.t

    def collect(self, local):
        count, width = local.shape[1:]
        whole = jnp.zeros((count * self.mp_n, width), local.dtype)
        for step in range(self.slots):
            slot = lax.rem(self.s + step, self.slots)
            piece = lax.dynamic_index_in_dim(
                local, jnp.clip(slot - self.per * self.c, 0, self.per - 1), 0, keepdims=False
            )
            if step > 0:
                piece = self.move(
                    piece,
                    lambda q, c, s, t: (
                        (q, c, (s + step) % self.slots, t)
                        if (s + step) % self.slots // self.per == c
                        else None
                    ),
                )
            other = self.move(
                piece, lambda q, c, s, t: (q, 1 - c, s, t) if c == s // self.per else None
            )
            piece = jnp.where(self.at_home, piece, other)
            origin = lax.rem(self.s + self.slots - step, self.slots)
            for turn in range(self.t_n):
                got = self.to_team(piece, turn) if turn > 0 else piece
                from_t = lax.rem(self.t + self.t_n - turn, self.t_n)
                whole = lax.dynamic_update_slice_in_dim(
                    whole, got, (origin * self.t_n + from_t) * count, 0
                )
        return whole

    def deliver(self, blocks):
        arrived = []
        for step in range(self.slots):
            flip, index = step // self.per, step % self.per
            value = blocks[index]
            if step > 0:
                value = self.move(
                    value,
                    lambda q, c, s, t: (
                        (q, s // self.per, (s + step) % self.slots, t)
                        if c == (s // self.per) ^ flip
                        else None
                    ),
                )
            arrived.append(value)
        results = []
        for index in range(self.per):
            slot = self.per * self.c + index
            step = lax.rem(self.s + self.slots - slot, self.slots)
            picked = arrived[0]
            for number in range(1, self.slots):
                picked = jnp.where(step == number, arrived[number], picked)
            results.append(picked)
        return jnp.stack(results)

    def share(self, values, length, flip, team):
        side = jnp.where(self.at_home, 0, 1) ^ flip
        parts = []
        for index in range(self.per):
            slot = lax.rem(self.s + self.per * side + index, self.slots)
            block = slot * self.t_n + lax.rem(self.t + team, self.t_n)
            parts.append(lax.dynamic_slice_in_dim(values, block * length, length, 0))
        return jnp.concatenate(parts, axis=0)

    def sum_share(self, partial, length):
        total = self.share(partial, length, 0, 0).astype(f32)
        for team in range(self.t_n):
            for flip in (0, 1):
                if (team, flip) != (0, 0):
                    sent = self.share(partial, length, flip, team).astype(bf16)
                    total = total + self.move(
                        sent, lambda q, c, s, t: (q, c ^ flip, s, (t + team) % self.t_n)
                    ).astype(f32)
        return total

    def sum_team(self, partial):
        total = partial.astype(f32)
        total = total + self.to_core(partial).astype(f32)
        if self.t_n > 1:
            low = total.astype(bf16)
            for team in range(1, self.t_n):
                total = total + self.to_team(low, team).astype(f32)
        return total

    def gather_chips(self, piece, first_bit):
        bits = self.q_bits if first_bit == 0 else self.q_bits[::-1]
        pieces = {0: piece}
        for bit in bits:
            for k in list(pieces):
                pieces[k | bit] = self.to_chip(pieces[k], bit)
        return jnp.concatenate([pieces[k] for k in range(self.q_n)], axis=0)

    def scatter_chips(self, values, first_bit):
        count = values.shape[0] // self.q_n
        bits = self.q_bits if first_bit == 0 else self.q_bits[::-1]
        pieces = {k: values[k * count : (k + 1) * count] for k in range(self.q_n)}
        for number, bit in enumerate(bits):
            last = number == len(bits) - 1
            for k in [k for k in pieces if k & bit]:
                got = self.to_chip(pieces.pop(k).astype(bf16), bit).astype(f32)
                pieces[k ^ bit] = pieces[k ^ bit].astype(f32) + got
        return pieces[0]

    def sum_all(self, values, chips_only=False):
        if not chips_only:
            values = values + self.to_core(values)
        for low in range(0, len(self.q_bits), 2):
            bits = self.q_bits[low : low + 2]
            got = [self.to_chip(values, bit) for bit in bits]
            if len(bits) == 2:
                both = self.to_chip(values, bits[0] | bits[1])
                values = (values + got[0]) + (got[1] + both)
            else:
                values = values + got[0]
        if not chips_only:
            bit, bits = 1, []
            while bit < self.mp_n:
                bits.append(bit)
                bit *= 2
            flip = lambda mask: self.move(
                values,
                lambda q, c, s, t: (
                    q,
                    c,
                    ((s * self.t_n + t) ^ mask) // self.t_n,
                    ((s * self.t_n + t) ^ mask) % self.t_n,
                ),
            )
            for low in range(0, len(bits), 2):
                pair = bits[low : low + 2]
                if len(pair) == 2:
                    one, two, both = flip(pair[0]), flip(pair[1]), flip(pair[0] | pair[1])
                    values = (values + one) + (two + both)
                else:
                    values = values + flip(pair[0])
        return values


def norm_parts(values):
    center = values - jnp.mean(values, axis=-1, keepdims=True)
    spread = jnp.mean(center * center, axis=-1, keepdims=True)
    inverse = lax.rsqrt(spread + norm_eps)
    return (center * inverse, inverse)


def norm_back(upstream, normed, inverse, gain_vec):
    scaled = upstream * gain_vec
    return inverse * (
        scaled
        - jnp.mean(scaled, axis=-1, keepdims=True)
        - normed * jnp.mean(scaled * normed, axis=-1, keepdims=True)
    )


def adjust(weight, first, second, gradient, decay_rate, first_fix, second_fix):
    first_new = 0.9 * first + 0.1 * gradient
    second_new = 0.999 * second + 0.001 * gradient * gradient
    update = (
        first_new / first_fix / (jnp.sqrt(second_new / second_fix) + adam_eps) + decay_rate * weight
    )
    return (first_new, second_new, update)


def gelu_parts(values):
    half = 0.5 * (1.0 + lax.erf(values * (0.5**0.5)))
    bell = jnp.exp(-0.5 * values * values) * 0.3989422804014327
    return (values * half, half + values * bell)


def local(
    tokens,
    cotangent,
    lengths,
    buckets,
    step_count,
    qkv_weight,
    out_weight,
    up_weight,
    down_weight,
    up_bias,
    rel_bias,
    norm_vectors,
    qkv_moments,
    out_moments,
    up_moments,
    down_moments,
    bias_moments,
    rel_moments,
    vector_moments,
):
    per, length_rows, width = tokens.shape
    at = Places(per)
    seq_len = length_rows * at.mp_n
    blocks = at.slots
    q_n, c, q = at.q_n, at.c, at.q
    head_width = out_weight.shape[0] // 2
    heads = head_width // HD
    units = up_weight.shape[1] // 2
    bucket_count, local_heads = rel_bias.shape

    inputs_low = at.collect(at.relative(tokens, 2))
    all_lengths = lengths
    length_grid = at.move(
        all_lengths, lambda q, c, s, t: (q, 1 - c, s, t)
    )
    four = jnp.where(
        c == 0,
        jnp.concatenate([all_lengths, length_grid]),
        jnp.concatenate([length_grid, all_lengths]),
    )
    length = lax.dynamic_slice_in_dim(four, at.s, 1, 0)
    row_keep = jnp.arange(seq_len)[:, None] < length[0]
    row_mask = row_keep.astype(f32)
    vectors = at.relative(norm_vectors, 1)

    def half(values, dim, size):
        return lax.dynamic_slice_in_dim(values, c * size, size, dim)

    attn_own = at.relative(
        jnp.concatenate(
            [
                half(qkv_weight, 2, head_width).reshape(width, 3 * head_width).astype(bf16),
                half(out_weight, 0, head_width).astype(bf16).T,
            ],
            axis=1,
        ),
        0,
    )
    up_own = at.relative(half(up_weight, 1, units).astype(bf16), 0)
    down_own = at.relative(half(down_weight, 0, units).astype(bf16).T, 0)
    part = width // q_n
    small_own = jnp.concatenate(
        [half(up_bias, 0, units), half(rel_bias, 1, heads).T.reshape(-1)]
    )
    attn_w, up_w, down_w, small = [attn_own], [up_own], [down_own], [small_own]
    for step in range(1, blocks):
        small.append(at.to_slot(small_own, step))
        piece = at.to_slot(attn_own[:part], step)
        attn_w.append(at.gather_chips(piece, step % 2))
    for step in range(1, blocks):
        piece = at.to_slot(up_own[:part], step)
        up_w.append(at.gather_chips(piece, 0))
        piece = at.to_slot(down_own[:part], step)
        down_w.append(at.gather_chips(piece, 1))
    qkv_w = [values[:, : 3 * head_width] for values in attn_w]
    out_w = [values[:, 3 * head_width :] for values in attn_w]

    tile = tile_of(seq_len)
    tiles = seq_len // tile
    padded = jnp.concatenate([jnp.zeros((tile,), jnp.int32), buckets])
    spread = jnp.concatenate(
        [padded[kk * tile : (kk + 2) * tile] for kk in range(tiles)]
    )
    choose = (jnp.arange(bucket_count, dtype=jnp.int32)[:, None] == spread[None, :]).astype(f32)
    rel_rows = jnp.concatenate(
        [values[units:].reshape(heads, bucket_count) for values in small], axis=0
    )
    lines = jnp.dot(rel_rows, choose, precision=lax.Precision.HIGHEST)

    inputs = inputs_low.astype(f32)
    first_normed, first_inverse = norm_parts(inputs)
    first_low = (first_normed * vectors[0] + vectors[1]).astype(bf16)
    qkv, contexts, totals = [], [], []
    for r in range(blocks):
        qkv.append(dot_nn(first_low, qkv_w[r]).astype(bf16))
        context, total = attend(length, qkv[r], lines[r * heads : (r + 1) * heads], heads)
        contexts.append(context)
        totals.append(total)
    mixed = dot_nt(contexts[0], out_w[0])
    for r in range(1, blocks):
        mixed = mixed + dot_nt(contexts[r], out_w[r])
    mixed = at.sum_team(jnp.where(row_keep, mixed, 0.0).astype(bf16))
    middle = inputs + (mixed + vectors[4]) * row_mask
    second_normed, second_inverse = norm_parts(middle)
    second_low = (second_normed * vectors[2] + vectors[3]).astype(bf16)
    acts, slopes = [], []
    for r in range(blocks):
        pre = dot_nn(second_low, up_w[r]) + small[r][:units]
        act, slope = gelu_parts(pre)
        acts.append(act.astype(bf16))
        slopes.append(slope)
    fed = dot_nt(acts[0], down_w[0])
    for r in range(1, blocks):
        fed = fed + dot_nt(acts[r], down_w[r])
    fed_share = at.sum_share(fed.astype(bf16), length_rows)
    middle_share = at.share(middle, length_rows, 0, 0)
    mask_share = at.share(row_mask, length_rows, 0, 0)
    out_share = (middle_share + (fed_share + vectors[5]) * mask_share).astype(bf16)
    block_out = at.deliver(
        [out_share[i * length_rows : (i + 1) * length_rows] for i in range(per)]
    )
    block_out = at.relative(block_out, 2)

    incoming_low = at.collect(at.relative(cotangent, 2))
    kept = jnp.where(row_keep, incoming_low, jnp.zeros_like(incoming_low))
    fed_bias_grad = jnp.sum(kept.astype(f32), axis=0)
    back = None
    mlp_grads, bias_grads = [], []
    for r in range(blocks):
        down_grad = dot_tn(kept, acts[r]).astype(bf16)
        pre_low = (dot_nn(kept, down_w[r]) * slopes[r]).astype(bf16)
        bias_grads.append(jnp.sum(pre_low.astype(f32), axis=0))
        up_grad = dot_tn(second_low, pre_low).astype(bf16)
        term = dot_nt(pre_low, up_w[r])
        back = term if back is None else back + term
        mlp_grads.append((up_grad, down_grad))
    second_grad = at.sum_team(back.astype(bf16))
    lead = jnp.where((c == 0) & (at.t == 0), 1.0, 0.0)
    gain_two = jnp.sum(second_grad * second_normed, axis=0)
    shift_two = jnp.sum(second_grad, axis=0)
    middle_grad = incoming_low.astype(f32) + norm_back(
        second_grad, second_normed, second_inverse, vectors[2]
    )
    branch = jnp.where(row_keep, middle_grad, 0.0).astype(bf16)
    mix_bias_grad = jnp.sum(branch.astype(f32), axis=0)
    back = None
    attn_grads, rel_grads = [], []
    for r in range(blocks):
        context_grad = dot_nn(branch, out_w[r]).astype(bf16)
        proj_grad, dist = attend_back(
            length, qkv[r], lines[r * heads : (r + 1) * heads], totals[r], context_grad, heads
        )
        rel_grads.append(dist)
        qkv_grad = dot_tn(first_low, proj_grad).astype(bf16)
        out_grad = dot_tn(branch, contexts[r]).astype(bf16)
        attn_grads.append((qkv_grad, out_grad))
        term = dot_nt(proj_grad, qkv_w[r])
        back = term if back is None else back + term
    rel_grad = lax.dot_general(
        jnp.concatenate(rel_grads, axis=0),
        choose,
        (((1,), (1,)), ((), ())),
        precision=lax.Precision.HIGHEST,
    )
    first_grad = at.sum_share(back.astype(bf16), length_rows)
    normed_share = at.share(first_normed, length_rows, 0, 0)
    inverse_share = at.share(first_inverse, length_rows, 0, 0)
    middle_grad_share = at.share(middle_grad, length_rows, 0, 0)
    gain_one = jnp.sum(first_grad * normed_share, axis=0)
    shift_one = jnp.sum(first_grad, axis=0)
    input_share = middle_grad_share + norm_back(
        first_grad, normed_share, inverse_share, vectors[0]
    )
    input_share = input_share.astype(bf16)
    input_grad = at.deliver(
        [input_share[i * length_rows : (i + 1) * length_rows] for i in range(per)]
    )
    input_grad = at.relative(input_grad, 2).astype(f32)

    vector_grad = jnp.concatenate(
        [
            jnp.stack([gain_one, shift_one]),
            lead * jnp.stack([gain_two, shift_two, mix_bias_grad, fed_bias_grad]),
        ]
    )
    vector_grad = at.sum_all(at.relative(vector_grad, 1))

    def own_sum(pieces):
        total = pieces[0]
        for step in range(1, blocks):
            total = total + at.to_slot(pieces[step], blocks - step).astype(f32)
        return total

    def both_halves(mine, other, dim):
        return jnp.where(
            c == 0,
            jnp.concatenate([mine, other], axis=dim),
            jnp.concatenate([other, mine], axis=dim),
        )

    def scattered(parts, first_bit):
        low = []
        for step in range(blocks):
            piece = at.scatter_chips(parts[step], (first_bit + step) % 2)
            low.append(piece if step == 0 else piece.astype(bf16))
        mine = own_sum(low)
        rows = part // 2
        sent = lax.dynamic_slice_in_dim(mine, (1 - c) * rows, rows, 0)
        return lax.dynamic_slice_in_dim(mine, c * rows, rows, 0), at.to_core(sent)

    up_sum = both_halves(*scattered([pair[0] for pair in mlp_grads], 0), 1)
    down_sum = both_halves(*scattered([pair[1] for pair in mlp_grads], 1), 1).T
    rows = part // 2
    mine, other = scattered([pair[0] for pair in attn_grads], 0)
    qkv_sum = both_halves(
        mine.reshape(rows, 3, head_width), other.reshape(rows, 3, head_width), 2
    )
    out_sum = both_halves(*scattered([pair[1] for pair in attn_grads], 1), 1).T
    small_grads = [
        jnp.concatenate(
            [bias_grads[r], rel_grad[r * heads : (r + 1) * heads].reshape(-1)]
        )
        for r in range(blocks)
    ]
    small_mine = at.sum_all(own_sum(small_grads), chips_only=True)
    small_other = at.to_core(small_mine)
    bias_sum = both_halves(small_mine[:units], small_other[:units], 0)
    rel_sum = both_halves(
        small_mine[units:].reshape(heads, bucket_count),
        small_other[units:].reshape(heads, bucket_count),
        0,
    ).T

    def own_part(values, dim):
        count = values.shape[dim] // at.dp_n
        return lax.dynamic_slice_in_dim(values, at.dp_i * count, count, dim)

    steps_done = step_count[0].astype(f32)
    first_fix = 1.0 - jnp.power(jnp.float32(0.9), steps_done)
    second_fix = 1.0 - jnp.power(jnp.float32(0.999), steps_done)
    pieces = [
        (own_part(qkv_weight, 0), qkv_moments, qkv_sum, weight_decay),
        (own_part(out_weight, 1), out_moments, out_sum, weight_decay),
        (own_part(up_weight, 0), up_moments, up_sum, weight_decay),
        (own_part(down_weight, 1), down_moments, down_sum, weight_decay),
        (up_bias, bias_moments, bias_sum, 0.0),
        (rel_bias, rel_moments, rel_sum, 0.0),
        (norm_vectors, vector_moments, vector_grad, 0.0),
    ]
    adjusted = [
        adjust(weight, moments[0], moments[1], grad, decay, first_fix, second_fix)
        for weight, moments, grad, decay in pieces
    ]
    lead_dp = (at.dp_i == 0).astype(f32)
    share = [1.0, 1.0, 1.0, 1.0, lead_dp, lead_dp]
    squares = jnp.stack(
        [share[i] * jnp.sum(pieces[i][0] * pieces[i][0]) for i in range(6)]
        + [share[i] * jnp.sum(adjusted[i][2] * adjusted[i][2]) for i in range(6)]
    )
    squares = at.sum_all(squares)
    vector_sq = jnp.sum(norm_vectors * norm_vectors, axis=1)
    vector_up_sq = jnp.sum(adjusted[6][2] * adjusted[6][2], axis=1)
    weight_norm = jnp.sqrt(jnp.concatenate([squares[:6], vector_sq]))
    update_norm = jnp.sqrt(jnp.concatenate([squares[6:], vector_up_sq]))
    trust_ratio = weight_norm / (update_norm + adam_eps)
    results = [block_out, input_grad]
    for index in range(6):
        results.append(pieces[index][0] - learn_rate * trust_ratio[index] * adjusted[index][2])
        results.append(jnp.stack([adjusted[index][0], adjusted[index][1]]))
    results.append(norm_vectors - learn_rate * trust_ratio[6:][:, None] * adjusted[6][2])
    results.append(jnp.stack([adjusted[6][0], adjusted[6][1]]))
    results.append(jnp.stack([weight_norm, update_norm]))
    return tuple(results)


def solution(mesh):
    return jax.shard_map(
        local,
        mesh=mesh,
        in_specs=(
            P("dp", "mp", None),
            P("dp", "mp", None),
            P("dp"),
            P(),
            P(),
            P(None, None, "mp"),
            P("mp", None),
            P(None, "mp"),
            P("mp", None),
            P("mp"),
            P(None, "mp"),
            P(),
            P(None, "dp", None, "mp"),
            P(None, "mp", "dp"),
            P(None, "dp", "mp"),
            P(None, "mp", "dp"),
            P(None, "mp"),
            P(None, None, "mp"),
            P(),
        ),
        out_specs=(
            P("dp", "mp", None),
            P("dp", "mp", None),
            P("dp", None, "mp"),
            P(None, "dp", None, "mp"),
            P("mp", "dp"),
            P(None, "mp", "dp"),
            P("dp", "mp"),
            P(None, "dp", "mp"),
            P("mp", "dp"),
            P(None, "mp", "dp"),
            P("mp"),
            P(None, "mp"),
            P(None, "mp"),
            P(None, None, "mp"),
            P(),
            P(),
            P(),
        ),
        check_vma=False,
    )
```

```python
import jax
import jax.numpy as jnp
from jax import lax
from jax.experimental import pallas as pl
from jax.experimental.pallas import tpu as pltpu
from jax.sharding import PartitionSpec as P

HD = 64
f32 = jnp.float32
bf16 = jnp.bfloat16

norm_eps = 1e-05
adam_eps = 1e-06
learn_rate = 0.25
weight_decay = 0.1
masked_score = -1000000000.0
score_scale = HD ** (-0.5)
kernel_bytes = 16 << 20
back_bytes = 24 << 20

in_vmem = pl.BlockSpec(memory_space=pltpu.VMEM)
in_smem = pl.BlockSpec(memory_space=pltpu.SMEM)


def dot_nt(left, right):
    return lax.dot_general(left, right, (((1,), (1,)), ((), ())), preferred_element_type=f32)


def dot_nn(left, right):
    return lax.dot_general(left, right, (((1,), (0,)), ((), ())), preferred_element_type=f32)


def dot_tn(left, right):
    return lax.dot_general(left, right, (((0,), (0,)), ((), ())), preferred_element_type=f32)


def tile_of(rows):
    return min(256, rows)


def bias_tiles(line_ref, head, tiles, tile):
    causal = lax.broadcasted_iota(jnp.int32, (tile, tile), 0) <= lax.broadcasted_iota(
        jnp.int32, (tile, tile), 1
    )
    made = []
    for kk in range(tiles):
        line = line_ref[head : head + 1, kk * 2 * tile : (kk + 1) * 2 * tile]
        wide = jnp.broadcast_to(line, (tile, 2 * tile))
        made.append(pltpu.roll(wide, tile, 1, stride=1, stride_axis=0)[:, :tile])
    made[0] = jnp.where(causal, made[0], masked_score)
    return made


def scores_of(keys, query, toeplitz, block, tile, key_pos, length):
    count = (block + 1) * tile
    raw = dot_nt(keys[:count], query)
    raw = raw + jnp.concatenate([toeplitz[block - j] for j in range(block + 1)], axis=0)
    return jnp.where(key_pos[:count] < length, raw, masked_score)


def attend_kernel(heads, length_ref, qkv_ref, line_ref, ctx_ref, lse_ref):
    rows = qkv_ref.shape[0]
    tile = tile_of(rows)
    tiles = rows // tile
    width = heads * HD
    length = length_ref[0]
    key_pos = lax.broadcasted_iota(jnp.int32, (rows, tile), 0)
    for head in range(heads):
        toeplitz = bias_tiles(line_ref, head, tiles, tile)
        cols = slice(head * HD, (head + 1) * HD)
        keys = qkv_ref[:, width + head * HD : width + (head + 1) * HD]
        vals = qkv_ref[:, 2 * width + head * HD : 2 * width + (head + 1) * HD]
        for block in range(tiles):
            here = slice(block * tile, (block + 1) * tile)
            count = (block + 1) * tile
            query = qkv_ref[here, cols] * jnp.asarray(score_scale, bf16)
            raw = scores_of(keys, query, toeplitz, block, tile, key_pos, length)
            top = jnp.max(raw, axis=0, keepdims=True)
            grown = jnp.exp(raw - top)
            total = jnp.sum(grown, axis=0, keepdims=True)
            probs = (grown * (1.0 / total)).astype(bf16)
            ctx_ref[here, cols] = dot_tn(probs, vals[:count]).astype(bf16)
            lse_ref[head : head + 1, here] = top + jnp.log(total)


def attend_back_kernel(
    heads,
    length_ref,
    qkv_ref,
    line_ref,
    lse_ref,
    grad_ref,
    out_ref,
    dist_ref,
    key_acc,
    val_acc,
    diag_acc,
):
    rows = qkv_ref.shape[0]
    tile = tile_of(rows)
    tiles = rows // tile
    width = heads * HD
    length = length_ref[0]
    key_pos = lax.broadcasted_iota(jnp.int32, (rows, tile), 0)
    for head in range(heads):
        toeplitz = bias_tiles(line_ref, head, tiles, tile)
        cols = slice(head * HD, (head + 1) * HD)
        key_cols = slice(width + head * HD, width + (head + 1) * HD)
        val_cols = slice(2 * width + head * HD, 2 * width + (head + 1) * HD)
        keys = qkv_ref[:, key_cols]
        vals = qkv_ref[:, val_cols]
        key_acc[...] = jnp.zeros_like(key_acc)
        val_acc[...] = jnp.zeros_like(val_acc)
        diag_acc[...] = jnp.zeros_like(diag_acc)
        for block in range(tiles):
            here = slice(block * tile, (block + 1) * tile)
            count = (block + 1) * tile
            query = qkv_ref[here, cols] * jnp.asarray(score_scale, bf16)
            grad = grad_ref[here, cols]
            raw = scores_of(keys, query, toeplitz, block, tile, key_pos, length)
            probs = jnp.exp(raw - lse_ref[head : head + 1, here])
            pgrad = dot_nt(vals[:count], grad)
            drop = jnp.sum(probs * pgrad, axis=0, keepdims=True)
            sgrad = (probs * (pgrad - drop)).astype(bf16)
            val_acc[:count] += dot_nn(probs.astype(bf16), grad)
            key_acc[:count] += dot_nn(sgrad, query)
            out_ref[here, cols] = (dot_tn(sgrad, keys[:count]) * score_scale).astype(bf16)
            wide = sgrad.astype(f32)
            for j in range(block + 1):
                diag_acc[block - j] += wide[j * tile : (j + 1) * tile]
        out_ref[:, key_cols] = key_acc[...].astype(bf16)
        out_ref[:, val_cols] = val_acc[...].astype(bf16)
        for kk in range(tiles):
            held = jnp.concatenate([diag_acc[kk], jnp.zeros((tile, tile), f32)], axis=1)
            half = tile // 2
            while half >= 1:
                held = held[:half] + pltpu.roll(held[half : 2 * half], 2 * tile - half, 1)
                half //= 2
            dist_ref[head : head + 1, kk * 2 * tile : (kk + 1) * 2 * tile] = pltpu.roll(held, tile, 1)


def attend(length, qkv, line, heads):
    rows = qkv.shape[0]
    return pl.pallas_call(
        lambda *refs: attend_kernel(heads, *refs),
        out_shape=(
            jax.ShapeDtypeStruct((rows, heads * HD), bf16),
            jax.ShapeDtypeStruct((heads, rows), f32),
        ),
        in_specs=[in_smem, in_vmem, in_vmem],
        out_specs=(in_vmem, in_vmem),
        compiler_params=pltpu.CompilerParams(vmem_limit_bytes=kernel_bytes),
        cost_estimate=pl.CostEstimate(
            flops=heads * rows * rows * HD * 32,
            bytes_accessed=4 << 20,
            transcendentals=heads * rows * rows,
        ),
        name="attend",
    )(length, qkv, line)


def attend_back(length, qkv, line, lse, grad, heads):
    rows = qkv.shape[0]
    tile = tile_of(rows)
    return pl.pallas_call(
        lambda *refs: attend_back_kernel(heads, *refs),
        out_shape=(
            jax.ShapeDtypeStruct((rows, 3 * heads * HD), bf16),
            jax.ShapeDtypeStruct((heads, 2 * rows), f32),
        ),
        in_specs=[in_smem, in_vmem, in_vmem, in_vmem, in_vmem],
        out_specs=(in_vmem, in_vmem),
        scratch_shapes=[
            pltpu.VMEM((rows, HD), f32),
            pltpu.VMEM((rows, HD), f32),
            pltpu.VMEM((rows // tile, tile, tile), f32),
        ],
        compiler_params=pltpu.CompilerParams(vmem_limit_bytes=back_bytes),
        cost_estimate=pl.CostEstimate(
            flops=heads * rows * rows * HD * 64,
            bytes_accessed=4 << 20,
            transcendentals=heads * rows * rows,
        ),
        name="attend_back",
    )(length, qkv, line, lse, grad)


def tie(*values):
    return lax.optimization_barrier(values)


def after(values, *others):
    return lax.optimization_barrier((values, *others))[0]


class Places:
    def __init__(self, per):
        self.per = per
        self.dp_n = lax.axis_size("dp")
        self.mp_n = lax.axis_size("mp")
        self.q_n = self.dp_n // 2
        self.slots = 2 * per
        self.t_n = self.mp_n // self.slots
        assert self.dp_n % 2 == 0 and self.mp_n % self.slots == 0
        dp_i = lax.axis_index("dp")
        mp_i = lax.axis_index("mp")
        self.dp_i, self.mp_i = dp_i, mp_i
        self.q, self.c = dp_i // 2, lax.rem(dp_i, 2)
        self.s, self.t = mp_i // self.t_n, lax.rem(mp_i, self.t_n)
        assert per == 2
        self.home = self.s // per
        self.at_home = self.c == self.home
        self.q_bits = []
        while (1 << len(self.q_bits)) < self.q_n:
            self.q_bits.append(1 << len(self.q_bits))
        assert (1 << len(self.q_bits)) == self.q_n

    def move(self, values, target):
        pairs = []
        for q in range(self.q_n):
            for c in range(2):
                for s in range(self.slots):
                    for t in range(self.t_n):
                        found = target(q, c, s, t)
                        if found is not None:
                            nq, nc, ns, nt = found
                            pairs.append(
                                (
                                    (q * 2 + c) * self.mp_n + s * self.t_n + t,
                                    (nq * 2 + nc) * self.mp_n + ns * self.t_n + nt,
                                )
                            )
        return lax.ppermute(values, ("dp", "mp"), pairs)

    def to_core(self, values):
        return self.move(values, lambda q, c, s, t: (q, 1 - c, s, t))

    def to_slot(self, values, step):
        return self.move(values, lambda q, c, s, t: (q, c, s ^ step, t))

    def to_chip(self, values, bit):
        return self.move(values, lambda q, c, s, t: (q ^ bit, c, s, t))

    def to_team(self, values, step):
        return self.move(values, lambda q, c, s, t: (q, c, s, (t + step) % self.t_n))

    def relative(self, values, dim):
        size = values.shape[dim] // self.q_n
        return jnp.concatenate(
            [
                lax.dynamic_slice_in_dim(values, (self.q ^ k) * size, size, dim)
                for k in range(self.q_n)
            ],
            axis=dim,
        )

    def block_at(self, step):
        return lax.rem(self.s + step, self.slots) * self.t_n + self.t

    def collect_piece(self, local, step):
        piece = lax.dynamic_index_in_dim(local, (self.s ^ step) % 2, 0, keepdims=False)
        if step == 0:
            return piece
        return self.move(
            piece,
            lambda q, c, s, t: (
                (q, c, s ^ step, t) if (s ^ step) // self.per == c else None
            ),
        )

    def collect_end(self, pieces):
        count, width = pieces[0].shape
        whole = jnp.zeros((count * self.mp_n, width), pieces[0].dtype)
        for step, piece in enumerate(pieces):
            for turn in range(self.t_n):
                piece_t = self.to_team(piece, turn) if turn > 0 else piece
                from_t = lax.rem(self.t + self.t_n - turn, self.t_n)
                whole = lax.dynamic_update_slice_in_dim(
                    whole, piece_t, ((self.s ^ step) * self.t_n + from_t) * count, 0
                )
        return whole

    def collect_both(self, whole):
        other = self.move(
            whole, lambda q, c, s, t: (q, 1 - c, s, t) if c == s // self.per else None
        )
        return jnp.where(self.at_home, whole, other)

    def deliver_first(self, blocks):
        got = self.move(
            blocks, lambda q, c, s, t: (q, 1 - c, s ^ 2, t) if c != s // 2 else None
        )
        return jnp.where(self.at_home, blocks, got)

    def deliver_second(self, pair):
        count = pair.shape[0] // 2
        got = self.to_slot(pair[count:], 1)
        mine = pair[:count]
        even = self.s % 2 == 0
        return jnp.stack([jnp.where(even, mine, got), jnp.where(even, got, mine)])

    def share(self, values, length, flip, team):
        side = jnp.where(self.at_home, 0, 1) ^ flip
        parts = []
        for index in range(self.per):
            slot = self.s ^ (self.per * side + index)
            block = slot * self.t_n + lax.rem(self.t + team, self.t_n)
            parts.append(lax.dynamic_slice_in_dim(values, block * length, length, 0))
        return jnp.concatenate(parts, axis=0)

    def sum_share(self, partial, length):
        total = self.share(partial, length, 0, 0).astype(f32)
        for team in range(self.t_n):
            for flip in (0, 1):
                if (team, flip) != (0, 0):
                    sent = self.share(partial, length, flip, team).astype(bf16)
                    total = total + self.move(
                        sent, lambda q, c, s, t: (q, c ^ flip, s, (t + team) % self.t_n)
                    ).astype(f32)
        return total

    def sum_team(self, partial):
        total = partial.astype(f32)
        total = total + self.to_core(partial).astype(f32)
        if self.t_n > 1:
            low = total.astype(bf16)
            for team in range(1, self.t_n):
                total = total + self.to_team(low, team).astype(f32)
        return total

    def spread_inner(self, own, one):
        both = jnp.concatenate([own, one], axis=1)
        return self.move(both, lambda q, c, s, t: (q, c, s ^ 3, t) if s in (1, 2) else None)

    def spread_outer(self, inner):
        return self.move(inner, lambda q, c, s, t: (q, c, s ^ 1, t) if s in (1, 2) else None)

    def spread_pair(self, inner, outer):
        size = inner.shape[1] // 2
        turned = jnp.concatenate([inner[:, size:], inner[:, :size]], axis=1)
        return jnp.where((self.s == 1) | (self.s == 2), turned, outer)

    def fold_outer(self, far):
        size = far.shape[1] // 2
        got = self.move(far, lambda q, c, s, t: (q, c, s ^ 1, t) if s in (0, 3) else None)
        return far.astype(f32) + jnp.concatenate([got[:, size:], got[:, :size]], axis=1).astype(f32)

    def fold_inner(self, far):
        size = far.shape[1] // 2
        got = self.move(
            far.astype(bf16), lambda q, c, s, t: (q, c, s ^ 3, t) if s in (1, 2) else None
        ).astype(f32)
        return got[:, :size], got[:, size:]

    def bits_from(self, first):
        return self.q_bits[first:] + self.q_bits[:first]

    def gather_chips(self, piece, first):
        pieces = {0: piece}
        for bit in self.bits_from(first):
            for k in list(pieces):
                pieces[k | bit] = self.to_chip(pieces[k], bit)
        return [pieces[k] for k in range(self.q_n)]

    def gather_start(self, piece):
        return {bit: self.to_chip(piece, bit) for bit in self.q_bits}

    def gather_end(self, piece, near, first):
        pieces = {0: piece}
        for bit in self.bits_from(first):
            for k in list(pieces):
                pieces[k | bit] = near[bit] if k == 0 else self.to_chip(pieces[k], bit)
        return [pieces[k] for k in range(self.q_n)]

    def scatter_order(self, first):
        order = [0]
        for bit in reversed(self.bits_from(first)):
            order = order + [k | bit for k in order]
        return order

    def scatter_first(self, kept, sent, first):
        got = self.to_chip(sent, self.bits_from(first)[0])
        half = kept.shape[0] // 2
        if len(self.q_bits) == 1:
            return kept.astype(f32) + got.astype(f32), None
        sent_on = (kept[half:].astype(f32) + got[half:].astype(f32)).astype(bf16)
        return kept[:half].astype(f32) + got[:half].astype(f32), sent_on

    def scatter_rest(self, halves, first):
        total, sent = halves
        bits = self.bits_from(first)[1:]
        for number, bit in enumerate(bits):
            total = total + self.to_chip(sent, bit).astype(f32)
            if number + 1 < len(bits):
                half = total.shape[0] // 2
                total, sent = total[:half], total[half:].astype(bf16)
        return total

    def sum_all(self, values, chips_only=False):
        if not chips_only:
            values = values + self.to_core(values)
        for low in range(0, len(self.q_bits), 2):
            bits = self.q_bits[low : low + 2]
            got = [self.to_chip(values, bit) for bit in bits]
            if len(bits) == 2:
                both = self.to_chip(values, bits[0] | bits[1])
                values = (values + got[0]) + (got[1] + both)
            else:
                values = values + got[0]
        if not chips_only:
            bit, bits = 1, []
            while bit < self.mp_n:
                bits.append(bit)
                bit *= 2
            flip = lambda mask: self.move(
                values,
                lambda q, c, s, t: (
                    q,
                    c,
                    ((s * self.t_n + t) ^ mask) // self.t_n,
                    ((s * self.t_n + t) ^ mask) % self.t_n,
                ),
            )
            for low in range(0, len(bits), 2):
                pair = bits[low : low + 2]
                if len(pair) == 2:
                    one, two, both = flip(pair[0]), flip(pair[1]), flip(pair[0] | pair[1])
                    values = (values + one) + (two + both)
                else:
                    values = values + flip(pair[0])
        return values


def pack_attn_kernel(place_ref, qkv_ref, out_ref, qkv_full, out_full, piece_ref):
    size = qkv_ref.shape[2]
    for j in range(3):
        qkv_full[:, j * size : (j + 1) * size] = qkv_ref[j].astype(bf16)
    out_full[...] = out_ref[...].T.astype(bf16)

    @pl.when(pl.program_id(0) == 0)
    def _():
        piece_ref[:, : 3 * size] = qkv_full[...]
        piece_ref[:, 3 * size :] = out_full[...]


def pack_mlp_kernel(place_ref, up_ref, down_ref, up_full, down_full, up_piece, down_piece):
    up_full[...] = up_ref[...].astype(bf16)
    down_full[...] = down_ref[...].T.astype(bf16)

    @pl.when(pl.program_id(0) == 0)
    def _():
        up_piece[...] = up_full[...]
        down_piece[...] = down_full[...]


def packs_in_kernels(at, width, head_width):
    return (width // at.q_n) % 128 == 0 and head_width % 128 == 0


def pack_attn(at, qkv_weight, out_weight, head_width, after):
    width = qkv_weight.shape[0]
    part = width // at.q_n
    if packs_in_kernels(at, width, head_width):
        place = tie(jnp.stack([at.q, at.c]).astype(jnp.int32), after)[0]
        sizes = (3 * head_width, head_width)
        return pl.pallas_call(
            pack_attn_kernel,
            grid_spec=pltpu.PrefetchScalarGridSpec(
                num_scalar_prefetch=1,
                grid=(at.q_n,),
                in_specs=[
                    pl.BlockSpec((3, part, head_width), lambda k, p: (0, p[0] ^ k, p[1])),
                    pl.BlockSpec((head_width, part), lambda k, p: (p[1], p[0] ^ k)),
                ],
                out_specs=tuple(pl.BlockSpec((part, n), lambda k, p: (k, 0)) for n in sizes)
                + (pl.BlockSpec((part, sum(sizes)), lambda k, p: (0, 0)),),
            ),
            out_shape=tuple(jax.ShapeDtypeStruct((width, n), bf16) for n in sizes)
            + (jax.ShapeDtypeStruct((part, sum(sizes)), bf16),),
            name="pack_attn",
        )(place, jnp.transpose(qkv_weight, (1, 0, 2)), out_weight)
    qkv = lax.dynamic_slice_in_dim(qkv_weight, at.c * head_width, head_width, 2)
    out = lax.dynamic_slice_in_dim(out_weight, at.c * head_width, head_width, 0)
    qkv = at.relative(qkv.reshape(width, 3 * head_width).astype(bf16), 0)
    out = at.relative(out.astype(bf16).T, 0)
    return qkv, out, jnp.concatenate([qkv[:part], out[:part]], axis=1)


def pack_mlp(at, up_weight, down_weight, head_width, units, after):
    width = up_weight.shape[0]
    part = width // at.q_n
    if packs_in_kernels(at, width, head_width):
        place = tie(jnp.stack([at.q, at.c]).astype(jnp.int32), after)[0]
        return pl.pallas_call(
            pack_mlp_kernel,
            grid_spec=pltpu.PrefetchScalarGridSpec(
                num_scalar_prefetch=1,
                grid=(at.q_n,),
                in_specs=[
                    pl.BlockSpec((part, units), lambda k, p: (p[0] ^ k, p[1])),
                    pl.BlockSpec((units, part), lambda k, p: (p[1], p[0] ^ k)),
                ],
                out_specs=(
                    pl.BlockSpec((part, units), lambda k, p: (k, 0)),
                    pl.BlockSpec((part, units), lambda k, p: (k, 0)),
                    pl.BlockSpec((part, units), lambda k, p: (0, 0)),
                    pl.BlockSpec((part, units), lambda k, p: (0, 0)),
                ),
            ),
            out_shape=(jax.ShapeDtypeStruct((width, units), bf16),) * 2
            + (jax.ShapeDtypeStruct((part, units), bf16),) * 2,
            name="pack_mlp",
        )(place, up_weight, down_weight)
    up = lax.dynamic_slice_in_dim(up_weight, at.c * units, units, 1).astype(bf16)
    down = lax.dynamic_slice_in_dim(down_weight, at.c * units, units, 0).astype(bf16).T
    up, down = at.relative(up, 0), at.relative(down, 0)
    return up, down, up[:part], down[:part]


def halves_kernel(order, shape, *refs):
    operands, (kept_ref, sent_ref) = refs[:-2], refs[-2:]
    part = operands[0].shape[1] // len(order)
    middle = len(order) // 2
    for index, block in enumerate(order):
        target = kept_ref if index < middle else sent_ref
        rows = slice(index % middle * part, (index % middle + 1) * part)
        col = 0
        number = 0
        for count in shape:
            left = operands[number][:, block * part : (block + 1) * part]
            number += 1
            for _ in range(count):
                right_ref = operands[number]
                number += 1
                size = right_ref.shape[1]
                target[rows, col : col + size] = dot_tn(left, right_ref[...]).astype(bf16)
                col += size


def grad_halves(at, pairs, first):
    rows, width = pairs[0][0].shape
    part = width // at.q_n
    order = at.scatter_order(first)
    middle = at.q_n // 2
    cols = sum(right.shape[1] for _, rights in pairs for right in rights)
    if part % 128 == 0:
        halves = jax.ShapeDtypeStruct((middle * part, cols), bf16)
        operands = [value for left, rights in pairs for value in (left, *rights)]
        return pl.pallas_call(
            lambda *refs: halves_kernel(order, [len(rights) for _, rights in pairs], *refs),
            in_specs=[in_vmem] * len(operands),
            out_specs=(in_vmem, in_vmem),
            out_shape=(halves, halves),
            compiler_params=pltpu.CompilerParams(vmem_limit_bytes=kernel_bytes),
            cost_estimate=pl.CostEstimate(
                flops=3 * rows * width * cols, bytes_accessed=1 << 20, transcendentals=0
            ),
            name="grad_halves",
        )(*operands)
    return tuple(
        jnp.concatenate(
            [
                jnp.concatenate(
                    [
                        dot_tn(left[:, k * part : (k + 1) * part], right).astype(bf16)
                        for left, rights in pairs
                        for right in rights
                    ],
                    axis=1,
                )
                for k in side
            ],
            axis=0,
        )
        for side in (order[:middle], order[middle:])
    )


def adjust(weight, first, second, gradient, decay_rate, first_fix, second_fix):
    first_new = 0.9 * first + 0.1 * gradient
    second_new = 0.999 * second + 0.001 * gradient * gradient
    update = (
        first_new / first_fix / (jnp.sqrt(second_new / second_fix) + adam_eps) + decay_rate * weight
    )
    return (first_new, second_new, update)


def in_order(c, mine, other):
    return jnp.where(c == 0, mine, other), jnp.where(c == 0, other, mine)


def adjust_into(index, weight, moments_ref, gradient, fixes_ref, state_ref, update_ref, sums_ref):
    first_new, second_new, update = adjust(
        weight, moments_ref[0], moments_ref[1], gradient, weight_decay, fixes_ref[0], fixes_ref[1]
    )
    state_ref[0] = first_new
    state_ref[1] = second_new
    update_ref[...] = update
    sums_ref[2 * index] = jnp.sum(weight * weight)
    sums_ref[2 * index + 1] = jnp.sum(update * update)


def adjust_attn_kernel(
    place_ref, fixes_ref, mine_ref, other_ref, qkv_ref, out_ref, qkv_moments, out_moments,
    qkv_state, out_state, qkv_update, out_update, sums_ref,
):
    size = qkv_ref.shape[2] // 2
    one, two = in_order(place_ref[1], mine_ref[...], other_ref[...])
    parts = [
        jnp.concatenate([one[:, j * size : (j + 1) * size], two[:, j * size : (j + 1) * size]], 1)
        for j in range(4)
    ]
    adjust_into(
        0, qkv_ref[...], qkv_moments, jnp.stack(parts[:3]), fixes_ref, qkv_state, qkv_update, sums_ref
    )
    adjust_into(
        1, out_ref[...], out_moments, parts[3].T, fixes_ref, out_state, out_update, sums_ref
    )


def adjust_mlp_kernel(
    place_ref, fixes_ref, mine_ref, other_ref, up_ref, down_ref, up_moments, down_moments,
    up_state, down_state, up_update, down_update, sums_ref,
):
    size = up_ref.shape[1] // 2
    one, two = in_order(place_ref[1], mine_ref[...], other_ref[...])
    down_grad = jnp.concatenate([one[:, :size], two[:, :size]], axis=1)
    up_grad = jnp.concatenate([one[:, size:], two[:, size:]], axis=1)
    adjust_into(0, up_ref[...], up_moments, up_grad, fixes_ref, up_state, up_update, sums_ref)
    adjust_into(
        1, down_ref[...], down_moments, down_grad.T, fixes_ref, down_state, down_update, sums_ref
    )


def own_spec(shape, dim, count):
    block = list(shape)
    block[dim] //= count
    return pl.BlockSpec(
        tuple(block), lambda i, p: tuple(p[0] if d == dim else 0 for d in range(len(shape)))
    )


def whole_spec(shape):
    return pl.BlockSpec(shape, lambda i, p: (0,) * len(shape))


def adjust_pair(at, kernel, place, fixes, mine, other, weights, dims, moments):
    parts = [m.shape[1:] for m in moments]
    shapes = [jax.ShapeDtypeStruct(m.shape, f32) for m in moments]
    shapes += [jax.ShapeDtypeStruct(p, f32) for p in parts]
    return pl.pallas_call(
        kernel,
        grid_spec=pltpu.PrefetchScalarGridSpec(
            num_scalar_prefetch=1,
            grid=(1,),
            in_specs=[in_smem, whole_spec(mine.shape), whole_spec(other.shape)]
            + [own_spec(w.shape, d, at.dp_n) for w, d in zip(weights, dims)]
            + [whole_spec(m.shape) for m in moments],
            out_specs=tuple(whole_spec(s.shape) for s in shapes) + (in_smem,),
        ),
        out_shape=tuple(shapes) + (jax.ShapeDtypeStruct((4,), f32),),
        compiler_params=pltpu.CompilerParams(vmem_limit_bytes=back_bytes),
        name="adjust_pair",
    )(place, fixes, mine, other, *weights, *moments)


def apply_kernel(place_ref, rates_ref, *refs):
    count = len(refs) // 3
    for index in range(count):
        refs[2 * count + index][...] = (
            refs[index][...] - rates_ref[index] * refs[count + index][...]
        )


def apply_updates(at, place, rates, weights, dims, updates):
    return pl.pallas_call(
        apply_kernel,
        grid_spec=pltpu.PrefetchScalarGridSpec(
            num_scalar_prefetch=1,
            grid=(1,),
            in_specs=[in_smem]
            + [own_spec(w.shape, d, at.dp_n) for w, d in zip(weights, dims)]
            + [whole_spec(u.shape) for u in updates],
            out_specs=tuple(whole_spec(u.shape) for u in updates),
        ),
        out_shape=tuple(jax.ShapeDtypeStruct(u.shape, f32) for u in updates),
        compiler_params=pltpu.CompilerParams(vmem_limit_bytes=back_bytes),
        name="apply_updates",
    )(place, rates, *weights, *updates)


def norm_parts(values):
    center = values - jnp.mean(values, axis=-1, keepdims=True)
    spread = jnp.mean(center * center, axis=-1, keepdims=True)
    inverse = lax.rsqrt(spread + norm_eps)
    return (center * inverse, inverse)


def norm_back(upstream, normed, inverse, gain_vec):
    scaled = upstream * gain_vec
    return inverse * (
        scaled
        - jnp.mean(scaled, axis=-1, keepdims=True)
        - normed * jnp.mean(scaled * normed, axis=-1, keepdims=True)
    )


def gelu_parts(values):
    half = 0.5 * (1.0 + lax.erf(values * (0.5**0.5)))
    bell = jnp.exp(-0.5 * values * values) * 0.3989422804014327
    return (values * half, half + values * bell)


def local(
    tokens,
    cotangent,
    lengths,
    buckets,
    step_count,
    qkv_weight,
    out_weight,
    up_weight,
    down_weight,
    up_bias,
    rel_bias,
    norm_vectors,
    qkv_moments,
    out_moments,
    up_moments,
    down_moments,
    bias_moments,
    rel_moments,
    vector_moments,
):
    per, length_rows, width = tokens.shape
    at = Places(per)
    seq_len = length_rows * at.mp_n
    blocks = at.slots
    q_n, c, q = at.q_n, at.c, at.q
    head_width = out_weight.shape[0] // 2
    heads = head_width // HD
    units = up_weight.shape[1] // 2
    bucket_count, local_heads = rel_bias.shape

    other_lengths = at.to_core(lengths)
    all_lengths = jnp.where(
        c == 0,
        jnp.concatenate([lengths, other_lengths]),
        jnp.concatenate([other_lengths, lengths]),
    )
    length = lax.dynamic_slice_in_dim(all_lengths, at.s, 1, 0)
    row_keep = jnp.arange(seq_len)[:, None] < length[0]
    row_mask = row_keep.astype(f32)
    vectors = at.relative(norm_vectors, 1)

    def half(values, dim, size):
        return lax.dynamic_slice_in_dim(values, c * size, size, dim)

    part = width // q_n
    small_own = jnp.concatenate(
        [half(up_bias, 0, units), half(rel_bias, 1, heads).T.reshape(-1)]
    )
    qkv_cols = 3 * head_width
    attn_cols = 4 * head_width
    high = lax.reduce_precision(small_own, 8, 7)
    rest = small_own - high
    mid = lax.reduce_precision(rest, 8, 7)
    three = jnp.concatenate([high, mid, rest - mid]).astype(bf16)
    small_rows = -(-three.size // (16 * attn_cols)) * 16
    three = jnp.pad(three, (0, small_rows * attn_cols - three.size)).reshape(small_rows, attn_cols)

    def small_of(rows_low):
        flat = rows_low.reshape(-1).astype(f32)
        count = small_own.size
        return (flat[:count] + flat[count : 2 * count]) + flat[2 * count : 3 * count]

    tokens_near = at.relative(tokens, 2)
    token_pieces = {step: at.collect_piece(tokens_near, step) for step in (0, 2, 3, 1)}
    qkv_own, out_own, attn_piece = pack_attn(
        at, qkv_weight, out_weight, head_width, tokens_near
    )
    attn_piece = jnp.concatenate([attn_piece, three], axis=0)
    attn_one = at.to_slot(attn_piece, 1)
    up_own, down_own, up_piece, down_piece = pack_mlp(
        at, up_weight, down_weight, head_width, units, attn_piece
    )
    mlp_piece = jnp.concatenate([up_piece, down_piece], axis=1)
    attn_one = after(attn_one, token_pieces[1], mlp_piece)
    attn_inner = at.spread_inner(attn_piece, attn_one)
    attn_near = at.gather_start(attn_one[:part])
    tokens_there = (after(token_pieces[2], attn_one), token_pieces[3])
    token_pieces[2] = tokens_there[0]
    mlp_one = at.to_slot(after(mlp_piece, *tokens_there), 1)
    inputs_home = at.collect_end([token_pieces[k] for k in range(blocks)])
    attn_pieces = at.gather_end(
        attn_one[:part], {b: after(v, *tokens_there) for b, v in attn_near.items()}, 0
    )
    inputs_low = at.collect_both(inputs_home)
    inputs_low = after(inputs_low, attn_inner, *attn_pieces)
    attn_outer = at.spread_outer(attn_inner)
    up_one, down_one = mlp_one[:, :units], mlp_one[:, units:]
    up_inner = at.spread_inner(up_piece, up_one)
    mlp_near = at.gather_start(mlp_one)
    turn = 1 % len(at.q_bits)
    attn_pair = at.spread_pair(attn_inner, attn_outer)
    pair_first = after(attn_pair[:part], *mlp_near.values(), up_inner)
    pair_near = at.gather_start(pair_first)
    up_outer = at.spread_outer(after(up_inner, *mlp_near.values()))
    down_inner = at.spread_inner(after(down_piece, up_inner, *mlp_near.values()), down_one)
    near_done = (*pair_near.values(), up_outer, down_inner)
    pair_near = {b: after(v, *near_done) for b, v in pair_near.items()}
    small = [
        small_own,
        small_of(attn_one[part:]),
        small_of(attn_pair[part:, :attn_cols]),
        small_of(attn_pair[part:, attn_cols:]),
    ]
    qkv_w = [qkv_own, jnp.concatenate([v[:, :qkv_cols] for v in attn_pieces], axis=0)]
    out_w = [out_own, jnp.concatenate([v[:, qkv_cols:] for v in attn_pieces], axis=0)]
    pair_pieces = []
    for k in range(2):
        cols = slice(k * attn_cols, (k + 1) * attn_cols)
        pieces = at.gather_end(
            pair_first[:, cols], {b: v[:, cols] for b, v in pair_near.items()}, k * turn
        )
        pair_pieces += pieces
        qkv_w.append(jnp.concatenate([v[:, :qkv_cols] for v in pieces], axis=0))
        out_w.append(jnp.concatenate([v[:, qkv_cols:] for v in pieces], axis=0))
    down_outer = at.spread_outer(after(down_inner, *near_done))
    incoming_near = at.relative(after(cotangent, *near_done), 2)
    incoming_pieces = {step: at.collect_piece(incoming_near, step) for step in (2, 3)}
    mlp_near = {b: after(v, *pair_pieces) for b, v in mlp_near.items()}
    up_one_pieces = at.gather_end(up_one, {b: v[:, :units] for b, v in mlp_near.items()}, 0)
    down_one_pieces = at.gather_end(
        down_one, {b: v[:, units:] for b, v in mlp_near.items()}, turn
    )
    one_done = (*up_one_pieces, *down_one_pieces, down_outer)
    up_pair = after(at.spread_pair(up_inner, up_outer), *one_done)
    up_near = at.gather_start(up_pair)
    incoming_near = after(incoming_near, *one_done)
    incoming_pieces.update({step: at.collect_piece(incoming_near, step) for step in (0, 1)})
    down_pair = after(at.spread_pair(down_inner, down_outer), *up_near.values())

    def pair_halves(piece, near, first):
        halves = []
        for k in range(2):
            cols = slice(k * units, (k + 1) * units)
            halves.append(
                at.gather_end(piece[:, cols], {b: v[:, cols] for b, v in near.items()}, k * turn)
            )
        return [jnp.concatenate(pair, axis=1) for pair in zip(*halves)]

    up_pair_pieces = pair_halves(up_pair, up_near, 0)
    down_near = at.gather_start(down_pair)
    down_near = {b: after(v, *up_pair_pieces) for b, v in down_near.items()}
    down_pair_pieces = pair_halves(down_pair, down_near, turn)
    incoming_home = at.collect_end([incoming_pieces[k] for k in range(blocks)])
    up_w = [
        up_own,
        jnp.concatenate(up_one_pieces, axis=0),
        jnp.concatenate(up_pair_pieces, axis=0),
    ]
    down_w = [
        down_own,
        jnp.concatenate(down_one_pieces, axis=0),
        jnp.concatenate(down_pair_pieces, axis=0),
    ]

    tile = tile_of(seq_len)
    tiles = seq_len // tile
    padded = jnp.concatenate([jnp.zeros((tile,), jnp.int32), buckets])
    spread = jnp.concatenate(
        [padded[kk * tile : (kk + 2) * tile] for kk in range(tiles)]
    )
    choose = (jnp.arange(bucket_count, dtype=jnp.int32)[:, None] == spread[None, :]).astype(f32)
    rel_rows = jnp.concatenate(
        [values[units:].reshape(heads, bucket_count) for values in small], axis=0
    )
    lines = jnp.dot(rel_rows, choose, precision=lax.Precision.HIGHEST)

    inputs = inputs_low.astype(f32)
    first_normed, first_inverse = norm_parts(inputs)
    first_low = (first_normed * vectors[0] + vectors[1]).astype(bf16)
    qkv, contexts, totals = [], [], []
    for r in range(blocks):
        qkv_r = dot_nn(first_low, qkv_w[r]).astype(bf16)
        if r == 0:
            qkv_r = after(qkv_r, mlp_one)
        if r == 1:
            qkv_r = after(qkv_r, attn_outer)
        if r == 3:
            qkv_r = after(qkv_r, *one_done)
        qkv.append(qkv_r)
        context, total = attend(length, qkv[r], lines[r * heads : (r + 1) * heads], heads)
        contexts.append(context)
        totals.append(total)
    mixed = dot_nt(contexts[0], out_w[0])
    for r in range(1, blocks):
        mixed = mixed + dot_nt(contexts[r], out_w[r])
    mixed = at.sum_team(jnp.where(row_keep, mixed, 0.0).astype(bf16))
    mixed = after(mixed, *up_near.values())
    middle = inputs + (mixed + vectors[4]) * row_mask
    second_normed, second_inverse = norm_parts(middle)
    second_low = (second_normed * vectors[2] + vectors[3]).astype(bf16)
    acts, slopes = [], []
    biases = [small[0][:units], small[1][:units], jnp.concatenate([small[2][:units], small[3][:units]])]
    for r in range(3):
        pre = dot_nn(second_low, up_w[r]) + biases[r]
        act, slope = gelu_parts(pre)
        acts.append(act.astype(bf16))
        slopes.append(slope)
    fed = dot_nt(acts[0], down_w[0])
    for r in range(1, 3):
        fed = fed + dot_nt(acts[r], down_w[r])
    incoming_low = at.collect_both(incoming_home)
    kept = jnp.where(row_keep, incoming_low, jnp.zeros_like(incoming_low))
    fed_bias_grad = jnp.sum(kept.astype(f32), axis=0)
    bias_grads = [None] * blocks

    def back_through(r, kept=kept):
        pre_low = (dot_nn(kept, down_w[r]) * slopes[r]).astype(bf16)
        return pre_low, jnp.sum(pre_low.astype(f32), axis=0), dot_nt(pre_low, up_w[r])

    down_far = at.scatter_first(*grad_halves(at, [(kept, [acts[2]])], 0), 0)
    down_near_halves = grad_halves(at, [(kept, [acts[0], acts[1]])], 0)
    fed_low = after(fed.astype(bf16), *down_near_halves)
    fed_share = at.sum_share(fed_low, length_rows)
    middle_share = at.share(middle, length_rows, 0, 0)
    mask_share = at.share(row_mask, length_rows, 0, 0)
    out_share = (middle_share + (fed_share + vectors[5]) * mask_share).astype(bf16)
    pre_pair, bias_pair, back = back_through(2)
    bias_grads[2], bias_grads[3] = bias_pair[:units], bias_pair[units:]
    up_far_halves = grad_halves(at, [(second_low, [pre_pair])], 1)
    up_far = at.scatter_first(*up_far_halves, 1)
    out_pair = at.deliver_first(out_share)
    kept_late = after(kept, out_share, *up_far_halves)
    pre_own, bias_grads[0], term = back_through(0, kept_late)
    back = back + term
    pre_one, bias_grads[1], term = back_through(1, kept_late)
    back = back + term
    up_near_halves = grad_halves(at, [(second_low, [pre_own, pre_one])], 1)
    back_low = after(back.astype(bf16), *up_near_halves)
    second_grad = at.sum_team(back_low)
    second_grad = after(second_grad, *down_far)
    down_far = at.scatter_rest(down_far, 0)
    lead = jnp.where((c == 0) & (at.t == 0), 1.0, 0.0)
    gain_two = jnp.sum(second_grad * second_normed, axis=0)
    shift_two = jnp.sum(second_grad, axis=0)
    middle_grad = incoming_low.astype(f32) + norm_back(
        second_grad, second_normed, second_inverse, vectors[2]
    )
    branch = jnp.where(row_keep, middle_grad, 0.0).astype(bf16)
    mix_bias_grad = jnp.sum(branch.astype(f32), axis=0)
    back = None
    rel_grads = [None] * blocks
    context_grads = [dot_nn(branch, out_w[r]).astype(bf16) for r in range(blocks)]
    own_cols = slice(0, units)
    far_cols = slice(units, 2 * units)
    attn_sums = [None] * blocks
    attn_halves = [None] * blocks
    for r in reversed(range(blocks)):
        context_grad = context_grads[r]
        if r == 3:
            context_grad = after(context_grad, *up_far, out_pair)
            up_far = at.scatter_rest([after(v, out_pair) for v in up_far], 1)
            out_pair = after(out_pair, *up_far_halves)
            block_out = at.deliver_second(out_pair)
        if r == 2:
            context_grad = after(context_grad, down_far, up_far, block_out)
            mlp_far = jnp.concatenate(
                [
                    down_far[:, own_cols],
                    up_far[:, own_cols],
                    down_far[:, far_cols],
                    up_far[:, far_cols],
                ],
                axis=1,
            ).astype(bf16)
            mlp_far = at.fold_outer(after(mlp_far, block_out))
            down_near_halves = [after(v, up_far, block_out) for v in down_near_halves]
            up_near_halves = [after(v, down_far, block_out) for v in up_near_halves]
            down_near_sum = at.scatter_first(*down_near_halves, 0)
            up_near_sum = at.scatter_first(*up_near_halves, 1)
        if r == 0:
            context_grad = after(context_grad, *down_near_sum, *up_near_sum, mlp_far)
            mlp_one, mlp_own = at.fold_inner(after(mlp_far, *up_near_sum))
            for k in (3, 2):
                held = [after(v, *down_near_sum, *up_near_sum) for v in attn_halves[k]]
                attn_sums[k] = at.scatter_first(*held, k % 2)
            down_near_sum = at.scatter_rest(down_near_sum, 0)
            up_near_sum = at.scatter_rest(up_near_sum, 1)
        proj_grad, dist = attend_back(
            length, qkv[r], lines[r * heads : (r + 1) * heads], totals[r], context_grad, heads
        )
        rel_grads[r] = dist
        attn_halves[r] = grad_halves(
            at, [(first_low, [proj_grad]), (branch, [contexts[r]])], r % 2
        )
        term = dot_nt(proj_grad, qkv_w[r])
        back = term if back is None else back + term
    there = (*attn_sums[3], *attn_sums[2], down_near_sum, up_near_sum)
    for k in (1, 0):
        held = [after(v, *there) for v in attn_halves[k]]
        attn_sums[k] = at.scatter_first(*held, k % 2)
    for k in (3, 2, 1, 0):
        attn_sums[k] = at.scatter_rest(attn_sums[k], k % 2)
    mlp_one = mlp_one + jnp.concatenate(
        [down_near_sum[:, far_cols], up_near_sum[:, far_cols]], axis=1
    )
    mlp_own = mlp_own + jnp.concatenate(
        [down_near_sum[:, own_cols], up_near_sum[:, own_cols]], axis=1
    )
    mlp_mine = mlp_own + at.to_slot(mlp_one.astype(bf16), 1).astype(f32)
    attn_far = jnp.concatenate([attn_sums[2], attn_sums[3]], axis=1).astype(bf16)
    attn_one_sum, attn_own_sum = at.fold_inner(at.fold_outer(attn_far))
    attn_one_sum = (attn_one_sum + attn_sums[1]).astype(bf16)
    attn_mine = attn_own_sum + attn_sums[0] + at.to_slot(attn_one_sum, 1).astype(f32)
    rel_grad = lax.dot_general(
        jnp.concatenate(rel_grads, axis=0),
        choose,
        (((1,), (1,)), ((), ())),
        precision=lax.Precision.HIGHEST,
    )
    first_grad = at.sum_share(back.astype(bf16), length_rows)
    normed_share = at.share(first_normed, length_rows, 0, 0)
    inverse_share = at.share(first_inverse, length_rows, 0, 0)
    middle_grad_share = at.share(middle_grad, length_rows, 0, 0)
    gain_one = jnp.sum(first_grad * normed_share, axis=0)
    shift_one = jnp.sum(first_grad, axis=0)
    input_share = middle_grad_share + norm_back(
        first_grad, normed_share, inverse_share, vectors[0]
    )
    input_pair = at.deliver_first(input_share.astype(bf16))
    input_grad = at.relative(at.deliver_second(input_pair), 2).astype(f32)

    def by_place(rows_of):
        around = jnp.stack(rows_of)
        moved = []
        for place in range(blocks):
            picked = around[0]
            for k in range(1, blocks):
                picked = jnp.where(at.s ^ k == place, around[k], picked)
            moved.append(picked)
        moved = jnp.stack(moved)[:, None, None, :]
        here = (jnp.arange(at.t_n)[:, None] == at.t) & (jnp.arange(2)[None, :] == c)
        return jnp.where(here[None, :, :, None], moved, 0.0).reshape(at.mp_n, 2, -1)

    vector_grad = jnp.concatenate(
        [
            jnp.stack([gain_one, shift_one]),
            lead * jnp.stack([gain_two, shift_two, mix_bias_grad, fed_bias_grad]),
        ]
    )
    small_grad = by_place(
        [
            jnp.concatenate([bias_grads[r], rel_grad[r * heads : (r + 1) * heads].reshape(-1)])
            for r in range(blocks)
        ]
    )
    joined = at.sum_all(
        jnp.concatenate([at.relative(vector_grad, 1).reshape(-1), small_grad.reshape(-1)])
    )
    vector_grad = joined[: vector_grad.size].reshape(vector_grad.shape)
    small_sum = lax.dynamic_index_in_dim(
        joined[vector_grad.size :].reshape(small_grad.shape), at.mp_i, 0, keepdims=False
    )
    bias_sum = small_sum[:, :units].reshape(-1)
    rel_sum = small_sum[:, units:].reshape(2 * heads, bucket_count).T

    rows = part // 2

    def exchanged(mine):
        sent = lax.dynamic_slice_in_dim(mine, (1 - c) * rows, rows, 0)
        return lax.dynamic_slice_in_dim(mine, c * rows, rows, 0), at.to_core(sent)

    mlp_mine, mlp_other = exchanged(mlp_mine)
    attn_mine, attn_other = exchanged(attn_mine)

    steps_done = step_count[0].astype(f32)
    first_fix = 1.0 - jnp.power(jnp.float32(0.9), steps_done)
    second_fix = 1.0 - jnp.power(jnp.float32(0.999), steps_done)
    vector_pieces = [
        (up_bias, bias_moments, bias_sum),
        (rel_bias, rel_moments, rel_sum),
        (norm_vectors, vector_moments, vector_grad),
    ]
    vector_adjusted = [
        adjust(weight, moments[0], moments[1], grad, 0.0, first_fix, second_fix)
        for weight, moments, grad in vector_pieces
    ]
    qkv_view = jnp.transpose(qkv_weight, (1, 0, 2))
    qkv_mom = jnp.transpose(qkv_moments, (0, 2, 1, 3))
    weights = [qkv_view, out_weight, up_weight, down_weight]
    dims = [1, 1, 0, 1]
    in_kernels = rows % 128 == 0
    if in_kernels:
        place = jnp.stack([at.dp_i, c]).astype(jnp.int32)
        fixes = jnp.stack([first_fix, second_fix])
        up_state, down_state, up_update, down_update, mlp_squares = adjust_pair(
            at, adjust_mlp_kernel, place, fixes, mlp_mine, mlp_other,
            weights[2:], dims[2:], [up_moments, down_moments],
        )
        qkv_state, out_state, qkv_update, out_update, attn_squares = adjust_pair(
            at, adjust_attn_kernel, place, fixes, attn_mine, attn_other,
            weights[:2], dims[:2], [qkv_mom, out_moments],
        )
        squares = jnp.concatenate([attn_squares, mlp_squares])
        updates = [qkv_update, out_update, up_update, down_update]
        states = [qkv_state, out_state, up_state, down_state]
    else:
        one, two = in_order(c, attn_mine, attn_other)
        parts = [
            jnp.concatenate(
                [v[:, j * head_width : (j + 1) * head_width] for v in (one, two)], axis=1
            )
            for j in range(4)
        ]
        one, two = in_order(c, mlp_mine, mlp_other)
        grads = [
            jnp.stack(parts[:3]),
            parts[3].T,
            jnp.concatenate([one[:, units:], two[:, units:]], axis=1),
            jnp.concatenate([one[:, :units], two[:, :units]], axis=1).T,
        ]
        own_weights, updates, states, squares = [], [], [], []
        for weight, dim, moments, grad in zip(
            weights, dims, [qkv_mom, out_moments, up_moments, down_moments], grads
        ):
            count = weight.shape[dim] // at.dp_n
            weight = lax.dynamic_slice_in_dim(weight, at.dp_i * count, count, dim)
            first_new, second_new, update = adjust(
                weight, moments[0], moments[1], grad, weight_decay, first_fix, second_fix
            )
            own_weights.append(weight)
            updates.append(update)
            states.append(jnp.stack([first_new, second_new]))
            squares += [jnp.sum(weight * weight), jnp.sum(update * update)]
        squares = jnp.stack(squares)
    lead_dp = (at.dp_i == 0).astype(f32)
    small_squares = jnp.stack(
        [
            lead_dp * jnp.sum(values * values)
            for values in (up_bias, vector_adjusted[0][2], rel_bias, vector_adjusted[1][2])
        ]
    )
    squares = at.sum_all(jnp.concatenate([squares, small_squares])).reshape(6, 2)
    vector_squares = jnp.stack(
        [jnp.sum(v * v, axis=1) for v in (norm_vectors, vector_adjusted[2][2])], axis=1
    )
    norms = jnp.sqrt(jnp.concatenate([squares, vector_squares]))
    rates = learn_rate * (norms[:, 0] / (norms[:, 1] + adam_eps))
    if in_kernels:
        new = apply_updates(at, place, rates[:4], weights, dims, updates)
    else:
        new = [own_weights[k] - rates[k] * updates[k] for k in range(4)]
    new, states = list(new), list(states)
    new[0] = jnp.transpose(new[0], (1, 0, 2))
    states[0] = jnp.transpose(states[0], (0, 2, 1, 3))
    results = [at.relative(block_out, 2), input_grad]
    for k in range(4):
        results += [new[k], states[k]]
    for k in range(2):
        first_new, second_new, update = vector_adjusted[k]
        results.append(vector_pieces[k][0] - rates[4 + k] * update)
        results.append(jnp.stack([first_new, second_new]))
    first_new, second_new, update = vector_adjusted[2]
    results.append(norm_vectors - rates[6:, None] * update)
    results.append(jnp.stack([first_new, second_new]))
    results.append(norms.T)
    return tuple(results)


def solution(mesh):
    return jax.shard_map(
        local,
        mesh=mesh,
        in_specs=(
            P("dp", "mp", None),
            P("dp", "mp", None),
            P("dp"),
            P(),
            P(),
            P(None, None, "mp"),
            P("mp", None),
            P(None, "mp"),
            P("mp", None),
            P("mp"),
            P(None, "mp"),
            P(),
            P(None, "dp", None, "mp"),
            P(None, "mp", "dp"),
            P(None, "dp", "mp"),
            P(None, "mp", "dp"),
            P(None, "mp"),
            P(None, None, "mp"),
            P(),
        ),
        out_specs=(
            P("dp", "mp", None),
            P("dp", "mp", None),
            P("dp", None, "mp"),
            P(None, "dp", None, "mp"),
            P("mp", "dp"),
            P(None, "mp", "dp"),
            P("dp", "mp"),
            P(None, "dp", "mp"),
            P("mp", "dp"),
            P(None, "mp", "dp"),
            P("mp"),
            P(None, "mp"),
            P(None, "mp"),
            P(None, None, "mp"),
            P(),
            P(),
            P(),
        ),
        check_vma=False,
    )
```

```python
import jax
import jax.numpy as jnp
from jax import lax
from jax.experimental import pallas as pl
from jax.experimental.pallas import tpu as pltpu
from jax.sharding import PartitionSpec as P

HD = 64
f32 = jnp.float32
bf16 = jnp.bfloat16

norm_eps = 1e-05
adam_eps = 1e-06
learn_rate = 0.25
weight_decay = 0.1
masked_score = -1000000000.0
score_scale = HD ** (-0.5)
kernel_bytes = 16 << 20
back_bytes = 24 << 20

in_vmem = pl.BlockSpec(memory_space=pltpu.VMEM)
in_smem = pl.BlockSpec(memory_space=pltpu.SMEM)


def dot_nt(left, right):
    return lax.dot_general(left, right, (((1,), (1,)), ((), ())), preferred_element_type=f32)


def dot_nn(left, right):
    return lax.dot_general(left, right, (((1,), (0,)), ((), ())), preferred_element_type=f32)


def dot_tn(left, right):
    return lax.dot_general(left, right, (((0,), (0,)), ((), ())), preferred_element_type=f32)


def tile_of(rows):
    return min(256, rows)


def bias_tiles(line_ref, head, tiles, tile):
    causal = lax.broadcasted_iota(jnp.int32, (tile, tile), 0) <= lax.broadcasted_iota(
        jnp.int32, (tile, tile), 1
    )
    made = []
    for kk in range(tiles):
        line = line_ref[head : head + 1, kk * 2 * tile : (kk + 1) * 2 * tile]
        wide = jnp.broadcast_to(line, (tile, 2 * tile))
        made.append(pltpu.roll(wide, tile, 1, stride=1, stride_axis=0)[:, :tile])
    made[0] = jnp.where(causal, made[0], masked_score)
    return made


def scores_of(keys, query, toeplitz, block, tile, key_pos, length):
    count = (block + 1) * tile
    raw = dot_nt(keys[:count], query)
    raw = raw + jnp.concatenate([toeplitz[block - j] for j in range(block + 1)], axis=0)
    return jnp.where(key_pos[:count] < length, raw, masked_score)


def attend_kernel(heads, length_ref, qkv_ref, line_ref, ctx_ref, lse_ref):
    rows = qkv_ref.shape[0]
    tile = tile_of(rows)
    tiles = rows // tile
    width = heads * HD
    length = length_ref[0]
    key_pos = lax.broadcasted_iota(jnp.int32, (rows, tile), 0)
    for head in range(heads):
        toeplitz = bias_tiles(line_ref, head, tiles, tile)
        cols = slice(head * HD, (head + 1) * HD)
        keys = qkv_ref[:, width + head * HD : width + (head + 1) * HD]
        vals = qkv_ref[:, 2 * width + head * HD : 2 * width + (head + 1) * HD]
        for block in range(tiles):
            here = slice(block * tile, (block + 1) * tile)
            count = (block + 1) * tile
            query = qkv_ref[here, cols] * jnp.asarray(score_scale, bf16)
            raw = scores_of(keys, query, toeplitz, block, tile, key_pos, length)
            top = jnp.max(raw, axis=0, keepdims=True)
            grown = jnp.exp(raw - top)
            total = jnp.sum(grown, axis=0, keepdims=True)
            probs = (grown * (1.0 / total)).astype(bf16)
            ctx_ref[here, cols] = dot_tn(probs, vals[:count]).astype(bf16)
            lse_ref[head : head + 1, here] = top + jnp.log(total)


def attend_back_kernel(
    heads,
    length_ref,
    qkv_ref,
    line_ref,
    lse_ref,
    grad_ref,
    out_ref,
    dist_ref,
    key_acc,
    val_acc,
    diag_acc,
):
    rows = qkv_ref.shape[0]
    tile = tile_of(rows)
    tiles = rows // tile
    width = heads * HD
    length = length_ref[0]
    key_pos = lax.broadcasted_iota(jnp.int32, (rows, tile), 0)
    for head in range(heads):
        toeplitz = bias_tiles(line_ref, head, tiles, tile)
        cols = slice(head * HD, (head + 1) * HD)
        key_cols = slice(width + head * HD, width + (head + 1) * HD)
        val_cols = slice(2 * width + head * HD, 2 * width + (head + 1) * HD)
        keys = qkv_ref[:, key_cols]
        vals = qkv_ref[:, val_cols]
        key_acc[...] = jnp.zeros_like(key_acc)
        val_acc[...] = jnp.zeros_like(val_acc)
        diag_acc[...] = jnp.zeros_like(diag_acc)
        for block in range(tiles):
            here = slice(block * tile, (block + 1) * tile)
            count = (block + 1) * tile
            query = qkv_ref[here, cols] * jnp.asarray(score_scale, bf16)
            grad = grad_ref[here, cols]
            raw = scores_of(keys, query, toeplitz, block, tile, key_pos, length)
            probs = jnp.exp(raw - lse_ref[head : head + 1, here])
            pgrad = dot_nt(vals[:count], grad)
            drop = jnp.sum(probs * pgrad, axis=0, keepdims=True)
            sgrad = (probs * (pgrad - drop)).astype(bf16)
            val_acc[:count] += dot_nn(probs.astype(bf16), grad)
            key_acc[:count] += dot_nn(sgrad, query)
            out_ref[here, cols] = (dot_tn(sgrad, keys[:count]) * score_scale).astype(bf16)
            wide = sgrad.astype(f32)
            for j in range(block + 1):
                diag_acc[block - j] += wide[j * tile : (j + 1) * tile]
        out_ref[:, key_cols] = key_acc[...].astype(bf16)
        out_ref[:, val_cols] = val_acc[...].astype(bf16)
        for kk in range(tiles):
            held = jnp.concatenate([diag_acc[kk], jnp.zeros((tile, tile), f32)], axis=1)
            half = tile // 2
            while half >= 1:
                held = held[:half] + pltpu.roll(held[half : 2 * half], 2 * tile - half, 1)
                half //= 2
            dist_ref[head : head + 1, kk * 2 * tile : (kk + 1) * 2 * tile] = pltpu.roll(held, tile, 1)


def attend(length, qkv, line, heads):
    rows = qkv.shape[0]
    return pl.pallas_call(
        lambda *refs: attend_kernel(heads, *refs),
        out_shape=(
            jax.ShapeDtypeStruct((rows, heads * HD), bf16),
            jax.ShapeDtypeStruct((heads, rows), f32),
        ),
        in_specs=[in_smem, in_vmem, in_vmem],
        out_specs=(in_vmem, in_vmem),
        compiler_params=pltpu.CompilerParams(vmem_limit_bytes=kernel_bytes),
        cost_estimate=pl.CostEstimate(
            flops=heads * rows * rows * HD * 10,
            bytes_accessed=1 << 20,
            transcendentals=0,
        ),
        name="attend",
    )(length, qkv, line)


def attend_back(length, qkv, line, lse, grad, heads):
    rows = qkv.shape[0]
    tile = tile_of(rows)
    return pl.pallas_call(
        lambda *refs: attend_back_kernel(heads, *refs),
        out_shape=(
            jax.ShapeDtypeStruct((rows, 3 * heads * HD), bf16),
            jax.ShapeDtypeStruct((heads, 2 * rows), f32),
        ),
        in_specs=[in_smem, in_vmem, in_vmem, in_vmem, in_vmem],
        out_specs=(in_vmem, in_vmem),
        scratch_shapes=[
            pltpu.VMEM((rows, HD), f32),
            pltpu.VMEM((rows, HD), f32),
            pltpu.VMEM((rows // tile, tile, tile), f32),
        ],
        compiler_params=pltpu.CompilerParams(vmem_limit_bytes=back_bytes),
        cost_estimate=pl.CostEstimate(
            flops=heads * rows * rows * HD * 20,
            bytes_accessed=1 << 20,
            transcendentals=0,
        ),
        name="attend_back",
    )(length, qkv, line, lse, grad)


def tie(*values):
    return lax.optimization_barrier(values)


def after(values, *others):
    return lax.optimization_barrier((values, *others))[0]


class Places:
    def __init__(self, per):
        self.per = per
        self.dp_n = lax.axis_size("dp")
        self.mp_n = lax.axis_size("mp")
        self.q_n = self.dp_n // 2
        self.slots = 2 * per
        self.t_n = self.mp_n // self.slots
        assert self.dp_n % 2 == 0 and self.mp_n % self.slots == 0
        dp_i = lax.axis_index("dp")
        mp_i = lax.axis_index("mp")
        self.dp_i, self.mp_i = dp_i, mp_i
        self.q, self.c = dp_i // 2, lax.rem(dp_i, 2)
        self.s, self.t = mp_i // self.t_n, lax.rem(mp_i, self.t_n)
        assert per == 2
        self.home = self.s // per
        self.at_home = self.c == self.home
        self.q_bits = []
        while (1 << len(self.q_bits)) < self.q_n:
            self.q_bits.append(1 << len(self.q_bits))
        assert (1 << len(self.q_bits)) == self.q_n

    def move(self, values, target):
        pairs = []
        for q in range(self.q_n):
            for c in range(2):
                for s in range(self.slots):
                    for t in range(self.t_n):
                        found = target(q, c, s, t)
                        if found is not None:
                            nq, nc, ns, nt = found
                            pairs.append(
                                (
                                    (q * 2 + c) * self.mp_n + s * self.t_n + t,
                                    (nq * 2 + nc) * self.mp_n + ns * self.t_n + nt,
                                )
                            )
        return lax.ppermute(values, ("dp", "mp"), pairs)

    def to_core(self, values):
        return self.move(values, lambda q, c, s, t: (q, 1 - c, s, t))

    def to_slot(self, values, step):
        return self.move(values, lambda q, c, s, t: (q, c, s ^ step, t))

    def to_chip(self, values, bit):
        return self.move(values, lambda q, c, s, t: (q ^ bit, c, s, t))

    def to_team(self, values, step):
        return self.move(values, lambda q, c, s, t: (q, c, s, (t + step) % self.t_n))

    def relative(self, values, dim):
        size = values.shape[dim] // self.q_n
        return jnp.concatenate(
            [
                lax.dynamic_slice_in_dim(values, (self.q ^ k) * size, size, dim)
                for k in range(self.q_n)
            ],
            axis=dim,
        )

    def block_at(self, step):
        return lax.rem(self.s + step, self.slots) * self.t_n + self.t

    def collect_piece(self, local, step):
        piece = lax.dynamic_index_in_dim(local, (self.s ^ step) % 2, 0, keepdims=False)
        if step == 0:
            return piece
        return self.move(
            piece,
            lambda q, c, s, t: (
                (q, c, s ^ step, t) if (s ^ step) // self.per == c else None
            ),
        )

    def collect_end(self, pieces):
        count, width = pieces[0].shape
        whole = jnp.zeros((count * self.mp_n, width), pieces[0].dtype)
        for step, piece in enumerate(pieces):
            for turn in range(self.t_n):
                piece_t = self.to_team(piece, turn) if turn > 0 else piece
                from_t = lax.rem(self.t + self.t_n - turn, self.t_n)
                whole = lax.dynamic_update_slice_in_dim(
                    whole, piece_t, ((self.s ^ step) * self.t_n + from_t) * count, 0
                )
        return whole

    def collect_both(self, whole):
        other = self.move(
            whole, lambda q, c, s, t: (q, 1 - c, s, t) if c == s // self.per else None
        )
        return jnp.where(self.at_home, whole, other)

    def deliver_first(self, blocks):
        return self.move(
            blocks, lambda q, c, s, t: (q, 1 - c, s ^ 2, t) if c != s // 2 else None
        )

    def deliver_pair(self, blocks, got):
        return jnp.where(self.at_home, blocks, got)

    def deliver_last(self, pair):
        return self.to_slot(pair[pair.shape[0] // 2 :], 1)

    def delivered(self, pair, got):
        mine = pair[: pair.shape[0] // 2]
        even = self.s % 2 == 0
        return jnp.stack([jnp.where(even, mine, got), jnp.where(even, got, mine)])

    def share(self, values, length, flip, team):
        side = jnp.where(self.at_home, 0, 1) ^ flip
        parts = []
        for index in range(self.per):
            slot = self.s ^ (self.per * side + index)
            block = slot * self.t_n + lax.rem(self.t + team, self.t_n)
            parts.append(lax.dynamic_slice_in_dim(values, block * length, length, 0))
        return jnp.concatenate(parts, axis=0)

    def sum_share(self, partial, length):
        total = self.share(partial, length, 0, 0).astype(f32)
        for team in range(self.t_n):
            for flip in (0, 1):
                if (team, flip) != (0, 0):
                    sent = self.share(partial, length, flip, team).astype(bf16)
                    total = total + self.move(
                        sent, lambda q, c, s, t: (q, c ^ flip, s, (t + team) % self.t_n)
                    ).astype(f32)
        return total

    def sum_team(self, partial):
        total = partial.astype(f32)
        total = total + self.to_core(partial).astype(f32)
        if self.t_n > 1:
            low = total.astype(bf16)
            for team in range(1, self.t_n):
                total = total + self.to_team(low, team).astype(f32)
        return total

    def spread_inner(self, own, one):
        both = jnp.concatenate([own, one], axis=1)
        return self.move(both, lambda q, c, s, t: (q, c, s ^ 3, t) if s in (1, 2) else None)

    def spread_outer(self, inner):
        return self.move(inner, lambda q, c, s, t: (q, c, s ^ 1, t) if s in (1, 2) else None)

    def spread_pair(self, inner, outer):
        size = inner.shape[1] // 2
        turned = jnp.concatenate([inner[:, size:], inner[:, :size]], axis=1)
        return jnp.where((self.s == 1) | (self.s == 2), turned, outer)

    def fold_outer(self, far):
        return self.move(far, lambda q, c, s, t: (q, c, s ^ 1, t) if s in (0, 3) else None)

    def fold_add(self, far, got):
        size = far.shape[1] // 2
        turned = jnp.concatenate([got[:, size:], got[:, :size]], axis=1)
        return (far.astype(f32) + turned.astype(f32)).astype(bf16)

    def fold_inner(self, far):
        return self.move(far, lambda q, c, s, t: (q, c, s ^ 3, t) if s in (1, 2) else None)

    def bits_from(self, first):
        return self.q_bits[first:] + self.q_bits[:first]

    def gather_chips(self, piece, first):
        pieces = {0: piece}
        for bit in self.bits_from(first):
            for k in list(pieces):
                pieces[k | bit] = self.to_chip(pieces[k], bit)
        return [pieces[k] for k in range(self.q_n)]

    def gather_start(self, piece):
        return {bit: self.to_chip(piece, bit) for bit in self.q_bits}

    def gather_end(self, piece, near, first):
        pieces = {0: piece}
        for bit in self.bits_from(first):
            for k in list(pieces):
                pieces[k | bit] = near[bit] if k == 0 else self.to_chip(pieces[k], bit)
        return [pieces[k] for k in range(self.q_n)]

    def scatter_order(self, first):
        order = [0]
        for bit in reversed(self.bits_from(first)):
            order = order + [k | bit for k in order]
        return order

    def sum_all(self, values, *others):
        values = values + self.to_core(values)
        for low in range(0, len(self.q_bits), 2):
            bits = self.q_bits[low : low + 2]
            got = [self.to_chip(values, bit) for bit in bits]
            if len(bits) == 2:
                both = self.to_chip(values, bits[0] | bits[1])
                values = (values + got[0]) + (got[1] + both)
            else:
                values = values + got[0]
        values = after(values, *others)
        bit, bits = 1, []
        while bit < self.mp_n:
            bits.append(bit)
            bit *= 2

        def flip(mask):
            def target(q, c, s, t):
                place = (s * self.t_n + t) ^ mask
                return (q, c, place // self.t_n, place % self.t_n)

            return self.move(values, target)

        for low in range(0, len(bits), 2):
            pair = bits[low : low + 2]
            if len(pair) == 2:
                one, two, both = flip(pair[0]), flip(pair[1]), flip(pair[0] | pair[1])
                values = (values + one) + (two + both)
            else:
                values = values + flip(pair[0])
        return values


class ChipSum:
    def __init__(self, at, halves, first):
        self.at = at
        self.bits = list(at.bits_from(first))
        self.parts, sent = [halves[0]], halves[1]
        self.exchange(sent)

    def exchange(self, sent):
        self.got = self.at.to_chip(sent, self.bits.pop(0))
        self.parts.append(self.got)

    def total(self, rows=None):
        total = self.parts[0][rows].astype(f32) if rows else self.parts[0].astype(f32)
        for part in self.parts[1:]:
            total = total + (part[rows] if rows else part).astype(f32)
        return total

    def step(self, *others):
        if not self.bits:
            return
        self.parts[-1] = after(self.parts[-1], *others)
        half = self.got.shape[0] // 2
        sent = self.total(slice(half, None)).astype(bf16)
        self.parts = [part[:half] for part in self.parts]
        self.exchange(sent)

    def rest(self, *others):
        while self.bits:
            self.step(*others)


def pack_attn_kernel(place_ref, qkv_ref, out_ref, qkv_full, out_full, piece_ref):
    size = qkv_ref.shape[2]
    for j in range(3):
        qkv_full[:, j * size : (j + 1) * size] = qkv_ref[j].astype(bf16)
    out_full[...] = out_ref[...].T.astype(bf16)

    @pl.when(pl.program_id(0) == 0)
    def _():
        piece_ref[:, : 3 * size] = qkv_full[...]
        piece_ref[:, 3 * size :] = out_full[...]


def pack_mlp_kernel(place_ref, up_ref, down_ref, up_full, down_full, up_piece, down_piece):
    up_full[...] = up_ref[...].astype(bf16)
    down_full[...] = down_ref[...].T.astype(bf16)

    @pl.when(pl.program_id(0) == 0)
    def _():
        up_piece[...] = up_full[...]
        down_piece[...] = down_full[...]


def packs_in_kernels(at, width, head_width):
    return (width // at.q_n) % 128 == 0 and head_width % 128 == 0


def pack_attn(at, qkv_weight, out_weight, head_width, after):
    width = qkv_weight.shape[0]
    part = width // at.q_n
    if packs_in_kernels(at, width, head_width):
        place = tie(jnp.stack([at.q, at.c]).astype(jnp.int32), after)[0]
        sizes = (3 * head_width, head_width)
        return pl.pallas_call(
            pack_attn_kernel,
            grid_spec=pltpu.PrefetchScalarGridSpec(
                num_scalar_prefetch=1,
                grid=(at.q_n,),
                in_specs=[
                    pl.BlockSpec((3, part, head_width), lambda k, p: (0, p[0] ^ k, p[1])),
                    pl.BlockSpec((head_width, part), lambda k, p: (p[1], p[0] ^ k)),
                ],
                out_specs=tuple(pl.BlockSpec((part, n), lambda k, p: (k, 0)) for n in sizes)
                + (pl.BlockSpec((part, sum(sizes)), lambda k, p: (0, 0)),),
            ),
            out_shape=tuple(jax.ShapeDtypeStruct((width, n), bf16) for n in sizes)
            + (jax.ShapeDtypeStruct((part, sum(sizes)), bf16),),
            name="pack_attn",
        )(place, jnp.transpose(qkv_weight, (1, 0, 2)), out_weight)
    qkv = lax.dynamic_slice_in_dim(qkv_weight, at.c * head_width, head_width, 2)
    out = lax.dynamic_slice_in_dim(out_weight, at.c * head_width, head_width, 0)
    qkv = at.relative(qkv.reshape(width, 3 * head_width).astype(bf16), 0)
    out = at.relative(out.astype(bf16).T, 0)
    return qkv, out, jnp.concatenate([qkv[:part], out[:part]], axis=1)


def pack_mlp(at, up_weight, down_weight, head_width, units, after):
    width = up_weight.shape[0]
    part = width // at.q_n
    if packs_in_kernels(at, width, head_width):
        place = tie(jnp.stack([at.q, at.c]).astype(jnp.int32), after)[0]
        return pl.pallas_call(
            pack_mlp_kernel,
            grid_spec=pltpu.PrefetchScalarGridSpec(
                num_scalar_prefetch=1,
                grid=(at.q_n,),
                in_specs=[
                    pl.BlockSpec((part, units), lambda k, p: (p[0] ^ k, p[1])),
                    pl.BlockSpec((units, part), lambda k, p: (p[1], p[0] ^ k)),
                ],
                out_specs=(
                    pl.BlockSpec((part, units), lambda k, p: (k, 0)),
                    pl.BlockSpec((part, units), lambda k, p: (k, 0)),
                    pl.BlockSpec((part, units), lambda k, p: (0, 0)),
                    pl.BlockSpec((part, units), lambda k, p: (0, 0)),
                ),
            ),
            out_shape=(jax.ShapeDtypeStruct((width, units), bf16),) * 2
            + (jax.ShapeDtypeStruct((part, units), bf16),) * 2,
            name="pack_mlp",
        )(place, up_weight, down_weight)
    up = lax.dynamic_slice_in_dim(up_weight, at.c * units, units, 1).astype(bf16)
    down = lax.dynamic_slice_in_dim(down_weight, at.c * units, units, 0).astype(bf16).T
    up, down = at.relative(up, 0), at.relative(down, 0)
    return up, down, up[:part], down[:part]


def join_kernel(plan, count, *refs):
    pieces, outs = refs[:count], refs[count:]
    for out_ref, (start_cols, rows) in zip(outs, plan):
        part = out_ref.shape[0] // len(rows)
        for k, chunks in enumerate(rows):
            col = 0
            for index, start, size in chunks:
                out_ref[k * part : (k + 1) * part, col : col + size] = pieces[index][
                    :part, start : start + size
                ]
                col += size


def join(pieces, part, plans):
    shapes = [
        jax.ShapeDtypeStruct((part * len(rows), sum(size for _, _, size in rows[0])), bf16)
        for rows in plans
    ]
    return pl.pallas_call(
        lambda *refs: join_kernel([(0, rows) for rows in plans], len(pieces), *refs),
        in_specs=[in_vmem] * len(pieces),
        out_specs=(in_vmem,) * len(plans),
        out_shape=tuple(shapes),
        compiler_params=pltpu.CompilerParams(vmem_limit_bytes=kernel_bytes),
        name="join",
    )(*pieces)


def gelu_parts(values):
    half = 0.5 * (1.0 + lax.erf(values * (0.5**0.5)))
    bell = jnp.exp(-0.5 * values * values) * 0.3989422804014327
    return (values * half, half + values * bell)


def row_tiles(rows, tile=256):
    tile = min(tile, rows)
    return [slice(start, start + tile) for start in range(0, rows, tile)]


def sum_nt_kernel(count, *refs):
    lefts, rights, out_ref = refs[:count], refs[count : 2 * count], refs[-1]
    for here in row_tiles(out_ref.shape[0]):
        total = dot_nt(lefts[0][here, :], rights[0][...])
        for left, right in zip(lefts[1:], rights[1:]):
            total = total + dot_nt(left[here, :], right[...])
        out_ref[here, :] = total.astype(bf16)


def cost_of(flops):
    return pl.CostEstimate(flops=flops // 2, bytes_accessed=1 << 20, transcendentals=0)


def sum_nt(lefts, rights):
    rows, width = lefts[0].shape[0], rights[0].shape[0]
    return pl.pallas_call(
        lambda *refs: sum_nt_kernel(len(lefts), *refs),
        in_specs=[in_vmem] * (2 * len(lefts)),
        out_specs=in_vmem,
        out_shape=jax.ShapeDtypeStruct((rows, width), bf16),
        compiler_params=pltpu.CompilerParams(vmem_limit_bytes=kernel_bytes),
        cost_estimate=cost_of(2 * rows * width * sum(v.shape[1] for v in lefts)),
        name="sum_nt",
    )(*lefts, *rights)


def up_kernel(normed_ref, weight_ref, bias_ref, act_ref, slope_ref):
    for here in row_tiles(act_ref.shape[0]):
        pre = dot_nn(normed_ref[here, :], weight_ref[...]) + bias_ref[...]
        act, slope = gelu_parts(pre)
        act_ref[here, :] = act.astype(bf16)
        slope_ref[here, :] = slope


def up_project(normed, weight, bias):
    rows, cols = normed.shape[0], weight.shape[1]
    return pl.pallas_call(
        up_kernel,
        in_specs=[in_vmem] * 3,
        out_specs=(in_vmem, in_vmem),
        out_shape=(
            jax.ShapeDtypeStruct((rows, cols), bf16),
            jax.ShapeDtypeStruct((rows, cols), f32),
        ),
        compiler_params=pltpu.CompilerParams(vmem_limit_bytes=kernel_bytes),
        cost_estimate=cost_of(2 * rows * cols * normed.shape[1]),
        name="up_project",
    )(normed, weight, bias[None, :])


def down_back_kernel(kept_ref, weight_ref, slope_ref, pre_ref, bias_ref):
    total = None
    for here in row_tiles(pre_ref.shape[0]):
        grad = (dot_nn(kept_ref[here, :], weight_ref[...]) * slope_ref[here, :]).astype(bf16)
        pre_ref[here, :] = grad
        part = jnp.sum(grad.astype(f32), axis=0, keepdims=True)
        total = part if total is None else total + part
    bias_ref[...] = total


def down_back(kept, weight, slope):
    rows, cols = slope.shape
    pre, bias = pl.pallas_call(
        down_back_kernel,
        in_specs=[in_vmem] * 3,
        out_specs=(in_vmem, in_vmem),
        out_shape=(
            jax.ShapeDtypeStruct((rows, cols), bf16),
            jax.ShapeDtypeStruct((1, cols), f32),
        ),
        compiler_params=pltpu.CompilerParams(vmem_limit_bytes=kernel_bytes),
        cost_estimate=cost_of(2 * rows * cols * kept.shape[1]),
        name="down_back",
    )(kept, weight, slope)
    return pre, bias[0]


def halves_kernel(order, shape, *refs):
    operands, (kept_ref, sent_ref) = refs[:-2], refs[-2:]
    part = operands[0].shape[1] // len(order)
    middle = len(order) // 2
    for index, block in enumerate(order):
        target = kept_ref if index < middle else sent_ref
        rows = slice(index % middle * part, (index % middle + 1) * part)
        col = 0
        number = 0
        for count in shape:
            left = operands[number][:, block * part : (block + 1) * part]
            number += 1
            for _ in range(count):
                right_ref = operands[number]
                number += 1
                size = right_ref.shape[1]
                target[rows, col : col + size] = dot_tn(left, right_ref[...]).astype(bf16)
                col += size


def grad_halves(at, pairs, first):
    rows, width = pairs[0][0].shape
    part = width // at.q_n
    order = at.scatter_order(first)
    middle = at.q_n // 2
    cols = sum(right.shape[1] for _, rights in pairs for right in rights)
    if part % 128 == 0:
        halves = jax.ShapeDtypeStruct((middle * part, cols), bf16)
        operands = [value for left, rights in pairs for value in (left, *rights)]
        return pl.pallas_call(
            lambda *refs: halves_kernel(order, [len(rights) for _, rights in pairs], *refs),
            in_specs=[in_vmem] * len(operands),
            out_specs=(in_vmem, in_vmem),
            out_shape=(halves, halves),
            compiler_params=pltpu.CompilerParams(vmem_limit_bytes=kernel_bytes),
            cost_estimate=pl.CostEstimate(
                flops=rows * width * cols, bytes_accessed=1 << 20, transcendentals=0
            ),
            name="grad_halves",
        )(*operands)
    return tuple(
        jnp.concatenate(
            [
                jnp.concatenate(
                    [
                        dot_tn(left[:, k * part : (k + 1) * part], right).astype(bf16)
                        for left, rights in pairs
                        for right in rights
                    ],
                    axis=1,
                )
                for k in side
            ],
            axis=0,
        )
        for side in (order[:middle], order[middle:])
    )


def adjust(weight, first, second, gradient, decay_rate, first_fix, second_fix):
    first_new = 0.9 * first + 0.1 * gradient
    second_new = 0.999 * second + 0.001 * gradient * gradient
    update = (
        first_new / first_fix / (jnp.sqrt(second_new / second_fix) + adam_eps) + decay_rate * weight
    )
    return (first_new, second_new, update)


def in_order(c, mine, other):
    return jnp.where(c == 0, mine, other), jnp.where(c == 0, other, mine)


def adjust_into(index, weight, moments_ref, gradient, fixes_ref, state_ref, update_ref, sums_ref):
    first_new, second_new, update = adjust(
        weight, moments_ref[0], moments_ref[1], gradient, weight_decay, fixes_ref[0], fixes_ref[1]
    )
    state_ref[0] = first_new
    state_ref[1] = second_new
    update_ref[...] = update
    sums_ref[2 * index] = jnp.sum(weight * weight)
    sums_ref[2 * index + 1] = jnp.sum(update * update)


def adjust_attn_kernel(
    place_ref, fixes_ref, mine_ref, other_ref, qkv_ref, out_ref, qkv_moments, out_moments,
    qkv_state, out_state, qkv_update, out_update, sums_ref,
):
    size = qkv_ref.shape[2] // 2
    one, two = in_order(place_ref[1], mine_ref[...], other_ref[...])
    parts = [
        jnp.concatenate([one[:, j * size : (j + 1) * size], two[:, j * size : (j + 1) * size]], 1)
        for j in range(4)
    ]
    adjust_into(
        0, qkv_ref[...], qkv_moments, jnp.stack(parts[:3]), fixes_ref, qkv_state, qkv_update, sums_ref
    )
    adjust_into(
        1, out_ref[...], out_moments, parts[3].T, fixes_ref, out_state, out_update, sums_ref
    )


def adjust_mlp_kernel(
    place_ref, fixes_ref, mine_ref, other_ref, up_ref, down_ref, up_moments, down_moments,
    up_state, down_state, up_update, down_update, sums_ref,
):
    size = up_ref.shape[1] // 2
    one, two = in_order(place_ref[1], mine_ref[...], other_ref[...])
    down_grad = jnp.concatenate([one[:, :size], two[:, :size]], axis=1)
    up_grad = jnp.concatenate([one[:, size:], two[:, size:]], axis=1)
    adjust_into(0, up_ref[...], up_moments, up_grad, fixes_ref, up_state, up_update, sums_ref)
    adjust_into(
        1, down_ref[...], down_moments, down_grad.T, fixes_ref, down_state, down_update, sums_ref
    )


def own_spec(shape, dim, count):
    block = list(shape)
    block[dim] //= count
    return pl.BlockSpec(
        tuple(block), lambda i, p: tuple(p[0] if d == dim else 0 for d in range(len(shape)))
    )


def whole_spec(shape):
    return pl.BlockSpec(shape, lambda i, p: (0,) * len(shape))


def adjust_pair(at, kernel, place, fixes, mine, other, weights, dims, moments):
    parts = [m.shape[1:] for m in moments]
    shapes = [jax.ShapeDtypeStruct(m.shape, f32) for m in moments]
    shapes += [jax.ShapeDtypeStruct(p, f32) for p in parts]
    return pl.pallas_call(
        kernel,
        grid_spec=pltpu.PrefetchScalarGridSpec(
            num_scalar_prefetch=1,
            grid=(1,),
            in_specs=[in_smem, whole_spec(mine.shape), whole_spec(other.shape)]
            + [own_spec(w.shape, d, at.dp_n) for w, d in zip(weights, dims)]
            + [whole_spec(m.shape) for m in moments],
            out_specs=tuple(whole_spec(s.shape) for s in shapes) + (in_smem,),
        ),
        out_shape=tuple(shapes) + (jax.ShapeDtypeStruct((4,), f32),),
        compiler_params=pltpu.CompilerParams(vmem_limit_bytes=back_bytes),
        name="adjust_pair",
    )(place, fixes, mine, other, *weights, *moments)


def apply_kernel(place_ref, rates_ref, *refs):
    count = len(refs) // 3
    for index in range(count):
        refs[2 * count + index][...] = (
            refs[index][...] - rates_ref[index] * refs[count + index][...]
        )


def apply_updates(at, place, rates, weights, dims, updates):
    return pl.pallas_call(
        apply_kernel,
        grid_spec=pltpu.PrefetchScalarGridSpec(
            num_scalar_prefetch=1,
            grid=(1,),
            in_specs=[in_smem]
            + [own_spec(w.shape, d, at.dp_n) for w, d in zip(weights, dims)]
            + [whole_spec(u.shape) for u in updates],
            out_specs=tuple(whole_spec(u.shape) for u in updates),
        ),
        out_shape=tuple(jax.ShapeDtypeStruct(u.shape, f32) for u in updates),
        compiler_params=pltpu.CompilerParams(vmem_limit_bytes=back_bytes),
        name="apply_updates",
    )(place, rates, *weights, *updates)


def norm_parts(values):
    center = values - jnp.mean(values, axis=-1, keepdims=True)
    spread = jnp.mean(center * center, axis=-1, keepdims=True)
    inverse = lax.rsqrt(spread + norm_eps)
    return (center * inverse, inverse)


def norm_back(upstream, normed, inverse, gain_vec):
    scaled = upstream * gain_vec
    return inverse * (
        scaled
        - jnp.mean(scaled, axis=-1, keepdims=True)
        - normed * jnp.mean(scaled * normed, axis=-1, keepdims=True)
    )


def local(
    tokens,
    cotangent,
    lengths,
    buckets,
    step_count,
    qkv_weight,
    out_weight,
    up_weight,
    down_weight,
    up_bias,
    rel_bias,
    norm_vectors,
    qkv_moments,
    out_moments,
    up_moments,
    down_moments,
    bias_moments,
    rel_moments,
    vector_moments,
):
    per, length_rows, width = tokens.shape
    at = Places(per)
    seq_len = length_rows * at.mp_n
    blocks = at.slots
    q_n, c, q = at.q_n, at.c, at.q
    head_width = out_weight.shape[0] // 2
    heads = head_width // HD
    units = up_weight.shape[1] // 2
    bucket_count, local_heads = rel_bias.shape

    other_lengths = at.to_core(lengths)
    all_lengths = jnp.where(
        c == 0,
        jnp.concatenate([lengths, other_lengths]),
        jnp.concatenate([other_lengths, lengths]),
    )
    length = lax.dynamic_slice_in_dim(all_lengths, at.s, 1, 0)
    row_keep = jnp.arange(seq_len)[:, None] < length[0]
    row_mask = row_keep.astype(f32)
    vectors = at.relative(norm_vectors, 1)

    def half(values, dim, size):
        return lax.dynamic_slice_in_dim(values, c * size, size, dim)

    part = width // q_n
    small_own = jnp.concatenate(
        [half(up_bias, 0, units), half(rel_bias, 1, heads).T.reshape(-1)]
    )
    qkv_cols = 3 * head_width
    attn_cols = 4 * head_width
    high = lax.reduce_precision(small_own, 8, 7)
    rest = small_own - high
    mid = lax.reduce_precision(rest, 8, 7)
    three = jnp.concatenate([high, mid, rest - mid]).astype(bf16)
    small_rows = -(-three.size // (16 * attn_cols)) * 16
    three = jnp.pad(three, (0, small_rows * attn_cols - three.size)).reshape(small_rows, attn_cols)

    def small_of(rows_low):
        flat = rows_low.reshape(-1).astype(f32)
        count = small_own.size
        return (flat[:count] + flat[count : 2 * count]) + flat[2 * count : 3 * count]

    tokens_near = at.relative(tokens, 2)
    token_pieces = {step: at.collect_piece(tokens_near, step) for step in (0, 2, 3, 1)}
    qkv_own, out_own, attn_piece = pack_attn(
        at, qkv_weight, out_weight, head_width, tokens_near
    )
    attn_piece = jnp.concatenate([attn_piece, three], axis=0)
    attn_one = at.to_slot(attn_piece, 1)
    up_own, down_own, up_piece, down_piece = pack_mlp(
        at, up_weight, down_weight, head_width, units, attn_piece
    )
    mlp_piece = jnp.concatenate([up_piece, down_piece], axis=1)
    attn_one = after(attn_one, token_pieces[1], mlp_piece)
    attn_inner = at.spread_inner(attn_piece, attn_one)
    attn_near = at.gather_start(attn_one[:part])
    tokens_there = (after(token_pieces[2], attn_one), token_pieces[3])
    token_pieces[2] = tokens_there[0]
    mlp_one = at.to_slot(after(mlp_piece, *tokens_there), 1)
    inputs_home = at.collect_end([token_pieces[k] for k in range(blocks)])
    attn_pieces = at.gather_end(
        attn_one[:part], {b: after(v, *tokens_there) for b, v in attn_near.items()}, 0
    )
    inputs_low = at.collect_both(inputs_home)
    inputs_low = after(inputs_low, attn_inner, *attn_pieces)
    attn_outer = at.spread_outer(attn_inner)
    up_one, down_one = mlp_one[:, :units], mlp_one[:, units:]
    up_inner = at.spread_inner(up_piece, up_one)
    mlp_near = at.gather_start(mlp_one)
    turn = 1 % len(at.q_bits)
    attn_pair = at.spread_pair(attn_inner, attn_outer)
    pair_first = after(attn_pair[:part], *mlp_near.values(), up_inner)
    small = [
        small_own,
        small_of(attn_one[part:]),
        small_of(attn_pair[part:, :attn_cols]),
        small_of(attn_pair[part:, attn_cols:]),
    ]
    tile = tile_of(seq_len)
    tiles = seq_len // tile
    padded = jnp.concatenate([jnp.zeros((tile,), jnp.int32), buckets])
    spread = jnp.concatenate(
        [padded[kk * tile : (kk + 2) * tile] for kk in range(tiles)]
    )
    choose = (jnp.arange(bucket_count, dtype=jnp.int32)[:, None] == spread[None, :]).astype(f32)

    def lines_of(r):
        rel_rows = small[r][units:].reshape(heads, bucket_count)
        return jnp.dot(rel_rows, choose, precision=lax.Precision.HIGHEST)


    columns = range(q_n)
    qkv_one, out_one = join(
        attn_pieces,
        part,
        [
            [[(k, 0, qkv_cols)] for k in columns],
            [[(k, qkv_cols, head_width)] for k in columns],
        ],
    )
    qkv_w, out_w = [qkv_own, qkv_one], [out_own, out_one]

    first_parts = norm_parts(inputs_low.astype(f32))
    first_normed, first_inverse = first_parts
    first_low = (first_normed * vectors[0] + vectors[1]).astype(bf16)
    qkv, contexts, totals = [], [], []

    def attention(r, *others):
        qkv.append(after(dot_nn(first_low, qkv_w[r]).astype(bf16), *others))
        context, total = attend(length, qkv[r], lines_of(r), heads)
        contexts.append(context)
        totals.append(total)

    attention(0, mlp_one)
    pair_first = after(pair_first, contexts[0])
    pair_near = at.gather_start(pair_first)
    up_outer = at.spread_outer(after(up_inner, *mlp_near.values()))
    down_inner = at.spread_inner(after(down_piece, up_inner, *mlp_near.values()), down_one)
    attention(1, attn_outer)
    near_done = (*pair_near.values(), up_outer, down_inner)
    pair_near = {b: after(v, *near_done, contexts[1]) for b, v in pair_near.items()}
    pair_pieces = []
    for k in range(2):
        cols = slice(k * attn_cols, (k + 1) * attn_cols)
        pair_pieces.append(
            at.gather_end(
                pair_first[:, cols], {b: v[:, cols] for b, v in pair_near.items()}, k * turn
            )
        )
    down_outer = at.spread_outer(after(down_inner, *near_done))
    incoming_near = at.relative(after(cotangent, *near_done), 2)
    incoming_pieces = {step: at.collect_piece(incoming_near, step) for step in (2, 3)}
    pair_done = [v for pieces in pair_pieces for v in pieces[1:]]
    mlp_near = {b: after(v, *pair_done) for b, v in mlp_near.items()}
    up_one_pieces = at.gather_end(up_one, {b: v[:, :units] for b, v in mlp_near.items()}, 0)
    down_one_pieces = at.gather_end(
        down_one, {b: v[:, units:] for b, v in mlp_near.items()}, turn
    )
    one_done = (*up_one_pieces, *down_one_pieces, down_outer)
    up_pair = after(at.spread_pair(up_inner, up_outer), *one_done)
    up_near = at.gather_start(up_pair)
    incoming_near = after(incoming_near, *one_done)
    incoming_pieces.update({step: at.collect_piece(incoming_near, step) for step in (0, 1)})
    down_pair = after(at.spread_pair(down_inner, down_outer), *up_near.values())

    def pair_halves(piece, near):
        halves = []
        for k in range(2):
            cols = slice(k * units, (k + 1) * units)
            halves.append(
                at.gather_end(piece[:, cols], {b: v[:, cols] for b, v in near.items()}, k * turn)
            )
        return halves

    def pair_join(halves):
        return join(
            halves[0] + halves[1], part, [[[(k, 0, units), (k + q_n, 0, units)] for k in columns]]
        )[0]

    up_halves = pair_halves(up_pair, up_near)
    down_near = at.gather_start(down_pair)
    down_near = {b: after(v, up_halves[0][-1], up_halves[1][-1]) for b, v in down_near.items()}
    down_halves = pair_halves(down_pair, down_near)
    joined = join(
        pair_pieces[0] + pair_pieces[1],
        part,
        [
            [[(k + half_at, start, size)] for k in columns]
            for half_at in (0, q_n)
            for start, size in ((0, qkv_cols), (qkv_cols, head_width))
        ],
    )
    qkv_w += joined[0::2]
    out_w += joined[1::2]
    attention(2, *one_done)
    attention(3, *up_near.values())
    incoming_home = at.collect_end([incoming_pieces[k] for k in range(blocks)])
    rows_of = [[(k, 0, units)] for k in columns]
    up_w = [up_own, join(up_one_pieces, part, [rows_of])[0], pair_join(up_halves)]
    down_w = [down_own, join(down_one_pieces, part, [rows_of])[0], pair_join(down_halves)]

    inputs = inputs_low.astype(f32)
    mixed = at.sum_team(sum_nt(contexts, out_w))
    mixed = after(mixed, *up_near.values())
    middle = inputs + (mixed + vectors[4]) * row_mask
    second_normed, second_inverse = norm_parts(middle)
    second_low = (second_normed * vectors[2] + vectors[3]).astype(bf16)
    acts, slopes = [], []
    biases = [small[0][:units], small[1][:units], jnp.concatenate([small[2][:units], small[3][:units]])]
    for r in range(3):
        act, slope = up_project(second_low, up_w[r], biases[r])
        acts.append(act)
        slopes.append(slope)
    incoming_low = at.collect_both(incoming_home)
    kept = jnp.where(row_keep, incoming_low, jnp.zeros_like(incoming_low))
    fed_bias_grad = jnp.sum(kept.astype(f32), axis=0)
    bias_grads = [None] * blocks

    pre_pair, bias_pair = down_back(kept, down_w[2], slopes[2])
    bias_grads[2], bias_grads[3] = bias_pair[:units], bias_pair[units:]
    up_far_halves = grad_halves(at, [(second_low, [pre_pair])], 1)
    up_far = ChipSum(at, up_far_halves, 1)
    down_far_halves = grad_halves(at, [(after(kept, *up_far_halves), [acts[2]])], 0)
    down_far = ChipSum(at, down_far_halves, 0)
    down_near_halves = grad_halves(at, [(after(kept, *down_far_halves), acts[:2])], 0)
    fed_low = sum_nt([after(acts[0], *down_far_halves)] + acts[1:], down_w)
    fed_share = at.sum_share(fed_low, length_rows)
    middle_share = at.share(middle, length_rows, 0, 0)
    mask_share = at.share(row_mask, length_rows, 0, 0)
    out_share = (middle_share + (fed_share + vectors[5]) * mask_share).astype(bf16)
    out_got = at.deliver_first(out_share)
    kept_late = after(kept, fed_low, *down_far_halves)
    pre_own, bias_grads[0] = down_back(kept_late, down_w[0], slopes[0])
    pre_one, bias_grads[1] = down_back(kept_late, down_w[1], slopes[1])
    back_low = sum_nt([pre_own, pre_one, pre_pair], up_w)
    up_near_halves = grad_halves(at, [(after(second_low, back_low), [pre_own, pre_one])], 1)
    second_grad = at.sum_team(back_low)
    second_grad = after(second_grad, *up_near_halves)
    lead = jnp.where((c == 0) & (at.t == 0), 1.0, 0.0)
    gain_two = jnp.sum(second_grad * second_normed, axis=0)
    shift_two = jnp.sum(second_grad, axis=0)
    middle_grad = incoming_low.astype(f32) + norm_back(
        second_grad, second_normed, second_inverse, vectors[2]
    )
    branch = jnp.where(row_keep, middle_grad, 0.0).astype(bf16)
    mix_bias_grad = jnp.sum(branch.astype(f32), axis=0)
    rel_grads = [None] * blocks
    branch = after(branch, up_far.got, down_far.got)
    context_grads = [dot_nn(branch, out_w[r]).astype(bf16) for r in range(blocks)]
    own_cols = slice(0, units)
    far_cols = slice(units, 2 * units)
    attn_sums = [None] * blocks
    attn_halves = [None] * blocks
    proj_grads = [None] * blocks
    for r in reversed(range(blocks)):
        context_grad = context_grads[r]
        if r == 3:
            up_far.rest(down_far.got)
            down_far.rest(up_far.got)
        if r == 2:
            far_done = (up_far.got, down_far.got)
            context_grad = after(context_grad, *far_done)
            down_near_sum = ChipSum(at, [after(v, *far_done) for v in down_near_halves], 0)
            up_near_sum = ChipSum(at, [after(v, *far_done) for v in up_near_halves], 1)
            far_sums = (down_far.total(), up_far.total())
            mlp_far = jnp.concatenate(
                [v[:, cols] for cols in (own_cols, far_cols) for v in far_sums], axis=1
            ).astype(bf16)
            far_got = at.fold_outer(mlp_far)
        if r == 1:
            context_grad = after(context_grad, out_got)
        if r == 0:
            near_firsts = (down_near_sum.got, up_near_sum.got)
            context_grad = after(context_grad, *near_firsts, far_got)
            mlp_far = at.fold_add(mlp_far, after(far_got, *near_firsts))
            inner_got = at.fold_inner(mlp_far)
            out_pair = at.deliver_pair(out_share, after(out_got, far_got))
            out_last = at.deliver_last(out_pair)
            down_near_sum.rest(*near_firsts)
            up_near_sum.rest(*near_firsts)
            near_done = (down_near_sum.got, up_near_sum.got)
        proj_grad, dist = attend_back(
            length, qkv[r], lines_of(r), totals[r], context_grad, heads
        )
        rel_grads[r] = dist
        attn_halves[r] = grad_halves(
            at, [(first_low, [proj_grad]), (branch, [contexts[r]])], r % 2
        )
        proj_grads[r] = proj_grad
    back_low = after(sum_nt(proj_grads, qkv_w), *near_done)
    for k in (3, 2):
        attn_sums[k] = ChipSum(at, [after(v, *near_done) for v in attn_halves[k]], k % 2)
    firsts = (attn_sums[3].got, attn_sums[2].got)
    first_grad = at.sum_share(back_low, length_rows)
    for k in (1, 0):
        attn_sums[k] = ChipSum(at, [after(v, *firsts) for v in attn_halves[k]], k % 2)
    for k in (3, 2):
        attn_sums[k].rest(*firsts)
    first_grad = after(first_grad, *firsts)
    attn_far = jnp.concatenate([attn_sums[2].total(), attn_sums[3].total()], axis=1).astype(bf16)
    attn_got = at.fold_outer(attn_far)
    for k in (1, 0):
        attn_sums[k].rest(attn_sums[2].got, attn_sums[3].got, attn_sums[0].got, attn_sums[1].got)
    mlp_size = 2 * units
    mlp_near = (down_near_sum.total(), up_near_sum.total())
    mlp_one = jnp.concatenate([v[:, far_cols] for v in mlp_near], axis=1)
    mlp_own = jnp.concatenate([v[:, own_cols] for v in mlp_near], axis=1)
    mlp_one = (mlp_one + inner_got[:, :mlp_size].astype(f32)).astype(bf16)
    last_got = at.to_slot(mlp_one, 1)
    mlp_mine = mlp_own + inner_got[:, mlp_size:].astype(f32) + last_got.astype(f32)
    attn_got = after(attn_got, attn_sums[0].got, attn_sums[1].got)
    attn_inner_got = at.fold_inner(at.fold_add(attn_far, attn_got))
    attn_one_sum = attn_inner_got[:, :attn_cols].astype(f32) + attn_sums[1].total()
    attn_last_got = at.to_slot(attn_one_sum.astype(bf16), 1)
    attn_mine = (
        attn_sums[0].total()
        + attn_inner_got[:, attn_cols:].astype(f32)
        + attn_last_got.astype(f32)
    )
    rel_grad = lax.dot_general(
        jnp.concatenate(rel_grads, axis=0),
        choose,
        (((1,), (1,)), ((), ())),
        precision=lax.Precision.HIGHEST,
    )
    normed_share = at.share(first_normed, length_rows, 0, 0)
    inverse_share = at.share(first_inverse, length_rows, 0, 0)
    middle_grad_share = at.share(middle_grad, length_rows, 0, 0)
    gain_one = jnp.sum(first_grad * normed_share, axis=0)
    shift_one = jnp.sum(first_grad, axis=0)
    input_share = middle_grad_share + norm_back(
        first_grad, normed_share, inverse_share, vectors[0]
    )
    input_low = input_share.astype(bf16)
    input_got = at.deliver_first(after(input_low, attn_got))
    input_pair = at.deliver_pair(input_low, input_got)
    input_last = at.deliver_last(input_pair)
    input_grad = at.relative(at.delivered(input_pair, input_last), 2).astype(f32)

    def by_place(rows_of):
        around = jnp.stack(rows_of)
        moved = []
        for place in range(blocks):
            picked = around[0]
            for k in range(1, blocks):
                picked = jnp.where(at.s ^ k == place, around[k], picked)
            moved.append(picked)
        moved = jnp.stack(moved)[:, None, None, :]
        here = (jnp.arange(at.t_n)[:, None] == at.t) & (jnp.arange(2)[None, :] == c)
        return jnp.where(here[None, :, :, None], moved, 0.0).reshape(at.mp_n, 2, -1)

    vector_grad = jnp.concatenate(
        [
            jnp.stack([gain_one, shift_one]),
            lead * jnp.stack([gain_two, shift_two, mix_bias_grad, fed_bias_grad]),
        ]
    )
    small_grad = by_place(
        [
            jnp.concatenate([bias_grads[r], rel_grad[r * heads : (r + 1) * heads].reshape(-1)])
            for r in range(blocks)
        ]
    )
    joined = at.sum_all(
        jnp.concatenate([at.relative(vector_grad, 1).reshape(-1), small_grad.reshape(-1)]),
        attn_inner_got,
        last_got,
    )
    vector_grad = joined[: vector_grad.size].reshape(vector_grad.shape)
    small_sum = lax.dynamic_index_in_dim(
        joined[vector_grad.size :].reshape(small_grad.shape), at.mp_i, 0, keepdims=False
    )
    bias_sum = small_sum[:, :units].reshape(-1)
    rel_sum = small_sum[:, units:].reshape(2 * heads, bucket_count).T

    rows = part // 2

    def exchanged(mine):
        sent = lax.dynamic_slice_in_dim(mine, (1 - c) * rows, rows, 0)
        return lax.dynamic_slice_in_dim(mine, c * rows, rows, 0), at.to_core(sent)

    mlp_mine, mlp_other = exchanged(mlp_mine)
    attn_mine, attn_other = exchanged(attn_mine)

    steps_done = step_count[0].astype(f32)
    first_fix = 1.0 - jnp.power(jnp.float32(0.9), steps_done)
    second_fix = 1.0 - jnp.power(jnp.float32(0.999), steps_done)
    vector_pieces = [
        (up_bias, bias_moments, bias_sum),
        (rel_bias, rel_moments, rel_sum),
        (norm_vectors, vector_moments, vector_grad),
    ]
    vector_adjusted = [
        adjust(weight, moments[0], moments[1], grad, 0.0, first_fix, second_fix)
        for weight, moments, grad in vector_pieces
    ]
    qkv_view = jnp.transpose(qkv_weight, (1, 0, 2))
    qkv_mom = jnp.transpose(qkv_moments, (0, 2, 1, 3))
    weights = [qkv_view, out_weight, up_weight, down_weight]
    dims = [1, 1, 0, 1]
    in_kernels = rows % 128 == 0
    if in_kernels:
        place = jnp.stack([at.dp_i, c]).astype(jnp.int32)
        fixes = jnp.stack([first_fix, second_fix])
        up_state, down_state, up_update, down_update, mlp_squares = adjust_pair(
            at, adjust_mlp_kernel, place, fixes, mlp_mine, mlp_other,
            weights[2:], dims[2:], [up_moments, down_moments],
        )
        qkv_state, out_state, qkv_update, out_update, attn_squares = adjust_pair(
            at, adjust_attn_kernel, place, fixes, attn_mine, attn_other,
            weights[:2], dims[:2], [qkv_mom, out_moments],
        )
        squares = jnp.concatenate([attn_squares, mlp_squares])
        updates = [qkv_update, out_update, up_update, down_update]
        states = [qkv_state, out_state, up_state, down_state]
    else:
        one, two = in_order(c, attn_mine, attn_other)
        parts = [
            jnp.concatenate(
                [v[:, j * head_width : (j + 1) * head_width] for v in (one, two)], axis=1
            )
            for j in range(4)
        ]
        one, two = in_order(c, mlp_mine, mlp_other)
        grads = [
            jnp.stack(parts[:3]),
            parts[3].T,
            jnp.concatenate([one[:, units:], two[:, units:]], axis=1),
            jnp.concatenate([one[:, :units], two[:, :units]], axis=1).T,
        ]
        own_weights, updates, states, squares = [], [], [], []
        for weight, dim, moments, grad in zip(
            weights, dims, [qkv_mom, out_moments, up_moments, down_moments], grads
        ):
            count = weight.shape[dim] // at.dp_n
            weight = lax.dynamic_slice_in_dim(weight, at.dp_i * count, count, dim)
            first_new, second_new, update = adjust(
                weight, moments[0], moments[1], grad, weight_decay, first_fix, second_fix
            )
            own_weights.append(weight)
            updates.append(update)
            states.append(jnp.stack([first_new, second_new]))
            squares += [jnp.sum(weight * weight), jnp.sum(update * update)]
        squares = jnp.stack(squares)
    lead_dp = (at.dp_i == 0).astype(f32)
    small_squares = jnp.stack(
        [
            lead_dp * jnp.sum(values * values)
            for values in (up_bias, vector_adjusted[0][2], rel_bias, vector_adjusted[1][2])
        ]
    )
    squares = at.sum_all(jnp.concatenate([squares, small_squares])).reshape(6, 2)
    vector_squares = jnp.stack(
        [jnp.sum(v * v, axis=1) for v in (norm_vectors, vector_adjusted[2][2])], axis=1
    )
    norms = jnp.sqrt(jnp.concatenate([squares, vector_squares]))
    rates = learn_rate * (norms[:, 0] / (norms[:, 1] + adam_eps))
    if in_kernels:
        new = apply_updates(at, place, rates[:4], weights, dims, updates)
    else:
        new = [own_weights[k] - rates[k] * updates[k] for k in range(4)]
    new, states = list(new), list(states)
    new[0] = jnp.transpose(new[0], (1, 0, 2))
    states[0] = jnp.transpose(states[0], (0, 2, 1, 3))
    block_out = at.relative(at.delivered(out_pair, out_last), 2)
    results = [block_out, input_grad]
    for k in range(4):
        results += [new[k], states[k]]
    for k in range(2):
        first_new, second_new, update = vector_adjusted[k]
        results.append(vector_pieces[k][0] - rates[4 + k] * update)
        results.append(jnp.stack([first_new, second_new]))
    first_new, second_new, update = vector_adjusted[2]
    results.append(norm_vectors - rates[6:, None] * update)
    results.append(jnp.stack([first_new, second_new]))
    results.append(norms.T)
    return tuple(results)


def solution(mesh):
    return jax.shard_map(
        local,
        mesh=mesh,
        in_specs=(
            P("dp", "mp", None),
            P("dp", "mp", None),
            P("dp"),
            P(),
            P(),
            P(None, None, "mp"),
            P("mp", None),
            P(None, "mp"),
            P("mp", None),
            P("mp"),
            P(None, "mp"),
            P(),
            P(None, "dp", None, "mp"),
            P(None, "mp", "dp"),
            P(None, "dp", "mp"),
            P(None, "mp", "dp"),
            P(None, "mp"),
            P(None, None, "mp"),
            P(),
        ),
        out_specs=(
            P("dp", "mp", None),
            P("dp", "mp", None),
            P("dp", None, "mp"),
            P(None, "dp", None, "mp"),
            P("mp", "dp"),
            P(None, "mp", "dp"),
            P("dp", "mp"),
            P(None, "dp", "mp"),
            P("mp", "dp"),
            P(None, "mp", "dp"),
            P("mp"),
            P(None, "mp"),
            P(None, "mp"),
            P(None, None, "mp"),
            P(),
            P(),
            P(),
        ),
        check_vma=False,
    )
```

```python
import jax
import jax.numpy as jnp
from jax import lax
from jax.experimental import pallas as pl
from jax.experimental.pallas import tpu as pltpu
from jax.sharding import PartitionSpec as P

HD = 64
f32 = jnp.float32
bf16 = jnp.bfloat16

norm_eps = 1e-05
adam_eps = 1e-06
learn_rate = 0.25
weight_decay = 0.1
masked_score = -1000000000.0
score_scale = HD ** (-0.5)
kernel_bytes = 12 << 20
back_bytes = 16 << 20

in_vmem = pl.BlockSpec(memory_space=pltpu.VMEM)
in_smem = pl.BlockSpec(memory_space=pltpu.SMEM)


def dot_nt(left, right):
    return lax.dot_general(left, right, (((1,), (1,)), ((), ())), preferred_element_type=f32)


def dot_nn(left, right):
    return lax.dot_general(left, right, (((1,), (0,)), ((), ())), preferred_element_type=f32)


def dot_tn(left, right):
    return lax.dot_general(left, right, (((0,), (0,)), ((), ())), preferred_element_type=f32)


def tile_of(rows):
    return min(256, rows)


def bias_tiles(line_ref, head, tiles, tile):
    causal = lax.broadcasted_iota(jnp.int32, (tile, tile), 0) <= lax.broadcasted_iota(
        jnp.int32, (tile, tile), 1
    )
    made = []
    for kk in range(tiles):
        line = line_ref[head : head + 1, kk * 2 * tile : (kk + 1) * 2 * tile]
        wide = jnp.broadcast_to(line, (tile, 2 * tile))
        made.append(pltpu.roll(wide, tile, 1, stride=1, stride_axis=0)[:, :tile])
    made[0] = jnp.where(causal, made[0], masked_score)
    return made


def scores_of(keys, query, toeplitz, block, tile, key_pos, length):
    count = (block + 1) * tile
    raw = dot_nt(keys[:count], query)
    raw = raw + jnp.concatenate([toeplitz[block - j] for j in range(block + 1)], axis=0)
    return jnp.where(key_pos[:count] < length, raw, masked_score)


def attend_kernel(heads, length_ref, qkv_ref, line_ref, ctx_ref, lse_ref):
    rows = qkv_ref.shape[0]
    tile = tile_of(rows)
    tiles = rows // tile
    width = heads * HD
    length = length_ref[0]
    key_pos = lax.broadcasted_iota(jnp.int32, (rows, tile), 0)
    for head in range(heads):
        toeplitz = bias_tiles(line_ref, head, tiles, tile)
        cols = slice(head * HD, (head + 1) * HD)
        keys = qkv_ref[:, width + head * HD : width + (head + 1) * HD]
        vals = qkv_ref[:, 2 * width + head * HD : 2 * width + (head + 1) * HD]
        for block in range(tiles):
            here = slice(block * tile, (block + 1) * tile)
            count = (block + 1) * tile
            query = qkv_ref[here, cols] * jnp.asarray(score_scale, bf16)
            raw = scores_of(keys, query, toeplitz, block, tile, key_pos, length)
            top = jnp.max(raw, axis=0, keepdims=True)
            grown = jnp.exp(raw - top)
            total = jnp.sum(grown, axis=0, keepdims=True)
            probs = (grown * (1.0 / total)).astype(bf16)
            ctx_ref[here, cols] = dot_tn(probs, vals[:count]).astype(bf16)
            lse_ref[head : head + 1, here] = top + jnp.log(total)


def attend_back_kernel(
    heads,
    length_ref,
    qkv_ref,
    line_ref,
    lse_ref,
    grad_ref,
    out_ref,
    dist_ref,
    key_acc,
    val_acc,
    diag_acc,
):
    rows = qkv_ref.shape[0]
    tile = tile_of(rows)
    tiles = rows // tile
    width = heads * HD
    length = length_ref[0]
    key_pos = lax.broadcasted_iota(jnp.int32, (rows, tile), 0)
    for head in range(heads):
        toeplitz = bias_tiles(line_ref, head, tiles, tile)
        cols = slice(head * HD, (head + 1) * HD)
        key_cols = slice(width + head * HD, width + (head + 1) * HD)
        val_cols = slice(2 * width + head * HD, 2 * width + (head + 1) * HD)
        keys = qkv_ref[:, key_cols]
        vals = qkv_ref[:, val_cols]
        key_acc[...] = jnp.zeros_like(key_acc)
        val_acc[...] = jnp.zeros_like(val_acc)
        diag_acc[...] = jnp.zeros_like(diag_acc)
        for block in range(tiles):
            here = slice(block * tile, (block + 1) * tile)
            count = (block + 1) * tile
            query = qkv_ref[here, cols] * jnp.asarray(score_scale, bf16)
            grad = grad_ref[here, cols]
            raw = scores_of(keys, query, toeplitz, block, tile, key_pos, length)
            probs = jnp.exp(raw - lse_ref[head : head + 1, here])
            pgrad = dot_nt(vals[:count], grad)
            drop = jnp.sum(probs * pgrad, axis=0, keepdims=True)
            sgrad = (probs * (pgrad - drop)).astype(bf16)
            val_acc[:count] += dot_nn(probs.astype(bf16), grad)
            key_acc[:count] += dot_nn(sgrad, query)
            out_ref[here, cols] = (dot_tn(sgrad, keys[:count]) * score_scale).astype(bf16)
            wide = sgrad.astype(f32)
            for j in range(block + 1):
                diag_acc[block - j] += wide[j * tile : (j + 1) * tile]
        out_ref[:, key_cols] = key_acc[...].astype(bf16)
        out_ref[:, val_cols] = val_acc[...].astype(bf16)
        for kk in range(tiles):
            held = jnp.concatenate([diag_acc[kk], jnp.zeros((tile, tile), f32)], axis=1)
            half = tile // 2
            while half >= 1:
                held = held[:half] + pltpu.roll(held[half : 2 * half], 2 * tile - half, 1)
                half //= 2
            dist_ref[head : head + 1, kk * 2 * tile : (kk + 1) * 2 * tile] = pltpu.roll(held, tile, 1)


def attend(length, qkv, line, heads):
    rows = qkv.shape[0]
    return pl.pallas_call(
        lambda *refs: attend_kernel(heads, *refs),
        out_shape=(
            jax.ShapeDtypeStruct((rows, heads * HD), bf16),
            jax.ShapeDtypeStruct((heads, rows), f32),
        ),
        in_specs=[in_smem, in_vmem, in_vmem],
        out_specs=(in_vmem, in_vmem),
        compiler_params=pltpu.CompilerParams(vmem_limit_bytes=kernel_bytes),
        cost_estimate=pl.CostEstimate(
            flops=heads * rows * rows * HD * 10,
            bytes_accessed=1 << 20,
            transcendentals=0,
        ),
        name="attend",
    )(length, qkv, line)


def attend_back(length, qkv, line, lse, grad, heads):
    rows = qkv.shape[0]
    tile = tile_of(rows)
    return pl.pallas_call(
        lambda *refs: attend_back_kernel(heads, *refs),
        out_shape=(
            jax.ShapeDtypeStruct((rows, 3 * heads * HD), bf16),
            jax.ShapeDtypeStruct((heads, 2 * rows), f32),
        ),
        in_specs=[in_smem, in_vmem, in_vmem, in_vmem, in_vmem],
        out_specs=(in_vmem, in_vmem),
        scratch_shapes=[
            pltpu.VMEM((rows, HD), f32),
            pltpu.VMEM((rows, HD), f32),
            pltpu.VMEM((rows // tile, tile, tile), f32),
        ],
        compiler_params=pltpu.CompilerParams(vmem_limit_bytes=back_bytes),
        cost_estimate=pl.CostEstimate(
            flops=heads * rows * rows * HD * 20,
            bytes_accessed=1 << 20,
            transcendentals=0,
        ),
        name="attend_back",
    )(length, qkv, line, lse, grad)


def tie(*values):
    return lax.optimization_barrier(values)


def after(values, *others):
    return lax.optimization_barrier((values, *others))[0]


class Places:
    def __init__(self, per):
        self.per = per
        self.dp_n = lax.axis_size("dp")
        self.mp_n = lax.axis_size("mp")
        self.q_n = self.dp_n // 2
        self.slots = 2 * per
        self.t_n = self.mp_n // self.slots
        assert self.dp_n % 2 == 0 and self.mp_n % self.slots == 0
        dp_i = lax.axis_index("dp")
        mp_i = lax.axis_index("mp")
        self.dp_i, self.mp_i = dp_i, mp_i
        self.q, self.c = dp_i // 2, lax.rem(dp_i, 2)
        self.s, self.t = mp_i // self.t_n, lax.rem(mp_i, self.t_n)
        assert per == 2
        self.home = self.s // per
        self.at_home = self.c == self.home
        self.q_bits = []
        while (1 << len(self.q_bits)) < self.q_n:
            self.q_bits.append(1 << len(self.q_bits))
        assert (1 << len(self.q_bits)) == self.q_n

    def move(self, values, target):
        pairs = []
        for q in range(self.q_n):
            for c in range(2):
                for s in range(self.slots):
                    for t in range(self.t_n):
                        found = target(q, c, s, t)
                        if found is not None:
                            nq, nc, ns, nt = found
                            pairs.append(
                                (
                                    (q * 2 + c) * self.mp_n + s * self.t_n + t,
                                    (nq * 2 + nc) * self.mp_n + ns * self.t_n + nt,
                                )
                            )
        return lax.ppermute(values, ("dp", "mp"), pairs)

    def to_core(self, values):
        return self.move(values, lambda q, c, s, t: (q, 1 - c, s, t))

    def to_slot(self, values, step):
        return self.move(values, lambda q, c, s, t: (q, c, s ^ step, t))

    def to_chip(self, values, bit):
        return self.move(values, lambda q, c, s, t: (q ^ bit, c, s, t))

    def to_team(self, values, step):
        return self.move(values, lambda q, c, s, t: (q, c, s, (t + step) % self.t_n))

    def relative(self, values, dim):
        size = values.shape[dim] // self.q_n
        return jnp.concatenate(
            [
                lax.dynamic_slice_in_dim(values, (self.q ^ k) * size, size, dim)
                for k in range(self.q_n)
            ],
            axis=dim,
        )

    def block_at(self, step):
        return lax.rem(self.s + step, self.slots) * self.t_n + self.t

    def collect_piece(self, local, step):
        piece = lax.dynamic_index_in_dim(local, (self.s ^ step) % 2, 0, keepdims=False)
        if step == 0:
            return piece
        return self.move(
            piece,
            lambda q, c, s, t: (
                (q, c, s ^ step, t) if (s ^ step) // self.per == c else None
            ),
        )

    def collect_end(self, pieces):
        count, width = pieces[0].shape
        whole = jnp.zeros((count * self.mp_n, width), pieces[0].dtype)
        for step, piece in enumerate(pieces):
            for turn in range(self.t_n):
                piece_t = self.to_team(piece, turn) if turn > 0 else piece
                from_t = lax.rem(self.t + self.t_n - turn, self.t_n)
                whole = lax.dynamic_update_slice_in_dim(
                    whole, piece_t, ((self.s ^ step) * self.t_n + from_t) * count, 0
                )
        return whole

    def collect_both(self, whole):
        other = self.move(
            whole, lambda q, c, s, t: (q, 1 - c, s, t) if c == s // self.per else None
        )
        return jnp.where(self.at_home, whole, other)

    def deliver_first(self, blocks):
        return self.move(
            blocks, lambda q, c, s, t: (q, 1 - c, s ^ 2, t) if c != s // 2 else None
        )

    def deliver_pair(self, blocks, got):
        return jnp.where(self.at_home, blocks, got)

    def deliver_last(self, pair):
        return self.to_slot(pair[pair.shape[0] // 2 :], 1)

    def delivered(self, pair, got):
        mine = pair[: pair.shape[0] // 2]
        even = self.s % 2 == 0
        return jnp.stack([jnp.where(even, mine, got), jnp.where(even, got, mine)])

    def share(self, values, length, flip, team):
        side = jnp.where(self.at_home, 0, 1) ^ flip
        parts = []
        for index in range(self.per):
            slot = self.s ^ (self.per * side + index)
            block = slot * self.t_n + lax.rem(self.t + team, self.t_n)
            parts.append(lax.dynamic_slice_in_dim(values, block * length, length, 0))
        return jnp.concatenate(parts, axis=0)

    def sum_share(self, partial, length):
        total = self.share(partial, length, 0, 0).astype(f32)
        for team in range(self.t_n):
            for flip in (0, 1):
                if (team, flip) != (0, 0):
                    sent = self.share(partial, length, flip, team).astype(bf16)
                    total = total + self.move(
                        sent, lambda q, c, s, t: (q, c ^ flip, s, (t + team) % self.t_n)
                    ).astype(f32)
        return total

    def sum_team(self, partial):
        total = partial.astype(f32)
        total = total + self.to_core(partial).astype(f32)
        if self.t_n > 1:
            low = total.astype(bf16)
            for team in range(1, self.t_n):
                total = total + self.to_team(low, team).astype(f32)
        return total

    def spread_inner(self, own, one):
        both = jnp.concatenate([own, one], axis=1)
        return self.move(both, lambda q, c, s, t: (q, c, s ^ 3, t) if s in (1, 2) else None)

    def spread_outer(self, inner):
        return self.move(inner, lambda q, c, s, t: (q, c, s ^ 1, t) if s in (1, 2) else None)

    def spread_pair(self, inner, outer):
        size = inner.shape[1] // 2
        turned = jnp.concatenate([inner[:, size:], inner[:, :size]], axis=1)
        return jnp.where((self.s == 1) | (self.s == 2), turned, outer)

    def fold_outer(self, far):
        return self.move(far, lambda q, c, s, t: (q, c, s ^ 1, t) if s in (0, 3) else None)

    def fold_add(self, far, got):
        size = far.shape[1] // 2
        turned = jnp.concatenate([got[:, size:], got[:, :size]], axis=1)
        return (far.astype(f32) + turned.astype(f32)).astype(bf16)

    def fold_inner(self, far):
        return self.move(far, lambda q, c, s, t: (q, c, s ^ 3, t) if s in (1, 2) else None)

    def bits_from(self, first):
        return self.q_bits[first:] + self.q_bits[:first]

    def gather_chips(self, piece, first):
        pieces = {0: piece}
        for bit in self.bits_from(first):
            for k in list(pieces):
                pieces[k | bit] = self.to_chip(pieces[k], bit)
        return [pieces[k] for k in range(self.q_n)]

    def gather_start(self, piece):
        return {bit: self.to_chip(piece, bit) for bit in self.q_bits}

    def gather_end(self, piece, near, first):
        pieces = {0: piece}
        for bit in self.bits_from(first):
            for k in list(pieces):
                pieces[k | bit] = near[bit] if k == 0 else self.to_chip(pieces[k], bit)
        return [pieces[k] for k in range(self.q_n)]

    def scatter_order(self, first):
        order = [0]
        for bit in reversed(self.bits_from(first)):
            order = order + [k | bit for k in order]
        return order

    def sum_plane(self, values):
        values = values + self.to_core(values)
        for low in range(0, len(self.q_bits), 2):
            bits = self.q_bits[low : low + 2]
            got = [self.to_chip(values, bit) for bit in bits]
            if len(bits) == 2:
                both = self.to_chip(values, bits[0] | bits[1])
                values = (values + got[0]) + (got[1] + both)
            else:
                values = values + got[0]
        return values

    def sum_column(self, values):
        bit, bits = 1, []
        while bit < self.mp_n:
            bits.append(bit)
            bit *= 2

        def flip(mask):
            def target(q, c, s, t):
                place = (s * self.t_n + t) ^ mask
                return (q, c, place // self.t_n, place % self.t_n)

            return self.move(values, target)

        for low in range(0, len(bits), 2):
            pair = bits[low : low + 2]
            if len(pair) == 2:
                one, two, both = flip(pair[0]), flip(pair[1]), flip(pair[0] | pair[1])
                values = (values + one) + (two + both)
            else:
                values = values + flip(pair[0])
        return values


class ChipSum:
    def __init__(self, at, halves, first):
        self.at = at
        self.bits = list(at.bits_from(first))
        self.parts, sent = [halves[0]], halves[1]
        self.exchange(sent)

    def exchange(self, sent):
        self.got = self.at.to_chip(sent, self.bits.pop(0))
        self.parts.append(self.got)

    def total(self, rows=None):
        total = self.parts[0][rows].astype(f32) if rows else self.parts[0].astype(f32)
        for part in self.parts[1:]:
            total = total + (part[rows] if rows else part).astype(f32)
        return total

    def step(self, *others):
        if not self.bits:
            return
        self.parts[-1] = after(self.parts[-1], *others)
        half = self.got.shape[0] // 2
        sent = self.total(slice(half, None)).astype(bf16)
        self.parts = [part[:half] for part in self.parts]
        self.exchange(sent)

    def rest(self, *others):
        while self.bits:
            self.step(*others)


def pack_attn_kernel(place_ref, qkv_ref, out_ref, qkv_full, out_full, piece_ref):
    size = qkv_ref.shape[2]
    for j in range(3):
        qkv_full[:, j * size : (j + 1) * size] = qkv_ref[j].astype(bf16)
    out_full[...] = out_ref[...].T.astype(bf16)

    @pl.when(pl.program_id(0) == 0)
    def _():
        piece_ref[:, : 3 * size] = qkv_full[...]
        piece_ref[:, 3 * size :] = out_full[...]


def pack_mlp_kernel(place_ref, up_ref, down_ref, up_full, down_full, up_piece, down_piece):
    up_full[...] = up_ref[...].astype(bf16)
    down_full[...] = down_ref[...].T.astype(bf16)

    @pl.when(pl.program_id(0) == 0)
    def _():
        up_piece[...] = up_full[...]
        down_piece[...] = down_full[...]


def packs_in_kernels(at, width, head_width):
    return (width // at.q_n) % 128 == 0 and head_width % 128 == 0


def pack_attn(at, qkv_weight, out_weight, head_width, after):
    width = qkv_weight.shape[0]
    part = width // at.q_n
    if packs_in_kernels(at, width, head_width):
        place = tie(jnp.stack([at.q, at.c]).astype(jnp.int32), after)[0]
        sizes = (3 * head_width, head_width)
        return pl.pallas_call(
            pack_attn_kernel,
            grid_spec=pltpu.PrefetchScalarGridSpec(
                num_scalar_prefetch=1,
                grid=(at.q_n,),
                in_specs=[
                    pl.BlockSpec((3, part, head_width), lambda k, p: (0, p[0] ^ k, p[1])),
                    pl.BlockSpec((head_width, part), lambda k, p: (p[1], p[0] ^ k)),
                ],
                out_specs=tuple(pl.BlockSpec((part, n), lambda k, p: (k, 0)) for n in sizes)
                + (pl.BlockSpec((part, sum(sizes)), lambda k, p: (0, 0)),),
            ),
            out_shape=tuple(jax.ShapeDtypeStruct((width, n), bf16) for n in sizes)
            + (jax.ShapeDtypeStruct((part, sum(sizes)), bf16),),
            name="pack_attn",
        )(place, jnp.transpose(qkv_weight, (1, 0, 2)), out_weight)
    qkv = lax.dynamic_slice_in_dim(qkv_weight, at.c * head_width, head_width, 2)
    out = lax.dynamic_slice_in_dim(out_weight, at.c * head_width, head_width, 0)
    qkv = at.relative(qkv.reshape(width, 3 * head_width).astype(bf16), 0)
    out = at.relative(out.astype(bf16).T, 0)
    return qkv, out, jnp.concatenate([qkv[:part], out[:part]], axis=1)


def pack_mlp(at, up_weight, down_weight, head_width, units, after):
    width = up_weight.shape[0]
    part = width // at.q_n
    if packs_in_kernels(at, width, head_width):
        place = tie(jnp.stack([at.q, at.c]).astype(jnp.int32), after)[0]
        return pl.pallas_call(
            pack_mlp_kernel,
            grid_spec=pltpu.PrefetchScalarGridSpec(
                num_scalar_prefetch=1,
                grid=(at.q_n,),
                in_specs=[
                    pl.BlockSpec((part, units), lambda k, p: (p[0] ^ k, p[1])),
                    pl.BlockSpec((units, part), lambda k, p: (p[1], p[0] ^ k)),
                ],
                out_specs=(
                    pl.BlockSpec((part, units), lambda k, p: (k, 0)),
                    pl.BlockSpec((part, units), lambda k, p: (k, 0)),
                    pl.BlockSpec((part, units), lambda k, p: (0, 0)),
                    pl.BlockSpec((part, units), lambda k, p: (0, 0)),
                ),
            ),
            out_shape=(jax.ShapeDtypeStruct((width, units), bf16),) * 2
            + (jax.ShapeDtypeStruct((part, units), bf16),) * 2,
            name="pack_mlp",
        )(place, up_weight, down_weight)
    up = lax.dynamic_slice_in_dim(up_weight, at.c * units, units, 1).astype(bf16)
    down = lax.dynamic_slice_in_dim(down_weight, at.c * units, units, 0).astype(bf16).T
    up, down = at.relative(up, 0), at.relative(down, 0)
    return up, down, up[:part], down[:part]


def join_kernel(plan, count, *refs):
    pieces, outs = refs[:count], refs[count:]
    for out_ref, (start_cols, rows) in zip(outs, plan):
        part = out_ref.shape[0] // len(rows)
        for k, chunks in enumerate(rows):
            col = 0
            for index, start, size in chunks:
                out_ref[k * part : (k + 1) * part, col : col + size] = pieces[index][
                    :part, start : start + size
                ]
                col += size


def join(pieces, part, plans):
    shapes = [
        jax.ShapeDtypeStruct((part * len(rows), sum(size for _, _, size in rows[0])), bf16)
        for rows in plans
    ]
    return pl.pallas_call(
        lambda *refs: join_kernel([(0, rows) for rows in plans], len(pieces), *refs),
        in_specs=[in_vmem] * len(pieces),
        out_specs=(in_vmem,) * len(plans),
        out_shape=tuple(shapes),
        compiler_params=pltpu.CompilerParams(vmem_limit_bytes=kernel_bytes),
        name="join",
    )(*pieces)


def gelu_parts(values):
    half = 0.5 * (1.0 + lax.erf(values * (0.5**0.5)))
    bell = jnp.exp(-0.5 * values * values) * 0.3989422804014327
    return (values * half, half + values * bell)


def row_tiles(rows, tile=256):
    tile = min(tile, rows)
    return [slice(start, start + tile) for start in range(0, rows, tile)]


def sum_nt_kernel(count, *refs):
    lefts, rights, out_ref = refs[:count], refs[count : 2 * count], refs[-1]
    for here in row_tiles(out_ref.shape[0]):
        total = dot_nt(lefts[0][here, :], rights[0][...])
        for left, right in zip(lefts[1:], rights[1:]):
            total = total + dot_nt(left[here, :], right[...])
        out_ref[here, :] = total.astype(bf16)


def cost_of(flops):
    return pl.CostEstimate(flops=flops // 2, bytes_accessed=1 << 20, transcendentals=0)


def sum_nt(lefts, rights):
    rows, width = lefts[0].shape[0], rights[0].shape[0]
    return pl.pallas_call(
        lambda *refs: sum_nt_kernel(len(lefts), *refs),
        in_specs=[in_vmem] * (2 * len(lefts)),
        out_specs=in_vmem,
        out_shape=jax.ShapeDtypeStruct((rows, width), bf16),
        compiler_params=pltpu.CompilerParams(vmem_limit_bytes=kernel_bytes),
        cost_estimate=cost_of(2 * rows * width * sum(v.shape[1] for v in lefts)),
        name="sum_nt",
    )(*lefts, *rights)


def up_kernel(normed_ref, weight_ref, bias_ref, act_ref, slope_ref):
    for here in row_tiles(act_ref.shape[0]):
        pre = dot_nn(normed_ref[here, :], weight_ref[...]) + bias_ref[...]
        act, slope = gelu_parts(pre)
        act_ref[here, :] = act.astype(bf16)
        slope_ref[here, :] = slope


def up_project(normed, weight, bias):
    rows, cols = normed.shape[0], weight.shape[1]
    return pl.pallas_call(
        up_kernel,
        in_specs=[in_vmem] * 3,
        out_specs=(in_vmem, in_vmem),
        out_shape=(
            jax.ShapeDtypeStruct((rows, cols), bf16),
            jax.ShapeDtypeStruct((rows, cols), f32),
        ),
        compiler_params=pltpu.CompilerParams(vmem_limit_bytes=kernel_bytes),
        cost_estimate=cost_of(2 * rows * cols * normed.shape[1]),
        name="up_project",
    )(normed, weight, bias[None, :])


def down_back_kernel(kept_ref, weight_ref, slope_ref, pre_ref, bias_ref):
    total = None
    for here in row_tiles(pre_ref.shape[0]):
        grad = (dot_nn(kept_ref[here, :], weight_ref[...]) * slope_ref[here, :]).astype(bf16)
        pre_ref[here, :] = grad
        part = jnp.sum(grad.astype(f32), axis=0, keepdims=True)
        total = part if total is None else total + part
    bias_ref[...] = total


def down_back(kept, weight, slope):
    rows, cols = slope.shape
    pre, bias = pl.pallas_call(
        down_back_kernel,
        in_specs=[in_vmem] * 3,
        out_specs=(in_vmem, in_vmem),
        out_shape=(
            jax.ShapeDtypeStruct((rows, cols), bf16),
            jax.ShapeDtypeStruct((1, cols), f32),
        ),
        compiler_params=pltpu.CompilerParams(vmem_limit_bytes=kernel_bytes),
        cost_estimate=cost_of(2 * rows * cols * kept.shape[1]),
        name="down_back",
    )(kept, weight, slope)
    return pre, bias[0]


def halves_kernel(order, shape, *refs):
    operands, (kept_ref, sent_ref) = refs[:-2], refs[-2:]
    part = operands[0].shape[1] // len(order)
    middle = len(order) // 2
    for index, block in enumerate(order):
        target = kept_ref if index < middle else sent_ref
        rows = slice(index % middle * part, (index % middle + 1) * part)
        col = 0
        number = 0
        for count in shape:
            left = operands[number][:, block * part : (block + 1) * part]
            number += 1
            for _ in range(count):
                right_ref = operands[number]
                number += 1
                size = right_ref.shape[1]
                target[rows, col : col + size] = dot_tn(left, right_ref[...]).astype(bf16)
                col += size


def grad_halves(at, pairs, first):
    rows, width = pairs[0][0].shape
    part = width // at.q_n
    order = at.scatter_order(first)
    middle = at.q_n // 2
    cols = sum(right.shape[1] for _, rights in pairs for right in rights)
    if part % 128 == 0:
        halves = jax.ShapeDtypeStruct((middle * part, cols), bf16)
        operands = [value for left, rights in pairs for value in (left, *rights)]
        return pl.pallas_call(
            lambda *refs: halves_kernel(order, [len(rights) for _, rights in pairs], *refs),
            in_specs=[in_vmem] * len(operands),
            out_specs=(in_vmem, in_vmem),
            out_shape=(halves, halves),
            compiler_params=pltpu.CompilerParams(vmem_limit_bytes=kernel_bytes),
            cost_estimate=pl.CostEstimate(
                flops=rows * width * cols, bytes_accessed=1 << 20, transcendentals=0
            ),
            name="grad_halves",
        )(*operands)
    return tuple(
        jnp.concatenate(
            [
                jnp.concatenate(
                    [
                        dot_tn(left[:, k * part : (k + 1) * part], right).astype(bf16)
                        for left, rights in pairs
                        for right in rights
                    ],
                    axis=1,
                )
                for k in side
            ],
            axis=0,
        )
        for side in (order[:middle], order[middle:])
    )


def adjust(weight, first, second, gradient, decay_rate, first_fix, second_fix):
    first_new = 0.9 * first + 0.1 * gradient
    second_new = 0.999 * second + 0.001 * gradient * gradient
    update = (
        first_new / first_fix / (jnp.sqrt(second_new / second_fix) + adam_eps) + decay_rate * weight
    )
    return (first_new, second_new, update)


def in_order(c, mine, other):
    return jnp.where(c == 0, mine, other), jnp.where(c == 0, other, mine)


def adjust_into(
    index, weight, moments_ref, gradient, fixes_ref, state_ref, update_ref, own_ref, sums_ref
):
    own_ref[...] = weight
    first_new, second_new, update = adjust(
        weight, moments_ref[0], moments_ref[1], gradient, weight_decay, fixes_ref[0], fixes_ref[1]
    )
    state_ref[0] = first_new
    state_ref[1] = second_new
    update_ref[...] = update
    sums_ref[2 * index] = jnp.sum(weight * weight)
    sums_ref[2 * index + 1] = jnp.sum(update * update)


def adjust_attn_kernel(
    place_ref, fixes_ref, mine_ref, other_ref, qkv_ref, out_ref, qkv_moments, out_moments,
    qkv_state, out_state, qkv_update, out_update, qkv_own, out_own, sums_ref,
):
    size = qkv_ref.shape[2] // 2
    one, two = in_order(place_ref[1], mine_ref[...], other_ref[...])
    parts = [
        jnp.concatenate([one[:, j * size : (j + 1) * size], two[:, j * size : (j + 1) * size]], 1)
        for j in range(4)
    ]
    adjust_into(
        0, qkv_ref[...], qkv_moments, jnp.stack(parts[:3]), fixes_ref,
        qkv_state, qkv_update, qkv_own, sums_ref,
    )
    adjust_into(
        1, out_ref[...], out_moments, parts[3].T, fixes_ref,
        out_state, out_update, out_own, sums_ref,
    )


def adjust_mlp_kernel(
    place_ref, fixes_ref, mine_ref, other_ref, up_ref, down_ref, up_moments, down_moments,
    up_state, down_state, up_update, down_update, up_own, down_own, sums_ref,
):
    size = up_ref.shape[1] // 2
    one, two = in_order(place_ref[1], mine_ref[...], other_ref[...])
    down_grad = jnp.concatenate([one[:, :size], two[:, :size]], axis=1)
    up_grad = jnp.concatenate([one[:, size:], two[:, size:]], axis=1)
    adjust_into(
        0, up_ref[...], up_moments, up_grad, fixes_ref, up_state, up_update, up_own, sums_ref
    )
    adjust_into(
        1, down_ref[...], down_moments, down_grad.T, fixes_ref,
        down_state, down_update, down_own, sums_ref,
    )


def own_spec(shape, dim, count):
    block = list(shape)
    block[dim] //= count
    return pl.BlockSpec(
        tuple(block), lambda i, p: tuple(p[0] if d == dim else 0 for d in range(len(shape)))
    )


def whole_spec(shape):
    return pl.BlockSpec(shape, lambda i, p: (0,) * len(shape))


def adjust_pair(at, kernel, place, fixes, mine, other, weights, dims, moments):
    parts = [m.shape[1:] for m in moments]
    shapes = [jax.ShapeDtypeStruct(m.shape, f32) for m in moments]
    shapes += [jax.ShapeDtypeStruct(p, f32) for p in parts] * 2
    return pl.pallas_call(
        kernel,
        grid_spec=pltpu.PrefetchScalarGridSpec(
            num_scalar_prefetch=1,
            grid=(1,),
            in_specs=[in_smem, whole_spec(mine.shape), whole_spec(other.shape)]
            + [own_spec(w.shape, d, at.dp_n) for w, d in zip(weights, dims)]
            + [whole_spec(m.shape) for m in moments],
            out_specs=tuple(whole_spec(s.shape) for s in shapes) + (in_smem,),
        ),
        out_shape=tuple(shapes) + (jax.ShapeDtypeStruct((4,), f32),),
        compiler_params=pltpu.CompilerParams(vmem_limit_bytes=back_bytes),
        name="adjust_pair",
    )(place, fixes, mine, other, *weights, *moments)


def adjust_small_kernel(
    fixes_ref, vec_grad, vec_moments, vec, bias_grad, bias_moments, bias, rel_grad, rel_moments,
    rel, vec_state, vec_new, weight_norms, update_norms, bias_state, bias_update, rel_state,
    rel_update, sums_ref,
):
    fixes = (fixes_ref[0], fixes_ref[1])
    first, second, update = adjust(
        vec[...], vec_moments[0], vec_moments[1], vec_grad[...], 0.0, *fixes
    )
    vec_state[0] = first
    vec_state[1] = second
    weight_norm = jnp.sqrt(jnp.sum(vec[...] * vec[...], axis=1, keepdims=True))
    update_norm = jnp.sqrt(jnp.sum(update * update, axis=1, keepdims=True))
    weight_norms[...] = weight_norm
    update_norms[...] = update_norm
    vec_new[...] = vec[...] - learn_rate * (weight_norm / (update_norm + adam_eps)) * update
    first, second, update = adjust(
        bias[...], bias_moments[0:1, :], bias_moments[1:2, :], bias_grad[...], 0.0, *fixes
    )
    bias_state[0:1, :] = first
    bias_state[1:2, :] = second
    bias_update[...] = update
    sums_ref[0] = jnp.sum(bias[...] * bias[...])
    sums_ref[1] = jnp.sum(update * update)
    first, second, update = adjust(
        rel[...], rel_moments[0], rel_moments[1], rel_grad[...], 0.0, *fixes
    )
    rel_state[0] = first
    rel_state[1] = second
    rel_update[...] = update
    sums_ref[2] = jnp.sum(rel[...] * rel[...])
    sums_ref[3] = jnp.sum(update * update)


def adjust_small(fixes, vec, bias, rel):
    shape = jax.ShapeDtypeStruct
    rows = vec[2].shape[0]
    return pl.pallas_call(
        adjust_small_kernel,
        in_specs=[in_smem] + [in_vmem] * 9,
        out_specs=(in_vmem,) * 8 + (in_smem,),
        out_shape=(
            shape(vec[1].shape, f32),
            shape(vec[2].shape, f32),
            shape((rows, 1), f32),
            shape((rows, 1), f32),
            shape(bias[1].shape, f32),
            shape(bias[2].shape, f32),
            shape(rel[1].shape, f32),
            shape(rel[2].shape, f32),
            shape((4,), f32),
        ),
        name="adjust_small",
    )(fixes, *vec, *bias, *rel)


def apply_kernel(rates_ref, *refs):
    count = len(refs) // 3
    for index in range(count):
        refs[2 * count + index][...] = (
            refs[index][...] - rates_ref[index] * refs[count + index][...]
        )


def apply_updates(rates, weights, updates):
    return pl.pallas_call(
        apply_kernel,
        in_specs=[in_smem] + [in_vmem] * (2 * len(updates)),
        out_specs=(in_vmem,) * len(updates),
        out_shape=tuple(jax.ShapeDtypeStruct(u.shape, f32) for u in updates),
        compiler_params=pltpu.CompilerParams(vmem_limit_bytes=kernel_bytes),
        name="apply_updates",
    )(rates, *weights, *updates)


def norm_parts(values):
    center = values - jnp.mean(values, axis=-1, keepdims=True)
    spread = jnp.mean(center * center, axis=-1, keepdims=True)
    inverse = lax.rsqrt(spread + norm_eps)
    return (center * inverse, inverse)


def norm_back(upstream, normed, inverse, gain_vec):
    scaled = upstream * gain_vec
    return inverse * (
        scaled
        - jnp.mean(scaled, axis=-1, keepdims=True)
        - normed * jnp.mean(scaled * normed, axis=-1, keepdims=True)
    )


def local(
    tokens,
    cotangent,
    lengths,
    buckets,
    step_count,
    qkv_weight,
    out_weight,
    up_weight,
    down_weight,
    up_bias,
    rel_bias,
    norm_vectors,
    qkv_moments,
    out_moments,
    up_moments,
    down_moments,
    bias_moments,
    rel_moments,
    vector_moments,
):
    per, length_rows, width = tokens.shape
    at = Places(per)
    seq_len = length_rows * at.mp_n
    blocks = at.slots
    q_n, c, q = at.q_n, at.c, at.q
    head_width = out_weight.shape[0] // 2
    heads = head_width // HD
    units = up_weight.shape[1] // 2
    bucket_count, local_heads = rel_bias.shape

    other_lengths = at.to_core(lengths)
    all_lengths = jnp.where(
        c == 0,
        jnp.concatenate([lengths, other_lengths]),
        jnp.concatenate([other_lengths, lengths]),
    )
    length = lax.dynamic_slice_in_dim(all_lengths, at.s, 1, 0)
    row_keep = jnp.arange(seq_len)[:, None] < length[0]
    row_mask = row_keep.astype(f32)
    vectors = at.relative(norm_vectors, 1)

    def half(values, dim, size):
        return lax.dynamic_slice_in_dim(values, c * size, size, dim)

    part = width // q_n
    small_own = jnp.concatenate(
        [half(up_bias, 0, units), half(rel_bias, 1, heads).T.reshape(-1)]
    )
    qkv_cols = 3 * head_width
    attn_cols = 4 * head_width
    high = lax.reduce_precision(small_own, 8, 7)
    rest = small_own - high
    mid = lax.reduce_precision(rest, 8, 7)
    three = jnp.concatenate([high, mid, rest - mid]).astype(bf16)
    small_rows = -(-three.size // (16 * attn_cols)) * 16
    three = jnp.pad(three, (0, small_rows * attn_cols - three.size)).reshape(small_rows, attn_cols)

    def small_of(rows_low):
        flat = rows_low.reshape(-1).astype(f32)
        count = small_own.size
        return (flat[:count] + flat[count : 2 * count]) + flat[2 * count : 3 * count]

    tokens_near = at.relative(tokens, 2)
    token_pieces = {step: at.collect_piece(tokens_near, step) for step in (0, 2, 3, 1)}
    qkv_own, out_own, attn_piece = pack_attn(
        at, qkv_weight, out_weight, head_width, tokens_near
    )
    attn_piece = jnp.concatenate([attn_piece, three], axis=0)
    attn_one = at.to_slot(attn_piece, 1)
    up_own, down_own, up_piece, down_piece = pack_mlp(
        at, up_weight, down_weight, head_width, units, attn_piece
    )
    mlp_piece = jnp.concatenate([up_piece, down_piece], axis=1)
    attn_one = after(attn_one, token_pieces[1], mlp_piece)
    attn_inner = at.spread_inner(attn_piece, attn_one)
    attn_near = at.gather_start(attn_one[:part])
    tokens_there = (after(token_pieces[2], attn_one), token_pieces[3])
    token_pieces[2] = tokens_there[0]
    mlp_one = at.to_slot(after(mlp_piece, *tokens_there), 1)
    inputs_home = at.collect_end([token_pieces[k] for k in range(blocks)])
    attn_pieces = at.gather_end(
        attn_one[:part], {b: after(v, *tokens_there) for b, v in attn_near.items()}, 0
    )
    inputs_low = at.collect_both(inputs_home)
    inputs_low = after(inputs_low, attn_inner, *attn_pieces)
    attn_outer = at.spread_outer(attn_inner)
    up_one, down_one = mlp_one[:, :units], mlp_one[:, units:]
    up_inner = at.spread_inner(up_piece, up_one)
    mlp_near = at.gather_start(mlp_one)
    turn = 1 % len(at.q_bits)
    attn_pair = at.spread_pair(attn_inner, attn_outer)
    pair_first = after(attn_pair[:part], *mlp_near.values(), up_inner)
    small = [
        small_own,
        small_of(attn_one[part:]),
        small_of(attn_pair[part:, :attn_cols]),
        small_of(attn_pair[part:, attn_cols:]),
    ]
    tile = tile_of(seq_len)
    tiles = seq_len // tile
    padded = jnp.concatenate([jnp.zeros((tile,), jnp.int32), buckets])
    spread = jnp.concatenate(
        [padded[kk * tile : (kk + 2) * tile] for kk in range(tiles)]
    )
    choose = (jnp.arange(bucket_count, dtype=jnp.int32)[:, None] == spread[None, :]).astype(f32)

    def lines_of(r):
        rel_rows = small[r][units:].reshape(heads, bucket_count)
        return jnp.dot(rel_rows, choose, precision=lax.Precision.HIGHEST)


    columns = range(q_n)
    qkv_one, out_one = join(
        attn_pieces,
        part,
        [
            [[(k, 0, qkv_cols)] for k in columns],
            [[(k, qkv_cols, head_width)] for k in columns],
        ],
    )
    qkv_w, out_w = [qkv_own, qkv_one], [out_own, out_one]

    first_parts = norm_parts(inputs_low.astype(f32))
    first_normed, first_inverse = first_parts
    first_low = (first_normed * vectors[0] + vectors[1]).astype(bf16)
    qkv, contexts, totals = [], [], []

    def attention(r, *others):
        qkv.append(after(dot_nn(first_low, qkv_w[r]).astype(bf16), *others))
        context, total = attend(length, qkv[r], lines_of(r), heads)
        contexts.append(context)
        totals.append(total)

    attention(0, mlp_one)
    pair_first = after(pair_first, contexts[0])
    pair_near = at.gather_start(pair_first)
    up_outer = at.spread_outer(after(up_inner, *mlp_near.values()))
    down_inner = at.spread_inner(after(down_piece, up_inner, *mlp_near.values()), down_one)
    attention(1, attn_outer)
    near_done = (*pair_near.values(), up_outer, down_inner)
    pair_near = {b: after(v, *near_done, contexts[1]) for b, v in pair_near.items()}
    pair_pieces = []
    for k in range(2):
        cols = slice(k * attn_cols, (k + 1) * attn_cols)
        pair_pieces.append(
            at.gather_end(
                pair_first[:, cols], {b: v[:, cols] for b, v in pair_near.items()}, k * turn
            )
        )
    down_outer = at.spread_outer(after(down_inner, *near_done))
    incoming_near = at.relative(after(cotangent, *near_done), 2)
    incoming_pieces = {step: at.collect_piece(incoming_near, step) for step in (2, 3)}
    pair_done = [v for pieces in pair_pieces for v in pieces[1:]]
    mlp_near = {b: after(v, *pair_done) for b, v in mlp_near.items()}
    up_one_pieces = at.gather_end(up_one, {b: v[:, :units] for b, v in mlp_near.items()}, 0)
    down_one_pieces = at.gather_end(
        down_one, {b: v[:, units:] for b, v in mlp_near.items()}, turn
    )
    one_done = (*up_one_pieces, *down_one_pieces, down_outer)
    up_pair = after(at.spread_pair(up_inner, up_outer), *one_done)
    up_near = at.gather_start(up_pair)
    incoming_near = after(incoming_near, *one_done)
    incoming_pieces.update({step: at.collect_piece(incoming_near, step) for step in (0, 1)})
    down_pair = after(at.spread_pair(down_inner, down_outer), *up_near.values())

    def pair_halves(piece, near):
        halves = []
        for k in range(2):
            cols = slice(k * units, (k + 1) * units)
            halves.append(
                at.gather_end(piece[:, cols], {b: v[:, cols] for b, v in near.items()}, k * turn)
            )
        return halves

    def pair_join(halves):
        return join(
            halves[0] + halves[1], part, [[[(k, 0, units), (k + q_n, 0, units)] for k in columns]]
        )[0]

    up_halves = pair_halves(up_pair, up_near)
    down_near = at.gather_start(down_pair)
    down_near = {b: after(v, up_halves[0][-1], up_halves[1][-1]) for b, v in down_near.items()}
    down_halves = pair_halves(down_pair, down_near)
    joined = join(
        pair_pieces[0] + pair_pieces[1],
        part,
        [
            [[(k + half_at, start, size)] for k in columns]
            for half_at in (0, q_n)
            for start, size in ((0, qkv_cols), (qkv_cols, head_width))
        ],
    )
    qkv_w += joined[0::2]
    out_w += joined[1::2]
    attention(2, *one_done)
    attention(3, *up_near.values())
    incoming_home = at.collect_end([incoming_pieces[k] for k in range(blocks)])
    rows_of = [[(k, 0, units)] for k in columns]
    up_w = [up_own, join(up_one_pieces, part, [rows_of])[0], pair_join(up_halves)]
    down_w = [down_own, join(down_one_pieces, part, [rows_of])[0], pair_join(down_halves)]

    inputs = inputs_low.astype(f32)
    mixed = at.sum_team(sum_nt(contexts, out_w))
    mixed = after(mixed, *up_near.values())
    middle = inputs + (mixed + vectors[4]) * row_mask
    second_normed, second_inverse = norm_parts(middle)
    second_low = (second_normed * vectors[2] + vectors[3]).astype(bf16)
    acts, slopes = [], []
    biases = [small[0][:units], small[1][:units], jnp.concatenate([small[2][:units], small[3][:units]])]
    for r in range(3):
        act, slope = up_project(second_low, up_w[r], biases[r])
        acts.append(act)
        slopes.append(slope)
    incoming_low = at.collect_both(incoming_home)
    kept = jnp.where(row_keep, incoming_low, jnp.zeros_like(incoming_low))
    fed_bias_grad = jnp.sum(kept.astype(f32), axis=0)
    bias_grads = [None] * blocks

    pre_pair, bias_pair = down_back(kept, down_w[2], slopes[2])
    bias_grads[2], bias_grads[3] = bias_pair[:units], bias_pair[units:]
    up_far_halves = grad_halves(at, [(second_low, [pre_pair])], 1)
    up_far = ChipSum(at, up_far_halves, 1)
    down_far_halves = grad_halves(at, [(after(kept, *up_far_halves), [acts[2]])], 0)
    down_far = ChipSum(at, down_far_halves, 0)
    down_near_halves = grad_halves(at, [(after(kept, *down_far_halves), acts[:2])], 0)
    fed_low = sum_nt([after(acts[0], *down_far_halves)] + acts[1:], down_w)
    fed_share = at.sum_share(fed_low, length_rows)
    middle_share = at.share(middle, length_rows, 0, 0)
    mask_share = at.share(row_mask, length_rows, 0, 0)
    out_share = (middle_share + (fed_share + vectors[5]) * mask_share).astype(bf16)
    out_got = at.deliver_first(out_share)
    kept_late = after(kept, fed_low, *down_far_halves)
    pre_own, bias_grads[0] = down_back(kept_late, down_w[0], slopes[0])
    pre_one, bias_grads[1] = down_back(kept_late, down_w[1], slopes[1])
    back_low = sum_nt([pre_own, pre_one, pre_pair], up_w)
    up_near_halves = grad_halves(at, [(after(second_low, back_low), [pre_own, pre_one])], 1)
    second_grad = at.sum_team(back_low)
    second_grad = after(second_grad, *up_near_halves)
    lead = jnp.where((c == 0) & (at.t == 0), 1.0, 0.0)
    gain_two = jnp.sum(second_grad * second_normed, axis=0)
    shift_two = jnp.sum(second_grad, axis=0)
    middle_grad = incoming_low.astype(f32) + norm_back(
        second_grad, second_normed, second_inverse, vectors[2]
    )
    branch = jnp.where(row_keep, middle_grad, 0.0).astype(bf16)
    mix_bias_grad = jnp.sum(branch.astype(f32), axis=0)
    rel_grads = [None] * blocks
    branch = after(branch, up_far.got, down_far.got)
    context_grads = [dot_nn(branch, out_w[r]).astype(bf16) for r in range(blocks)]
    own_cols = slice(0, units)
    far_cols = slice(units, 2 * units)
    attn_sums = [None] * blocks
    attn_halves = [None] * blocks
    proj_grads = [None] * blocks
    for r in reversed(range(blocks)):
        context_grad = context_grads[r]
        if r == 3:
            there = (up_far.got, down_far.got)
            up_far.rest(*there)
            down_far.rest(*there)
        if r == 2:
            far_done = (up_far.got, down_far.got)
            context_grad = after(context_grad, *far_done)
            down_near_sum = ChipSum(at, [after(v, *far_done) for v in down_near_halves], 0)
            up_near_sum = ChipSum(at, [after(v, *far_done) for v in up_near_halves], 1)
            far_sums = (down_far.total(), up_far.total())
            mlp_far = jnp.concatenate(
                [v[:, cols] for cols in (own_cols, far_cols) for v in far_sums], axis=1
            ).astype(bf16)
            far_got = at.fold_outer(mlp_far)
        if r == 1:
            context_grad = after(context_grad, out_got)
        if r == 0:
            near_firsts = (down_near_sum.got, up_near_sum.got)
            context_grad = after(context_grad, *near_firsts, far_got)
            mlp_far = at.fold_add(mlp_far, after(far_got, *near_firsts))
            down_near_sum.rest(*near_firsts)
            up_near_sum.rest(*near_firsts)
            near_done = (down_near_sum.got, up_near_sum.got)
        proj_grad, dist = attend_back(
            length, qkv[r], lines_of(r), totals[r], context_grad, heads
        )
        rel_grads[r] = dist
        if r == 0:
            proj_grad = after(proj_grad, *near_done)
        attn_halves[r] = grad_halves(
            at, [(first_low, [proj_grad]), (branch, [contexts[r]])], r % 2
        )
        proj_grads[r] = proj_grad
    back_low = sum_nt(proj_grads, qkv_w)
    inner_got = at.fold_inner(after(mlp_far, back_low))
    out_pair = at.deliver_pair(out_share, after(out_got, far_got, back_low))
    out_last = at.deliver_last(out_pair)
    for k in (3, 2):
        attn_sums[k] = ChipSum(at, [after(v, *near_done) for v in attn_halves[k]], k % 2)
    firsts = (attn_sums[3].got, attn_sums[2].got)
    first_grad = at.sum_share(back_low, length_rows)
    for k in (3, 2):
        attn_sums[k].rest(*firsts)
    attn_far = jnp.concatenate([attn_sums[2].total(), attn_sums[3].total()], axis=1).astype(bf16)
    mlp_size = 2 * units
    mlp_near = (down_near_sum.total(), up_near_sum.total())
    mlp_one = jnp.concatenate([v[:, far_cols] for v in mlp_near], axis=1)
    mlp_own = jnp.concatenate([v[:, own_cols] for v in mlp_near], axis=1)
    mlp_one = (mlp_one + inner_got[:, :mlp_size].astype(f32)).astype(bf16)
    rel_grad = lax.dot_general(
        jnp.concatenate(rel_grads, axis=0),
        choose,
        (((1,), (1,)), ((), ())),
        precision=lax.Precision.HIGHEST,
    )
    normed_share = at.share(first_normed, length_rows, 0, 0)
    inverse_share = at.share(first_inverse, length_rows, 0, 0)
    middle_grad_share = at.share(middle_grad, length_rows, 0, 0)
    gain_one = jnp.sum(first_grad * normed_share, axis=0)
    shift_one = jnp.sum(first_grad, axis=0)
    input_share = middle_grad_share + norm_back(
        first_grad, normed_share, inverse_share, vectors[0]
    )
    input_low = input_share.astype(bf16)
    def by_place(rows_of):
        around = jnp.stack(rows_of)
        moved = []
        for place in range(blocks):
            picked = around[0]
            for k in range(1, blocks):
                picked = jnp.where(at.s ^ k == place, around[k], picked)
            moved.append(picked)
        moved = jnp.stack(moved)[:, None, None, :]
        here = (jnp.arange(at.t_n)[:, None] == at.t) & (jnp.arange(2)[None, :] == c)
        return jnp.where(here[None, :, :, None], moved, 0.0).reshape(at.mp_n, 2, -1)

    vector_grad = jnp.concatenate(
        [
            jnp.stack([gain_one, shift_one]),
            lead * jnp.stack([gain_two, shift_two, mix_bias_grad, fed_bias_grad]),
        ]
    )
    small_grad = by_place(
        [
            jnp.concatenate([bias_grads[r], rel_grad[r * heads : (r + 1) * heads].reshape(-1)])
            for r in range(blocks)
        ]
    )
    last_got = at.to_slot(mlp_one, 1)
    plane = at.sum_plane(
        jnp.concatenate([at.relative(vector_grad, 1).reshape(-1), small_grad.reshape(-1)])
    )
    there = (attn_sums[3].got, attn_sums[2].got, plane)
    for k in (1, 0):
        attn_sums[k] = ChipSum(at, [after(v, *there) for v in attn_halves[k]], k % 2)
    there = (attn_sums[1].got, attn_sums[0].got)
    for k in (1, 0):
        attn_sums[k].rest(*there)
    joined = at.sum_column(after(plane, last_got))
    input_got = at.deliver_first(after(input_low, joined))
    attn_got = at.fold_outer(after(attn_far, joined))
    mlp_mine = mlp_own + inner_got[:, mlp_size:].astype(f32) + last_got.astype(f32)
    attn_got = after(attn_got, attn_sums[0].got, attn_sums[1].got, input_got)
    attn_inner_got = at.fold_inner(at.fold_add(attn_far, attn_got))
    attn_one_sum = attn_inner_got[:, :attn_cols].astype(f32) + attn_sums[1].total()
    attn_last_got = at.to_slot(attn_one_sum.astype(bf16), 1)
    attn_mine = (
        attn_sums[0].total()
        + attn_inner_got[:, attn_cols:].astype(f32)
        + attn_last_got.astype(f32)
    )
    input_pair = at.deliver_pair(input_low, input_got)
    input_last = at.deliver_last(input_pair)
    input_grad = at.relative(at.delivered(input_pair, input_last), 2).astype(f32)
    vector_grad = joined[: vector_grad.size].reshape(vector_grad.shape)
    small_sum = lax.dynamic_index_in_dim(
        joined[vector_grad.size :].reshape(small_grad.shape), at.mp_i, 0, keepdims=False
    )
    bias_sum = small_sum[:, :units].reshape(1, -1)
    rel_sum = small_sum[:, units:].reshape(2 * heads, bucket_count).T

    rows = part // 2

    def exchanged(mine):
        sent = lax.dynamic_slice_in_dim(mine, (1 - c) * rows, rows, 0)
        return lax.dynamic_slice_in_dim(mine, c * rows, rows, 0), at.to_core(sent)

    mlp_mine, mlp_other = exchanged(mlp_mine)
    attn_mine, attn_other = exchanged(attn_mine)

    steps_done = step_count[0].astype(f32)
    first_fix = 1.0 - jnp.power(jnp.float32(0.9), steps_done)
    second_fix = 1.0 - jnp.power(jnp.float32(0.999), steps_done)
    fixes = jnp.stack([first_fix, second_fix])
    qkv_view = jnp.transpose(qkv_weight, (1, 0, 2))
    qkv_mom = jnp.transpose(qkv_moments, (0, 2, 1, 3))
    weights = [qkv_view, out_weight, up_weight, down_weight]
    dims = [1, 1, 0, 1]
    in_kernels = rows % 128 == 0
    if in_kernels:
        place = jnp.stack([at.dp_i, c]).astype(jnp.int32)
        up_state, down_state, up_update, down_update, up_mine, down_mine, mlp_squares = adjust_pair(
            at, adjust_mlp_kernel, place, after(fixes, attn_inner_got), mlp_mine, mlp_other,
            weights[2:], dims[2:], [up_moments, down_moments],
        )
        qkv_state, out_state, qkv_update, out_update, qkv_mine, out_mine, attn_squares = adjust_pair(
            at, adjust_attn_kernel, place, fixes, attn_mine, attn_other,
            weights[:2], dims[:2], [qkv_mom, out_moments],
        )
        squares = jnp.concatenate([attn_squares, mlp_squares])
        updates = [qkv_update, out_update, up_update, down_update]
        states = [qkv_state, out_state, up_state, down_state]
        own_weights = [qkv_mine, out_mine, up_mine, down_mine]
    else:
        one, two = in_order(c, attn_mine, attn_other)
        parts = [
            jnp.concatenate(
                [v[:, j * head_width : (j + 1) * head_width] for v in (one, two)], axis=1
            )
            for j in range(4)
        ]
        one, two = in_order(c, mlp_mine, mlp_other)
        grads = [
            jnp.stack(parts[:3]),
            parts[3].T,
            jnp.concatenate([one[:, units:], two[:, units:]], axis=1),
            jnp.concatenate([one[:, :units], two[:, :units]], axis=1).T,
        ]
        own_weights, updates, states, squares = [], [], [], []
        for weight, dim, moments, grad in zip(
            weights, dims, [qkv_mom, out_moments, up_moments, down_moments], grads
        ):
            count = weight.shape[dim] // at.dp_n
            weight = lax.dynamic_slice_in_dim(weight, at.dp_i * count, count, dim)
            first_new, second_new, update = adjust(
                weight, moments[0], moments[1], grad, weight_decay, first_fix, second_fix
            )
            own_weights.append(weight)
            updates.append(update)
            states.append(jnp.stack([first_new, second_new]))
            squares += [jnp.sum(weight * weight), jnp.sum(update * update)]
        squares = jnp.stack(squares)
    (
        vector_state, vector_new, vector_norms, vector_update_norms,
        bias_state, bias_update, rel_state, rel_update, small_squares,
    ) = adjust_small(
        fixes,
        (vector_grad, vector_moments, norm_vectors),
        (bias_sum, bias_moments, up_bias[None, :]),
        (rel_sum, rel_moments, rel_bias),
    )
    lead_dp = (at.dp_i == 0).astype(f32)
    squares = jnp.concatenate([squares, lead_dp * small_squares])
    squares = after(at.sum_plane(squares), input_last)
    squares = at.sum_column(squares).reshape(6, 2)
    norms = jnp.sqrt(squares)
    rates = learn_rate * (norms[:, 0] / (norms[:, 1] + adam_eps))
    small_weights = [up_bias[None, :], rel_bias]
    small_updates = [bias_update, rel_update]
    if in_kernels:
        *new, bias_new, rel_new = apply_updates(
            rates, own_weights + small_weights, updates + small_updates
        )
    else:
        new = [own_weights[k] - rates[k] * updates[k] for k in range(4)]
        bias_new, rel_new = apply_updates(rates[4:], small_weights, small_updates)
    new, states = list(new), list(states)
    new[0] = jnp.transpose(new[0], (1, 0, 2))
    states[0] = jnp.transpose(states[0], (0, 2, 1, 3))
    block_out = at.relative(at.delivered(out_pair, out_last), 2)
    results = [block_out, input_grad]
    for k in range(4):
        results += [new[k], states[k]]
    results += [bias_new[0], bias_state, rel_new, rel_state, vector_new, vector_state]
    results.append(
        jnp.concatenate(
            [norms, jnp.concatenate([vector_norms, vector_update_norms], axis=1)]
        ).T
    )
    return tuple(results)


def solution(mesh):
    return jax.shard_map(
        local,
        mesh=mesh,
        in_specs=(
            P("dp", "mp", None),
            P("dp", "mp", None),
            P("dp"),
            P(),
            P(),
            P(None, None, "mp"),
            P("mp", None),
            P(None, "mp"),
            P("mp", None),
            P("mp"),
            P(None, "mp"),
            P(),
            P(None, "dp", None, "mp"),
            P(None, "mp", "dp"),
            P(None, "dp", "mp"),
            P(None, "mp", "dp"),
            P(None, "mp"),
            P(None, None, "mp"),
            P(),
        ),
        out_specs=(
            P("dp", "mp", None),
            P("dp", "mp", None),
            P("dp", None, "mp"),
            P(None, "dp", None, "mp"),
            P("mp", "dp"),
            P(None, "mp", "dp"),
            P("dp", "mp"),
            P(None, "dp", "mp"),
            P("mp", "dp"),
            P(None, "mp", "dp"),
            P("mp"),
            P(None, "mp"),
            P(None, "mp"),
            P(None, None, "mp"),
            P(),
            P(),
            P(),
        ),
        check_vma=False,
    )
```

```python
import jax
import jax.numpy as jnp
from jax import lax
from jax.experimental import pallas as pl
from jax.experimental.pallas import tpu as pltpu
from jax.sharding import PartitionSpec as P

HD = 64
f32 = jnp.float32
bf16 = jnp.bfloat16

norm_eps = 1e-05
adam_eps = 1e-06
learn_rate = 0.25
weight_decay = 0.1
masked_score = -1000000000.0
score_scale = HD ** (-0.5)
kernel_bytes = 12 << 20
back_bytes = 16 << 20

in_vmem = pl.BlockSpec(memory_space=pltpu.VMEM)
in_smem = pl.BlockSpec(memory_space=pltpu.SMEM)


def dot_nt(left, right):
    return lax.dot_general(left, right, (((1,), (1,)), ((), ())), preferred_element_type=f32)


def dot_nn(left, right):
    return lax.dot_general(left, right, (((1,), (0,)), ((), ())), preferred_element_type=f32)


def dot_tn(left, right):
    return lax.dot_general(left, right, (((0,), (0,)), ((), ())), preferred_element_type=f32)


def tile_of(rows):
    return min(256, rows)


def bias_tiles(line_ref, head, tiles, tile):
    causal = lax.broadcasted_iota(jnp.int32, (tile, tile), 0) <= lax.broadcasted_iota(
        jnp.int32, (tile, tile), 1
    )
    made = []
    for kk in range(tiles):
        line = line_ref[head : head + 1, kk * 2 * tile : (kk + 1) * 2 * tile]
        wide = jnp.broadcast_to(line, (tile, 2 * tile))
        made.append(pltpu.roll(wide, tile, 1, stride=1, stride_axis=0)[:, :tile])
    made[0] = jnp.where(causal, made[0], masked_score)
    return made


def scores_of(keys, query, toeplitz, block, tile, key_pos, length):
    count = (block + 1) * tile
    raw = dot_nt(keys[:count], query)
    raw = raw + jnp.concatenate([toeplitz[block - j] for j in range(block + 1)], axis=0)
    return jnp.where(key_pos[:count] < length, raw, masked_score)


def attend_kernel(heads, length_ref, qkv_ref, line_ref, ctx_ref, lse_ref):
    rows = qkv_ref.shape[0]
    tile = tile_of(rows)
    tiles = rows // tile
    width = heads * HD
    length = length_ref[0]
    key_pos = lax.broadcasted_iota(jnp.int32, (rows, tile), 0)
    for head in range(heads):
        toeplitz = bias_tiles(line_ref, head, tiles, tile)
        cols = slice(head * HD, (head + 1) * HD)
        keys = qkv_ref[:, width + head * HD : width + (head + 1) * HD]
        vals = qkv_ref[:, 2 * width + head * HD : 2 * width + (head + 1) * HD]
        for block in range(tiles):
            here = slice(block * tile, (block + 1) * tile)
            count = (block + 1) * tile
            query = qkv_ref[here, cols] * jnp.asarray(score_scale, bf16)
            raw = scores_of(keys, query, toeplitz, block, tile, key_pos, length)
            top = jnp.max(raw, axis=0, keepdims=True)
            grown = jnp.exp(raw - top)
            total = jnp.sum(grown, axis=0, keepdims=True)
            probs = (grown * (1.0 / total)).astype(bf16)
            ctx_ref[here, cols] = dot_tn(probs, vals[:count]).astype(bf16)
            lse_ref[head : head + 1, here] = top + jnp.log(total)


def attend_back_kernel(
    heads,
    length_ref,
    qkv_ref,
    line_ref,
    lse_ref,
    grad_ref,
    out_ref,
    dist_ref,
    key_acc,
    val_acc,
    diag_acc,
):
    rows = qkv_ref.shape[0]
    tile = tile_of(rows)
    tiles = rows // tile
    width = heads * HD
    length = length_ref[0]
    key_pos = lax.broadcasted_iota(jnp.int32, (rows, tile), 0)
    for head in range(heads):
        toeplitz = bias_tiles(line_ref, head, tiles, tile)
        cols = slice(head * HD, (head + 1) * HD)
        key_cols = slice(width + head * HD, width + (head + 1) * HD)
        val_cols = slice(2 * width + head * HD, 2 * width + (head + 1) * HD)
        keys = qkv_ref[:, key_cols]
        vals = qkv_ref[:, val_cols]
        key_acc[...] = jnp.zeros_like(key_acc)
        val_acc[...] = jnp.zeros_like(val_acc)
        diag_acc[...] = jnp.zeros_like(diag_acc)
        for block in range(tiles):
            here = slice(block * tile, (block + 1) * tile)
            count = (block + 1) * tile
            query = qkv_ref[here, cols] * jnp.asarray(score_scale, bf16)
            grad = grad_ref[here, cols]
            raw = scores_of(keys, query, toeplitz, block, tile, key_pos, length)
            probs = jnp.exp(raw - lse_ref[head : head + 1, here])
            pgrad = dot_nt(vals[:count], grad)
            drop = jnp.sum(probs * pgrad, axis=0, keepdims=True)
            sgrad = (probs * (pgrad - drop)).astype(bf16)
            val_acc[:count] += dot_nn(probs.astype(bf16), grad)
            key_acc[:count] += dot_nn(sgrad, query)
            out_ref[here, cols] = (dot_tn(sgrad, keys[:count]) * score_scale).astype(bf16)
            wide = sgrad.astype(f32)
            for j in range(block + 1):
                diag_acc[block - j] += wide[j * tile : (j + 1) * tile]
        out_ref[:, key_cols] = key_acc[...].astype(bf16)
        out_ref[:, val_cols] = val_acc[...].astype(bf16)
        for kk in range(tiles):
            held = jnp.concatenate([diag_acc[kk], jnp.zeros((tile, tile), f32)], axis=1)
            half = tile // 2
            while half >= 1:
                held = held[:half] + pltpu.roll(held[half : 2 * half], 2 * tile - half, 1)
                half //= 2
            dist_ref[head : head + 1, kk * 2 * tile : (kk + 1) * 2 * tile] = pltpu.roll(held, tile, 1)


def attend(length, qkv, line, heads):
    rows = qkv.shape[0]
    return pl.pallas_call(
        lambda *refs: attend_kernel(heads, *refs),
        out_shape=(
            jax.ShapeDtypeStruct((rows, heads * HD), bf16),
            jax.ShapeDtypeStruct((heads, rows), f32),
        ),
        in_specs=[in_smem, in_vmem, in_vmem],
        out_specs=(in_vmem, in_vmem),
        compiler_params=pltpu.CompilerParams(vmem_limit_bytes=kernel_bytes),
        cost_estimate=pl.CostEstimate(
            flops=heads * rows * rows * HD * 10,
            bytes_accessed=1 << 20,
            transcendentals=0,
        ),
        name="attend",
    )(length, qkv, line)


def attend_back(length, qkv, line, lse, grad, heads):
    rows = qkv.shape[0]
    tile = tile_of(rows)
    return pl.pallas_call(
        lambda *refs: attend_back_kernel(heads, *refs),
        out_shape=(
            jax.ShapeDtypeStruct((rows, 3 * heads * HD), bf16),
            jax.ShapeDtypeStruct((heads, 2 * rows), f32),
        ),
        in_specs=[in_smem, in_vmem, in_vmem, in_vmem, in_vmem],
        out_specs=(in_vmem, in_vmem),
        scratch_shapes=[
            pltpu.VMEM((rows, HD), f32),
            pltpu.VMEM((rows, HD), f32),
            pltpu.VMEM((rows // tile, tile, tile), f32),
        ],
        compiler_params=pltpu.CompilerParams(vmem_limit_bytes=back_bytes),
        cost_estimate=pl.CostEstimate(
            flops=heads * rows * rows * HD * 20,
            bytes_accessed=1 << 20,
            transcendentals=0,
        ),
        name="attend_back",
    )(length, qkv, line, lse, grad)


def tie(*values):
    return lax.optimization_barrier(values)


def after(values, *others):
    return lax.optimization_barrier((values, *others))[0]


class Places:
    def __init__(self, per):
        self.per = per
        self.dp_n = lax.axis_size("dp")
        self.mp_n = lax.axis_size("mp")
        self.q_n = self.dp_n // 2
        self.slots = 2 * per
        self.t_n = self.mp_n // self.slots
        assert self.dp_n % 2 == 0 and self.mp_n % self.slots == 0
        dp_i = lax.axis_index("dp")
        mp_i = lax.axis_index("mp")
        self.dp_i, self.mp_i = dp_i, mp_i
        self.q, self.c = dp_i // 2, lax.rem(dp_i, 2)
        self.s, self.t = mp_i // self.t_n, lax.rem(mp_i, self.t_n)
        assert per == 2
        self.home = self.s // per
        self.at_home = self.c == self.home
        self.q_bits = []
        while (1 << len(self.q_bits)) < self.q_n:
            self.q_bits.append(1 << len(self.q_bits))
        assert (1 << len(self.q_bits)) == self.q_n

    def move(self, values, target):
        pairs = []
        for q in range(self.q_n):
            for c in range(2):
                for s in range(self.slots):
                    for t in range(self.t_n):
                        found = target(q, c, s, t)
                        if found is not None:
                            nq, nc, ns, nt = found
                            pairs.append(
                                (
                                    (q * 2 + c) * self.mp_n + s * self.t_n + t,
                                    (nq * 2 + nc) * self.mp_n + ns * self.t_n + nt,
                                )
                            )
        return lax.ppermute(values, ("dp", "mp"), pairs)

    def to_core(self, values):
        return self.move(values, lambda q, c, s, t: (q, 1 - c, s, t))

    def to_slot(self, values, step):
        return self.move(values, lambda q, c, s, t: (q, c, s ^ step, t))

    def to_chip(self, values, bit):
        return self.move(values, lambda q, c, s, t: (q ^ bit, c, s, t))

    def to_team(self, values, step):
        return self.move(values, lambda q, c, s, t: (q, c, s, (t + step) % self.t_n))

    def relative(self, values, dim):
        size = values.shape[dim] // self.q_n
        return jnp.concatenate(
            [
                lax.dynamic_slice_in_dim(values, (self.q ^ k) * size, size, dim)
                for k in range(self.q_n)
            ],
            axis=dim,
        )

    def block_at(self, step):
        return lax.rem(self.s + step, self.slots) * self.t_n + self.t

    def collect_piece(self, local, step):
        piece = lax.dynamic_index_in_dim(local, (self.s ^ step) % 2, 0, keepdims=False)
        if step == 0:
            return piece
        return self.move(
            piece,
            lambda q, c, s, t: (
                (q, c, s ^ step, t) if (s ^ step) // self.per == c else None
            ),
        )

    def collect_end(self, pieces):
        count, width = pieces[0].shape
        whole = jnp.zeros((count * self.mp_n, width), pieces[0].dtype)
        for step, piece in enumerate(pieces):
            for turn in range(self.t_n):
                piece_t = self.to_team(piece, turn) if turn > 0 else piece
                from_t = lax.rem(self.t + self.t_n - turn, self.t_n)
                whole = lax.dynamic_update_slice_in_dim(
                    whole, piece_t, ((self.s ^ step) * self.t_n + from_t) * count, 0
                )
        return whole

    def collect_both(self, whole):
        other = self.move(
            whole, lambda q, c, s, t: (q, 1 - c, s, t) if c == s // self.per else None
        )
        return jnp.where(self.at_home, whole, other)

    def deliver_first(self, blocks):
        return self.move(
            blocks, lambda q, c, s, t: (q, 1 - c, s ^ 2, t) if c != s // 2 else None
        )

    def deliver_pair(self, blocks, got):
        return jnp.where(self.at_home, blocks, got)

    def deliver_last(self, pair):
        return self.to_slot(pair[pair.shape[0] // 2 :], 1)

    def delivered(self, pair, got):
        mine = pair[: pair.shape[0] // 2]
        even = self.s % 2 == 0
        return jnp.stack([jnp.where(even, mine, got), jnp.where(even, got, mine)])

    def share(self, values, length, flip, team):
        side = jnp.where(self.at_home, 0, 1) ^ flip
        parts = []
        for index in range(self.per):
            slot = self.s ^ (self.per * side + index)
            block = slot * self.t_n + lax.rem(self.t + team, self.t_n)
            parts.append(lax.dynamic_slice_in_dim(values, block * length, length, 0))
        return jnp.concatenate(parts, axis=0)

    def sum_share(self, partial, length):
        total = self.share(partial, length, 0, 0).astype(f32)
        for team in range(self.t_n):
            for flip in (0, 1):
                if (team, flip) != (0, 0):
                    sent = self.share(partial, length, flip, team).astype(bf16)
                    total = total + self.move(
                        sent, lambda q, c, s, t: (q, c ^ flip, s, (t + team) % self.t_n)
                    ).astype(f32)
        return total

    def sum_team(self, partial):
        total = partial.astype(f32)
        total = total + self.to_core(partial).astype(f32)
        if self.t_n > 1:
            low = total.astype(bf16)
            for team in range(1, self.t_n):
                total = total + self.to_team(low, team).astype(f32)
        return total

    def spread_inner(self, own, one):
        both = jnp.concatenate([own, one], axis=1)
        return self.move(both, lambda q, c, s, t: (q, c, s ^ 3, t) if s in (1, 2) else None)

    def spread_outer(self, inner):
        return self.move(inner, lambda q, c, s, t: (q, c, s ^ 1, t) if s in (1, 2) else None)

    def spread_pair(self, inner, outer):
        size = inner.shape[1] // 2
        turned = jnp.concatenate([inner[:, size:], inner[:, :size]], axis=1)
        return jnp.where((self.s == 1) | (self.s == 2), turned, outer)

    def fold_outer(self, far):
        return self.move(far, lambda q, c, s, t: (q, c, s ^ 1, t) if s in (0, 3) else None)

    def fold_add(self, far, got):
        size = far.shape[1] // 2
        turned = jnp.concatenate([got[:, size:], got[:, :size]], axis=1)
        return (far.astype(f32) + turned.astype(f32)).astype(bf16)

    def fold_inner(self, far):
        return self.move(far, lambda q, c, s, t: (q, c, s ^ 3, t) if s in (1, 2) else None)

    def bits_from(self, first):
        return self.q_bits[first:] + self.q_bits[:first]

    def gather_chips(self, piece, first):
        pieces = {0: piece}
        for bit in self.bits_from(first):
            for k in list(pieces):
                pieces[k | bit] = self.to_chip(pieces[k], bit)
        return [pieces[k] for k in range(self.q_n)]

    def gather_start(self, piece):
        return {bit: self.to_chip(piece, bit) for bit in self.q_bits}

    def gather_end(self, piece, near, first):
        pieces = {0: piece}
        for bit in self.bits_from(first):
            for k in list(pieces):
                pieces[k | bit] = near[bit] if k == 0 else self.to_chip(pieces[k], bit)
        return [pieces[k] for k in range(self.q_n)]

    def scatter_order(self, first):
        order = [0]
        for bit in reversed(self.bits_from(first)):
            order = order + [k | bit for k in order]
        return order

    def sum_plane(self, values):
        values = values + self.to_core(values)
        for low in range(0, len(self.q_bits), 2):
            bits = self.q_bits[low : low + 2]
            got = [self.to_chip(values, bit) for bit in bits]
            if len(bits) == 2:
                both = self.to_chip(values, bits[0] | bits[1])
                values = (values + got[0]) + (got[1] + both)
            else:
                values = values + got[0]
        return values

    def sum_column(self, values):
        bit, bits = 1, []
        while bit < self.mp_n:
            bits.append(bit)
            bit *= 2

        def flip(mask):
            def target(q, c, s, t):
                place = (s * self.t_n + t) ^ mask
                return (q, c, place // self.t_n, place % self.t_n)

            return self.move(values, target)

        for low in range(0, len(bits), 2):
            pair = bits[low : low + 2]
            if len(pair) == 2:
                one, two, both = flip(pair[0]), flip(pair[1]), flip(pair[0] | pair[1])
                values = (values + one) + (two + both)
            else:
                values = values + flip(pair[0])
        return values


class ChipSum:
    def __init__(self, at, halves, first):
        self.at = at
        self.bits = list(at.bits_from(first))
        self.parts, sent = [halves[0]], halves[1]
        self.exchange(sent)

    def exchange(self, sent):
        self.got = self.at.to_chip(sent, self.bits.pop(0))
        self.parts.append(self.got)

    def total(self, rows=None):
        total = self.parts[0][rows].astype(f32) if rows else self.parts[0].astype(f32)
        for part in self.parts[1:]:
            total = total + (part[rows] if rows else part).astype(f32)
        return total

    def step(self, *others):
        if not self.bits:
            return
        self.parts[-1] = after(self.parts[-1], *others)
        half = self.got.shape[0] // 2
        sent = self.total(slice(half, None)).astype(bf16)
        self.parts = [part[:half] for part in self.parts]
        self.exchange(sent)

    def rest(self, *others):
        while self.bits:
            self.step(*others)


def pack_attn_kernel(place_ref, qkv_ref, out_ref, qkv_full, out_full, piece_ref):
    size = qkv_ref.shape[2]
    for j in range(3):
        qkv_full[:, j * size : (j + 1) * size] = qkv_ref[j].astype(bf16)
    out_full[...] = out_ref[...].T.astype(bf16)

    @pl.when(pl.program_id(0) == 0)
    def _():
        piece_ref[:, : 3 * size] = qkv_full[...]
        piece_ref[:, 3 * size :] = out_full[...]


def pack_mlp_kernel(place_ref, up_ref, down_ref, up_full, down_full, up_piece, down_piece):
    up_full[...] = up_ref[...].astype(bf16)
    down_full[...] = down_ref[...].T.astype(bf16)

    @pl.when(pl.program_id(0) == 0)
    def _():
        up_piece[...] = up_full[...]
        down_piece[...] = down_full[...]


def packs_in_kernels(at, width, head_width):
    return (width // at.q_n) % 128 == 0 and head_width % 128 == 0


def pack_attn(at, qkv_weight, out_weight, head_width, after):
    width = qkv_weight.shape[0]
    part = width // at.q_n
    if packs_in_kernels(at, width, head_width):
        place = tie(jnp.stack([at.q, at.c]).astype(jnp.int32), after)[0]
        sizes = (3 * head_width, head_width)
        return pl.pallas_call(
            pack_attn_kernel,
            grid_spec=pltpu.PrefetchScalarGridSpec(
                num_scalar_prefetch=1,
                grid=(at.q_n,),
                in_specs=[
                    pl.BlockSpec((3, part, head_width), lambda k, p: (0, p[0] ^ k, p[1])),
                    pl.BlockSpec((head_width, part), lambda k, p: (p[1], p[0] ^ k)),
                ],
                out_specs=tuple(pl.BlockSpec((part, n), lambda k, p: (k, 0)) for n in sizes)
                + (pl.BlockSpec((part, sum(sizes)), lambda k, p: (0, 0)),),
            ),
            out_shape=tuple(jax.ShapeDtypeStruct((width, n), bf16) for n in sizes)
            + (jax.ShapeDtypeStruct((part, sum(sizes)), bf16),),
            name="pack_attn",
        )(place, jnp.transpose(qkv_weight, (1, 0, 2)), out_weight)
    qkv = lax.dynamic_slice_in_dim(qkv_weight, at.c * head_width, head_width, 2)
    out = lax.dynamic_slice_in_dim(out_weight, at.c * head_width, head_width, 0)
    qkv = at.relative(qkv.reshape(width, 3 * head_width).astype(bf16), 0)
    out = at.relative(out.astype(bf16).T, 0)
    return qkv, out, jnp.concatenate([qkv[:part], out[:part]], axis=1)


def pack_mlp(at, up_weight, down_weight, head_width, units, after):
    width = up_weight.shape[0]
    part = width // at.q_n
    if packs_in_kernels(at, width, head_width):
        place = tie(jnp.stack([at.q, at.c]).astype(jnp.int32), after)[0]
        return pl.pallas_call(
            pack_mlp_kernel,
            grid_spec=pltpu.PrefetchScalarGridSpec(
                num_scalar_prefetch=1,
                grid=(at.q_n,),
                in_specs=[
                    pl.BlockSpec((part, units), lambda k, p: (p[0] ^ k, p[1])),
                    pl.BlockSpec((units, part), lambda k, p: (p[1], p[0] ^ k)),
                ],
                out_specs=(
                    pl.BlockSpec((part, units), lambda k, p: (k, 0)),
                    pl.BlockSpec((part, units), lambda k, p: (k, 0)),
                    pl.BlockSpec((part, units), lambda k, p: (0, 0)),
                    pl.BlockSpec((part, units), lambda k, p: (0, 0)),
                ),
            ),
            out_shape=(jax.ShapeDtypeStruct((width, units), bf16),) * 2
            + (jax.ShapeDtypeStruct((part, units), bf16),) * 2,
            name="pack_mlp",
        )(place, up_weight, down_weight)
    up = lax.dynamic_slice_in_dim(up_weight, at.c * units, units, 1).astype(bf16)
    down = lax.dynamic_slice_in_dim(down_weight, at.c * units, units, 0).astype(bf16).T
    up, down = at.relative(up, 0), at.relative(down, 0)
    return up, down, up[:part], down[:part]


def join_kernel(plan, count, *refs):
    pieces, outs = refs[:count], refs[count:]
    for out_ref, (start_cols, rows) in zip(outs, plan):
        part = out_ref.shape[0] // len(rows)
        for k, chunks in enumerate(rows):
            col = 0
            for index, start, size in chunks:
                out_ref[k * part : (k + 1) * part, col : col + size] = pieces[index][
                    :part, start : start + size
                ]
                col += size


def join(pieces, part, plans):
    shapes = [
        jax.ShapeDtypeStruct((part * len(rows), sum(size for _, _, size in rows[0])), bf16)
        for rows in plans
    ]
    return pl.pallas_call(
        lambda *refs: join_kernel([(0, rows) for rows in plans], len(pieces), *refs),
        in_specs=[in_vmem] * len(pieces),
        out_specs=(in_vmem,) * len(plans),
        out_shape=tuple(shapes),
        compiler_params=pltpu.CompilerParams(vmem_limit_bytes=kernel_bytes),
        name="join",
    )(*pieces)


def gelu_parts(values):
    half = 0.5 * (1.0 + lax.erf(values * (0.5**0.5)))
    bell = jnp.exp(-0.5 * values * values) * 0.3989422804014327
    return (values * half, half + values * bell)


def row_tiles(rows, tile=256):
    tile = min(tile, rows)
    return [slice(start, start + tile) for start in range(0, rows, tile)]


def sum_nt_kernel(count, *refs):
    lefts, rights, out_ref = refs[:count], refs[count : 2 * count], refs[-1]
    for here in row_tiles(out_ref.shape[0]):
        total = dot_nt(lefts[0][here, :], rights[0][...])
        for left, right in zip(lefts[1:], rights[1:]):
            total = total + dot_nt(left[here, :], right[...])
        out_ref[here, :] = total.astype(bf16)


def cost_of(flops):
    return pl.CostEstimate(flops=flops // 2, bytes_accessed=1 << 20, transcendentals=0)


def sum_nt(lefts, rights):
    rows, width = lefts[0].shape[0], rights[0].shape[0]
    return pl.pallas_call(
        lambda *refs: sum_nt_kernel(len(lefts), *refs),
        in_specs=[in_vmem] * (2 * len(lefts)),
        out_specs=in_vmem,
        out_shape=jax.ShapeDtypeStruct((rows, width), bf16),
        compiler_params=pltpu.CompilerParams(vmem_limit_bytes=kernel_bytes),
        cost_estimate=cost_of(2 * rows * width * sum(v.shape[1] for v in lefts)),
        name="sum_nt",
    )(*lefts, *rights)


def up_kernel(normed_ref, weight_ref, bias_ref, act_ref, slope_ref):
    for here in row_tiles(act_ref.shape[0]):
        pre = dot_nn(normed_ref[here, :], weight_ref[...]) + bias_ref[...]
        act, slope = gelu_parts(pre)
        act_ref[here, :] = act.astype(bf16)
        slope_ref[here, :] = slope


def up_project(normed, weight, bias):
    rows, cols = normed.shape[0], weight.shape[1]
    return pl.pallas_call(
        up_kernel,
        in_specs=[in_vmem] * 3,
        out_specs=(in_vmem, in_vmem),
        out_shape=(
            jax.ShapeDtypeStruct((rows, cols), bf16),
            jax.ShapeDtypeStruct((rows, cols), f32),
        ),
        compiler_params=pltpu.CompilerParams(vmem_limit_bytes=kernel_bytes),
        cost_estimate=cost_of(2 * rows * cols * normed.shape[1]),
        name="up_project",
    )(normed, weight, bias[None, :])


def down_back_kernel(kept_ref, weight_ref, slope_ref, pre_ref, bias_ref):
    total = None
    for here in row_tiles(pre_ref.shape[0]):
        grad = (dot_nn(kept_ref[here, :], weight_ref[...]) * slope_ref[here, :]).astype(bf16)
        pre_ref[here, :] = grad
        part = jnp.sum(grad.astype(f32), axis=0, keepdims=True)
        total = part if total is None else total + part
    bias_ref[...] = total


def down_back(kept, weight, slope):
    rows, cols = slope.shape
    pre, bias = pl.pallas_call(
        down_back_kernel,
        in_specs=[in_vmem] * 3,
        out_specs=(in_vmem, in_vmem),
        out_shape=(
            jax.ShapeDtypeStruct((rows, cols), bf16),
            jax.ShapeDtypeStruct((1, cols), f32),
        ),
        compiler_params=pltpu.CompilerParams(vmem_limit_bytes=kernel_bytes),
        cost_estimate=cost_of(2 * rows * cols * kept.shape[1]),
        name="down_back",
    )(kept, weight, slope)
    return pre, bias[0]


def halves_kernel(order, shape, *refs):
    operands, (kept_ref, sent_ref) = refs[:-2], refs[-2:]
    part = operands[0].shape[1] // len(order)
    middle = len(order) // 2
    for index, block in enumerate(order):
        target = kept_ref if index < middle else sent_ref
        rows = slice(index % middle * part, (index % middle + 1) * part)
        col = 0
        number = 0
        for count in shape:
            left = operands[number][:, block * part : (block + 1) * part]
            number += 1
            for _ in range(count):
                right_ref = operands[number]
                number += 1
                size = right_ref.shape[1]
                target[rows, col : col + size] = dot_tn(left, right_ref[...]).astype(bf16)
                col += size


def grad_halves(at, pairs, first):
    rows, width = pairs[0][0].shape
    part = width // at.q_n
    order = at.scatter_order(first)
    middle = at.q_n // 2
    cols = sum(right.shape[1] for _, rights in pairs for right in rights)
    if part % 128 == 0:
        halves = jax.ShapeDtypeStruct((middle * part, cols), bf16)
        operands = [value for left, rights in pairs for value in (left, *rights)]
        return pl.pallas_call(
            lambda *refs: halves_kernel(order, [len(rights) for _, rights in pairs], *refs),
            in_specs=[in_vmem] * len(operands),
            out_specs=(in_vmem, in_vmem),
            out_shape=(halves, halves),
            compiler_params=pltpu.CompilerParams(vmem_limit_bytes=kernel_bytes),
            cost_estimate=pl.CostEstimate(
                flops=rows * width * cols, bytes_accessed=1 << 20, transcendentals=0
            ),
            name="grad_halves",
        )(*operands)
    return tuple(
        jnp.concatenate(
            [
                jnp.concatenate(
                    [
                        dot_tn(left[:, k * part : (k + 1) * part], right).astype(bf16)
                        for left, rights in pairs
                        for right in rights
                    ],
                    axis=1,
                )
                for k in side
            ],
            axis=0,
        )
        for side in (order[:middle], order[middle:])
    )


def adjust(weight, first, second, gradient, decay_rate, first_fix, second_fix):
    first_new = 0.9 * first + 0.1 * gradient
    second_new = 0.999 * second + 0.001 * gradient * gradient
    update = (
        first_new / first_fix / (jnp.sqrt(second_new / second_fix) + adam_eps) + decay_rate * weight
    )
    return (first_new, second_new, update)


def in_order(c, mine, other):
    return jnp.where(c == 0, mine, other), jnp.where(c == 0, other, mine)


def adjust_into(
    index, weight, moments_ref, gradient, fixes_ref, state_ref, update_ref, own_ref, sums_ref
):
    own_ref[...] = weight
    first_new, second_new, update = adjust(
        weight, moments_ref[0], moments_ref[1], gradient, weight_decay, fixes_ref[0], fixes_ref[1]
    )
    state_ref[0] = first_new
    state_ref[1] = second_new
    update_ref[...] = update
    sums_ref[2 * index] = jnp.sum(weight * weight)
    sums_ref[2 * index + 1] = jnp.sum(update * update)


def adjust_attn_kernel(
    place_ref, fixes_ref, mine_ref, other_ref, qkv_ref, out_ref, qkv_moments, out_moments,
    qkv_state, out_state, qkv_update, out_update, qkv_own, out_own, sums_ref,
):
    size = qkv_ref.shape[2] // 2
    one, two = in_order(place_ref[1], mine_ref[...], other_ref[...])
    parts = [
        jnp.concatenate([one[:, j * size : (j + 1) * size], two[:, j * size : (j + 1) * size]], 1)
        for j in range(4)
    ]
    adjust_into(
        0, qkv_ref[...], qkv_moments, jnp.stack(parts[:3]), fixes_ref,
        qkv_state, qkv_update, qkv_own, sums_ref,
    )
    adjust_into(
        1, out_ref[...], out_moments, parts[3].T, fixes_ref,
        out_state, out_update, out_own, sums_ref,
    )


def adjust_mlp_kernel(
    place_ref, fixes_ref, mine_ref, other_ref, up_ref, down_ref, up_moments, down_moments,
    up_state, down_state, up_update, down_update, up_own, down_own, sums_ref,
):
    size = up_ref.shape[1] // 2
    one, two = in_order(place_ref[1], mine_ref[...], other_ref[...])
    down_grad = jnp.concatenate([one[:, :size], two[:, :size]], axis=1)
    up_grad = jnp.concatenate([one[:, size:], two[:, size:]], axis=1)
    adjust_into(
        0, up_ref[...], up_moments, up_grad, fixes_ref, up_state, up_update, up_own, sums_ref
    )
    adjust_into(
        1, down_ref[...], down_moments, down_grad.T, fixes_ref,
        down_state, down_update, down_own, sums_ref,
    )


def own_spec(shape, dim, count):
    block = list(shape)
    block[dim] //= count
    return pl.BlockSpec(
        tuple(block), lambda i, p: tuple(p[0] if d == dim else 0 for d in range(len(shape)))
    )


def whole_spec(shape):
    return pl.BlockSpec(shape, lambda i, p: (0,) * len(shape))


def adjust_pair(at, kernel, place, fixes, mine, other, weights, dims, moments):
    parts = [m.shape[1:] for m in moments]
    shapes = [jax.ShapeDtypeStruct(m.shape, f32) for m in moments]
    shapes += [jax.ShapeDtypeStruct(p, f32) for p in parts] * 2
    return pl.pallas_call(
        kernel,
        grid_spec=pltpu.PrefetchScalarGridSpec(
            num_scalar_prefetch=1,
            grid=(1,),
            in_specs=[in_smem, whole_spec(mine.shape), whole_spec(other.shape)]
            + [own_spec(w.shape, d, at.dp_n) for w, d in zip(weights, dims)]
            + [whole_spec(m.shape) for m in moments],
            out_specs=tuple(whole_spec(s.shape) for s in shapes) + (in_smem,),
        ),
        out_shape=tuple(shapes) + (jax.ShapeDtypeStruct((4,), f32),),
        compiler_params=pltpu.CompilerParams(vmem_limit_bytes=back_bytes),
        name="adjust_pair",
    )(place, fixes, mine, other, *weights, *moments)


def adjust_small_kernel(
    fixes_ref, vec_grad, vec_moments, vec, bias_grad, bias_moments, bias, rel_grad, rel_moments,
    rel, vec_state, vec_new, weight_norms, update_norms, bias_state, bias_update, rel_state,
    rel_update, sums_ref,
):
    fixes = (fixes_ref[0], fixes_ref[1])
    first, second, update = adjust(
        vec[...], vec_moments[0], vec_moments[1], vec_grad[...], 0.0, *fixes
    )
    vec_state[0] = first
    vec_state[1] = second
    weight_norm = jnp.sqrt(jnp.sum(vec[...] * vec[...], axis=1, keepdims=True))
    update_norm = jnp.sqrt(jnp.sum(update * update, axis=1, keepdims=True))
    weight_norms[...] = weight_norm
    update_norms[...] = update_norm
    vec_new[...] = vec[...] - learn_rate * (weight_norm / (update_norm + adam_eps)) * update
    first, second, update = adjust(
        bias[...], bias_moments[0:1, :], bias_moments[1:2, :], bias_grad[...], 0.0, *fixes
    )
    bias_state[0:1, :] = first
    bias_state[1:2, :] = second
    bias_update[...] = update
    sums_ref[0] = jnp.sum(bias[...] * bias[...])
    sums_ref[1] = jnp.sum(update * update)
    first, second, update = adjust(
        rel[...], rel_moments[0], rel_moments[1], rel_grad[...], 0.0, *fixes
    )
    rel_state[0] = first
    rel_state[1] = second
    rel_update[...] = update
    sums_ref[2] = jnp.sum(rel[...] * rel[...])
    sums_ref[3] = jnp.sum(update * update)


def adjust_small(fixes, vec, bias, rel):
    shape = jax.ShapeDtypeStruct
    rows = vec[2].shape[0]
    return pl.pallas_call(
        adjust_small_kernel,
        in_specs=[in_smem] + [in_vmem] * 9,
        out_specs=(in_vmem,) * 8 + (in_smem,),
        out_shape=(
            shape(vec[1].shape, f32),
            shape(vec[2].shape, f32),
            shape((rows, 1), f32),
            shape((rows, 1), f32),
            shape(bias[1].shape, f32),
            shape(bias[2].shape, f32),
            shape(rel[1].shape, f32),
            shape(rel[2].shape, f32),
            shape((4,), f32),
        ),
        name="adjust_small",
    )(fixes, *vec, *bias, *rel)


def apply_kernel(rates_ref, *refs):
    count = len(refs) // 3
    for index in range(count):
        refs[2 * count + index][...] = (
            refs[index][...] - rates_ref[index] * refs[count + index][...]
        )


def apply_updates(rates, weights, updates):
    return pl.pallas_call(
        apply_kernel,
        in_specs=[in_smem] + [in_vmem] * (2 * len(updates)),
        out_specs=(in_vmem,) * len(updates),
        out_shape=tuple(jax.ShapeDtypeStruct(u.shape, f32) for u in updates),
        compiler_params=pltpu.CompilerParams(vmem_limit_bytes=kernel_bytes),
        name="apply_updates",
    )(rates, *weights, *updates)


def norm_parts(values):
    center = values - jnp.mean(values, axis=-1, keepdims=True)
    spread = jnp.mean(center * center, axis=-1, keepdims=True)
    inverse = lax.rsqrt(spread + norm_eps)
    return (center * inverse, inverse)


def norm_back(upstream, normed, inverse, gain_vec):
    scaled = upstream * gain_vec
    return inverse * (
        scaled
        - jnp.mean(scaled, axis=-1, keepdims=True)
        - normed * jnp.mean(scaled * normed, axis=-1, keepdims=True)
    )


def local(
    tokens,
    cotangent,
    lengths,
    buckets,
    step_count,
    qkv_weight,
    out_weight,
    up_weight,
    down_weight,
    up_bias,
    rel_bias,
    norm_vectors,
    qkv_moments,
    out_moments,
    up_moments,
    down_moments,
    bias_moments,
    rel_moments,
    vector_moments,
):
    per, length_rows, width = tokens.shape
    at = Places(per)
    seq_len = length_rows * at.mp_n
    blocks = at.slots
    q_n, c, q = at.q_n, at.c, at.q
    head_width = out_weight.shape[0] // 2
    heads = head_width // HD
    units = up_weight.shape[1] // 2
    bucket_count, local_heads = rel_bias.shape

    other_lengths = at.to_core(lengths)
    all_lengths = jnp.where(
        c == 0,
        jnp.concatenate([lengths, other_lengths]),
        jnp.concatenate([other_lengths, lengths]),
    )
    length = lax.dynamic_slice_in_dim(all_lengths, at.s, 1, 0)
    row_keep = jnp.arange(seq_len)[:, None] < length[0]
    row_mask = row_keep.astype(f32)
    vectors = at.relative(norm_vectors, 1)

    def half(values, dim, size):
        return lax.dynamic_slice_in_dim(values, c * size, size, dim)

    part = width // q_n
    small_own = jnp.concatenate(
        [half(up_bias, 0, units), half(rel_bias, 1, heads).T.reshape(-1)]
    )
    qkv_cols = 3 * head_width
    attn_cols = 4 * head_width
    high = lax.reduce_precision(small_own, 8, 7)
    rest = small_own - high
    mid = lax.reduce_precision(rest, 8, 7)
    three = jnp.concatenate([high, mid, rest - mid]).astype(bf16)
    small_rows = -(-three.size // (16 * attn_cols)) * 16
    three = jnp.pad(three, (0, small_rows * attn_cols - three.size)).reshape(small_rows, attn_cols)

    def small_of(rows_low):
        flat = rows_low.reshape(-1).astype(f32)
        count = small_own.size
        return (flat[:count] + flat[count : 2 * count]) + flat[2 * count : 3 * count]

    tokens_near = at.relative(tokens, 2)
    token_pieces = {step: at.collect_piece(tokens_near, step) for step in (0, 2, 3, 1)}
    qkv_own, out_own, attn_piece = pack_attn(
        at, qkv_weight, out_weight, head_width, tokens_near
    )
    attn_piece = jnp.concatenate([attn_piece, three], axis=0)
    attn_one = at.to_slot(attn_piece, 1)
    up_own, down_own, up_piece, down_piece = pack_mlp(
        at, up_weight, down_weight, head_width, units, attn_piece
    )
    mlp_piece = jnp.concatenate([up_piece, down_piece], axis=1)
    attn_one = after(attn_one, token_pieces[1], mlp_piece)
    attn_inner = at.spread_inner(attn_piece, attn_one)
    attn_near = at.gather_start(attn_one[:part])
    tokens_there = (after(token_pieces[2], attn_one), token_pieces[3])
    token_pieces[2] = tokens_there[0]
    mlp_one = at.to_slot(after(mlp_piece, *tokens_there), 1)
    inputs_home = at.collect_end([token_pieces[k] for k in range(blocks)])
    attn_pieces = at.gather_end(
        attn_one[:part], {b: after(v, *tokens_there) for b, v in attn_near.items()}, 0
    )
    inputs_low = at.collect_both(inputs_home)
    inputs_low = after(inputs_low, attn_inner, *attn_pieces)
    attn_outer = at.spread_outer(attn_inner)
    up_one, down_one = mlp_one[:, :units], mlp_one[:, units:]
    up_inner = at.spread_inner(up_piece, up_one)
    mlp_near = at.gather_start(mlp_one)
    turn = 1 % len(at.q_bits)
    attn_pair = at.spread_pair(attn_inner, attn_outer)
    pair_first = after(attn_pair[:part], *mlp_near.values(), up_inner)
    small = [
        small_own,
        small_of(attn_one[part:]),
        small_of(attn_pair[part:, :attn_cols]),
        small_of(attn_pair[part:, attn_cols:]),
    ]
    tile = tile_of(seq_len)
    tiles = seq_len // tile
    padded = jnp.concatenate([jnp.zeros((tile,), jnp.int32), buckets])
    spread = jnp.concatenate(
        [padded[kk * tile : (kk + 2) * tile] for kk in range(tiles)]
    )
    choose = (jnp.arange(bucket_count, dtype=jnp.int32)[:, None] == spread[None, :]).astype(f32)

    def lines_of(r):
        rel_rows = small[r][units:].reshape(heads, bucket_count)
        return jnp.dot(rel_rows, choose, precision=lax.Precision.HIGHEST)


    columns = range(q_n)
    qkv_one, out_one = join(
        attn_pieces,
        part,
        [
            [[(k, 0, qkv_cols)] for k in columns],
            [[(k, qkv_cols, head_width)] for k in columns],
        ],
    )
    qkv_w, out_w = [qkv_own, qkv_one], [out_own, out_one]

    first_parts = norm_parts(inputs_low.astype(f32))
    first_normed, first_inverse = first_parts
    first_low = (first_normed * vectors[0] + vectors[1]).astype(bf16)
    qkv, contexts, totals = [], [], []

    def attention(r, *others):
        qkv.append(after(dot_nn(first_low, qkv_w[r]).astype(bf16), *others))
        context, total = attend(length, qkv[r], lines_of(r), heads)
        contexts.append(context)
        totals.append(total)

    attention(0, mlp_one)
    pair_first = after(pair_first, contexts[0])
    pair_near = at.gather_start(pair_first)
    up_outer = at.spread_outer(after(up_inner, *mlp_near.values()))
    down_inner = at.spread_inner(after(down_piece, up_inner, *mlp_near.values()), down_one)
    attention(1, attn_outer)
    near_done = (*pair_near.values(), up_outer, down_inner)
    pair_near = {b: after(v, *near_done, contexts[1]) for b, v in pair_near.items()}
    pair_pieces = []
    for k in range(2):
        cols = slice(k * attn_cols, (k + 1) * attn_cols)
        pair_pieces.append(
            at.gather_end(
                pair_first[:, cols], {b: v[:, cols] for b, v in pair_near.items()}, k * turn
            )
        )
    down_outer = at.spread_outer(after(down_inner, *near_done))
    incoming_near = at.relative(after(cotangent, *near_done), 2)
    incoming_pieces = {step: at.collect_piece(incoming_near, step) for step in (2, 3)}
    pair_done = [v for pieces in pair_pieces for v in pieces[1:]]
    mlp_near = {b: after(v, *pair_done) for b, v in mlp_near.items()}
    up_one_pieces = at.gather_end(up_one, {b: v[:, :units] for b, v in mlp_near.items()}, 0)
    down_one_pieces = at.gather_end(
        down_one, {b: v[:, units:] for b, v in mlp_near.items()}, turn
    )
    one_done = (*up_one_pieces, *down_one_pieces, down_outer)
    up_pair = after(at.spread_pair(up_inner, up_outer), *one_done)
    up_near = at.gather_start(up_pair)
    incoming_near = after(incoming_near, *one_done)
    incoming_pieces.update({step: at.collect_piece(incoming_near, step) for step in (0, 1)})
    down_pair = after(at.spread_pair(down_inner, down_outer), *up_near.values())

    def pair_halves(piece, near):
        halves = []
        for k in range(2):
            cols = slice(k * units, (k + 1) * units)
            halves.append(
                at.gather_end(piece[:, cols], {b: v[:, cols] for b, v in near.items()}, k * turn)
            )
        return halves

    def pair_join(halves):
        return join(
            halves[0] + halves[1], part, [[[(k, 0, units), (k + q_n, 0, units)] for k in columns]]
        )[0]

    up_halves = pair_halves(up_pair, up_near)
    down_near = at.gather_start(down_pair)
    down_near = {b: after(v, up_halves[0][-1], up_halves[1][-1]) for b, v in down_near.items()}
    down_halves = pair_halves(down_pair, down_near)
    joined = join(
        pair_pieces[0] + pair_pieces[1],
        part,
        [
            [[(k + half_at, start, size)] for k in columns]
            for half_at in (0, q_n)
            for start, size in ((0, qkv_cols), (qkv_cols, head_width))
        ],
    )
    qkv_w += joined[0::2]
    out_w += joined[1::2]
    attention(2, *one_done)
    attention(3, *up_near.values())
    incoming_home = at.collect_end([incoming_pieces[k] for k in range(blocks)])
    rows_of = [[(k, 0, units)] for k in columns]
    up_w = [up_own, join(up_one_pieces, part, [rows_of])[0], pair_join(up_halves)]
    down_w = [down_own, join(down_one_pieces, part, [rows_of])[0], pair_join(down_halves)]

    inputs = inputs_low.astype(f32)
    mixed = at.sum_team(sum_nt(contexts, out_w))
    mixed = after(mixed, *up_near.values())
    middle = inputs + (mixed + vectors[4]) * row_mask
    second_normed, second_inverse = norm_parts(middle)
    second_low = (second_normed * vectors[2] + vectors[3]).astype(bf16)
    acts, slopes = [], []
    biases = [small[0][:units], small[1][:units], jnp.concatenate([small[2][:units], small[3][:units]])]
    for r in range(3):
        act, slope = up_project(second_low, up_w[r], biases[r])
        acts.append(act)
        slopes.append(slope)
    incoming_low = at.collect_both(incoming_home)
    kept = jnp.where(row_keep, incoming_low, jnp.zeros_like(incoming_low))
    fed_bias_grad = jnp.sum(kept.astype(f32), axis=0)
    bias_grads = [None] * blocks

    pre_pair, bias_pair = down_back(kept, down_w[2], slopes[2])
    bias_grads[2], bias_grads[3] = bias_pair[:units], bias_pair[units:]
    up_far_halves = grad_halves(at, [(second_low, [pre_pair])], 1)
    up_far = ChipSum(at, up_far_halves, 1)
    down_far_halves = grad_halves(at, [(after(kept, *up_far_halves), [acts[2]])], 0)
    down_far = ChipSum(at, down_far_halves, 0)
    down_near_halves = grad_halves(at, [(after(kept, *down_far_halves), acts[:2])], 0)
    fed_low = sum_nt([after(acts[0], *down_far_halves)] + acts[1:], down_w)
    fed_share = at.sum_share(fed_low, length_rows)
    middle_share = at.share(middle, length_rows, 0, 0)
    mask_share = at.share(row_mask, length_rows, 0, 0)
    out_share = (middle_share + (fed_share + vectors[5]) * mask_share).astype(bf16)
    out_got = at.deliver_first(out_share)
    kept_late = after(kept, fed_low, *down_far_halves)
    pre_own, bias_grads[0] = down_back(kept_late, down_w[0], slopes[0])
    pre_one, bias_grads[1] = down_back(kept_late, down_w[1], slopes[1])
    back_low = sum_nt([pre_own, pre_one, pre_pair], up_w)
    up_near_halves = grad_halves(at, [(after(second_low, back_low), [pre_own, pre_one])], 1)
    second_grad = at.sum_team(back_low)
    second_grad = after(second_grad, *up_near_halves)
    lead = jnp.where((c == 0) & (at.t == 0), 1.0, 0.0)
    gain_two = jnp.sum(second_grad * second_normed, axis=0)
    shift_two = jnp.sum(second_grad, axis=0)
    middle_grad = incoming_low.astype(f32) + norm_back(
        second_grad, second_normed, second_inverse, vectors[2]
    )
    branch = jnp.where(row_keep, middle_grad, 0.0).astype(bf16)
    mix_bias_grad = jnp.sum(branch.astype(f32), axis=0)
    rel_grads = [None] * blocks
    branch = after(branch, up_far.got, down_far.got)
    context_grads = [dot_nn(branch, out_w[r]).astype(bf16) for r in range(blocks)]
    own_cols = slice(0, units)
    far_cols = slice(units, 2 * units)
    attn_sums = [None] * blocks
    attn_halves = [None] * blocks
    proj_grads = [None] * blocks
    for r in reversed(range(blocks)):
        context_grad = context_grads[r]
        if r == 3:
            there = (up_far.got, down_far.got)
            up_far.rest(*there)
            down_far.rest(*there)
        if r == 2:
            far_done = (up_far.got, down_far.got)
            context_grad = after(context_grad, *far_done)
            down_near_sum = ChipSum(at, [after(v, *far_done) for v in down_near_halves], 0)
            up_near_sum = ChipSum(at, [after(v, *far_done) for v in up_near_halves], 1)
            far_sums = (down_far.total(), up_far.total())
            mlp_far = jnp.concatenate(
                [v[:, cols] for cols in (own_cols, far_cols) for v in far_sums], axis=1
            ).astype(bf16)
            far_got = at.fold_outer(mlp_far)
        if r == 1:
            context_grad = after(context_grad, out_got)
        if r == 0:
            near_firsts = (down_near_sum.got, up_near_sum.got)
            context_grad = after(context_grad, *near_firsts, far_got)
            mlp_far = at.fold_add(mlp_far, after(far_got, *near_firsts))
            down_near_sum.rest(*near_firsts)
            up_near_sum.rest(*near_firsts)
            near_done = (down_near_sum.got, up_near_sum.got)
        proj_grad, dist = attend_back(
            length, qkv[r], lines_of(r), totals[r], context_grad, heads
        )
        rel_grads[r] = dist
        if r == 0:
            proj_grad = after(proj_grad, *near_done)
        attn_halves[r] = grad_halves(
            at, [(first_low, [proj_grad]), (branch, [contexts[r]])], r % 2
        )
        proj_grads[r] = proj_grad
    back_low = sum_nt(proj_grads, qkv_w)
    inner_got = at.fold_inner(after(mlp_far, back_low))
    out_pair = at.deliver_pair(out_share, after(out_got, far_got, back_low))
    out_last = at.deliver_last(out_pair)
    for k in (3, 2):
        attn_sums[k] = ChipSum(at, [after(v, *near_done) for v in attn_halves[k]], k % 2)
    firsts = (attn_sums[3].got, attn_sums[2].got)
    first_grad = at.sum_share(back_low, length_rows)
    for k in (3, 2):
        attn_sums[k].rest(*firsts)
    attn_far = jnp.concatenate([attn_sums[2].total(), attn_sums[3].total()], axis=1).astype(bf16)
    mlp_size = 2 * units
    mlp_near = (down_near_sum.total(), up_near_sum.total())
    mlp_one = jnp.concatenate([v[:, far_cols] for v in mlp_near], axis=1)
    mlp_own = jnp.concatenate([v[:, own_cols] for v in mlp_near], axis=1)
    mlp_one = (mlp_one + inner_got[:, :mlp_size].astype(f32)).astype(bf16)
    rel_grad = lax.dot_general(
        jnp.concatenate(rel_grads, axis=0),
        choose,
        (((1,), (1,)), ((), ())),
        precision=lax.Precision.HIGHEST,
    )
    normed_share = at.share(first_normed, length_rows, 0, 0)
    inverse_share = at.share(first_inverse, length_rows, 0, 0)
    middle_grad_share = at.share(middle_grad, length_rows, 0, 0)
    gain_one = jnp.sum(first_grad * normed_share, axis=0)
    shift_one = jnp.sum(first_grad, axis=0)
    input_share = middle_grad_share + norm_back(
        first_grad, normed_share, inverse_share, vectors[0]
    )
    input_low = input_share.astype(bf16)
    def by_place(rows_of):
        around = jnp.stack(rows_of)
        moved = []
        for place in range(blocks):
            picked = around[0]
            for k in range(1, blocks):
                picked = jnp.where(at.s ^ k == place, around[k], picked)
            moved.append(picked)
        moved = jnp.stack(moved)[:, None, None, :]
        here = (jnp.arange(at.t_n)[:, None] == at.t) & (jnp.arange(2)[None, :] == c)
        return jnp.where(here[None, :, :, None], moved, 0.0).reshape(at.mp_n, 2, -1)

    vector_grad = jnp.concatenate(
        [
            jnp.stack([gain_one, shift_one]),
            lead * jnp.stack([gain_two, shift_two, mix_bias_grad, fed_bias_grad]),
        ]
    )
    small_grad = by_place(
        [
            jnp.concatenate([bias_grads[r], rel_grad[r * heads : (r + 1) * heads].reshape(-1)])
            for r in range(blocks)
        ]
    )
    last_got = at.to_slot(mlp_one, 1)
    plane = at.sum_plane(
        jnp.concatenate([at.relative(vector_grad, 1).reshape(-1), small_grad.reshape(-1)])
    )
    there = (attn_sums[3].got, attn_sums[2].got, plane)
    for k in (1, 0):
        attn_sums[k] = ChipSum(at, [after(v, *there) for v in attn_halves[k]], k % 2)
    there = (attn_sums[1].got, attn_sums[0].got)
    for k in (1, 0):
        attn_sums[k].rest(*there)
    joined = at.sum_column(after(plane, last_got))
    input_got = at.deliver_first(after(input_low, joined))
    attn_got = at.fold_outer(after(attn_far, joined))
    mlp_mine = mlp_own + inner_got[:, mlp_size:].astype(f32) + last_got.astype(f32)
    attn_got = after(attn_got, attn_sums[0].got, attn_sums[1].got, input_got)
    rows = part // 2

    def exchanged(mine):
        sent = lax.dynamic_slice_in_dim(mine, (1 - c) * rows, rows, 0)
        return lax.dynamic_slice_in_dim(mine, c * rows, rows, 0), at.to_core(sent)

    mlp_mine, mlp_other = exchanged(mlp_mine)
    steps_done = step_count[0].astype(f32)
    first_fix = 1.0 - jnp.power(jnp.float32(0.9), steps_done)
    second_fix = 1.0 - jnp.power(jnp.float32(0.999), steps_done)
    fixes = jnp.stack([first_fix, second_fix])
    qkv_view = jnp.transpose(qkv_weight, (1, 0, 2))
    qkv_mom = jnp.transpose(qkv_moments, (0, 2, 1, 3))
    weights = [qkv_view, out_weight, up_weight, down_weight]
    dims = [1, 1, 0, 1]
    in_kernels = rows % 128 == 0
    if in_kernels:
        place = jnp.stack([at.dp_i, c]).astype(jnp.int32)
        up_state, down_state, up_update, down_update, up_mine, down_mine, mlp_squares = adjust_pair(
            at, adjust_mlp_kernel, place, fixes, mlp_mine, mlp_other,
            weights[2:], dims[2:], [up_moments, down_moments],
        )
        attn_got = after(attn_got, mlp_squares)
    attn_inner_got = at.fold_inner(at.fold_add(attn_far, attn_got))
    attn_one_sum = attn_inner_got[:, :attn_cols].astype(f32) + attn_sums[1].total()
    attn_last_got = at.to_slot(attn_one_sum.astype(bf16), 1)
    attn_mine = (
        attn_sums[0].total()
        + attn_inner_got[:, attn_cols:].astype(f32)
        + attn_last_got.astype(f32)
    )
    input_pair = at.deliver_pair(input_low, input_got)
    input_last = at.deliver_last(input_pair)
    input_grad = at.relative(at.delivered(input_pair, input_last), 2).astype(f32)
    vector_grad = joined[: vector_grad.size].reshape(vector_grad.shape)
    small_sum = lax.dynamic_index_in_dim(
        joined[vector_grad.size :].reshape(small_grad.shape), at.mp_i, 0, keepdims=False
    )
    bias_sum = small_sum[:, :units].reshape(1, -1)
    rel_sum = small_sum[:, units:].reshape(2 * heads, bucket_count).T

    attn_mine, attn_other = exchanged(attn_mine)

    if in_kernels:
        qkv_state, out_state, qkv_update, out_update, qkv_mine, out_mine, attn_squares = adjust_pair(
            at, adjust_attn_kernel, place, fixes, attn_mine, attn_other,
            weights[:2], dims[:2], [qkv_mom, out_moments],
        )
        squares = jnp.concatenate([attn_squares, mlp_squares])
        updates = [qkv_update, out_update, up_update, down_update]
        states = [qkv_state, out_state, up_state, down_state]
        own_weights = [qkv_mine, out_mine, up_mine, down_mine]
    else:
        one, two = in_order(c, attn_mine, attn_other)
        parts = [
            jnp.concatenate(
                [v[:, j * head_width : (j + 1) * head_width] for v in (one, two)], axis=1
            )
            for j in range(4)
        ]
        one, two = in_order(c, mlp_mine, mlp_other)
        grads = [
            jnp.stack(parts[:3]),
            parts[3].T,
            jnp.concatenate([one[:, units:], two[:, units:]], axis=1),
            jnp.concatenate([one[:, :units], two[:, :units]], axis=1).T,
        ]
        own_weights, updates, states, squares = [], [], [], []
        for weight, dim, moments, grad in zip(
            weights, dims, [qkv_mom, out_moments, up_moments, down_moments], grads
        ):
            count = weight.shape[dim] // at.dp_n
            weight = lax.dynamic_slice_in_dim(weight, at.dp_i * count, count, dim)
            first_new, second_new, update = adjust(
                weight, moments[0], moments[1], grad, weight_decay, first_fix, second_fix
            )
            own_weights.append(weight)
            updates.append(update)
            states.append(jnp.stack([first_new, second_new]))
            squares += [jnp.sum(weight * weight), jnp.sum(update * update)]
        squares = jnp.stack(squares)
    (
        vector_state, vector_new, vector_norms, vector_update_norms,
        bias_state, bias_update, rel_state, rel_update, small_squares,
    ) = adjust_small(
        fixes,
        (vector_grad, vector_moments, norm_vectors),
        (bias_sum, bias_moments, up_bias[None, :]),
        (rel_sum, rel_moments, rel_bias),
    )
    lead_dp = (at.dp_i == 0).astype(f32)
    squares = jnp.concatenate([squares, lead_dp * small_squares])
    squares = after(at.sum_plane(squares), input_last)
    squares = at.sum_column(squares).reshape(6, 2)
    norms = jnp.sqrt(squares)
    rates = learn_rate * (norms[:, 0] / (norms[:, 1] + adam_eps))
    small_weights = [up_bias[None, :], rel_bias]
    small_updates = [bias_update, rel_update]
    if in_kernels:
        *new, bias_new, rel_new = apply_updates(
            rates, own_weights + small_weights, updates + small_updates
        )
    else:
        new = [own_weights[k] - rates[k] * updates[k] for k in range(4)]
        bias_new, rel_new = apply_updates(rates[4:], small_weights, small_updates)
    new, states = list(new), list(states)
    new[0] = jnp.transpose(new[0], (1, 0, 2))
    states[0] = jnp.transpose(states[0], (0, 2, 1, 3))
    block_out = at.relative(at.delivered(out_pair, out_last), 2)
    results = [block_out, input_grad]
    for k in range(4):
        results += [new[k], states[k]]
    results += [bias_new[0], bias_state, rel_new, rel_state, vector_new, vector_state]
    results.append(
        jnp.concatenate(
            [norms, jnp.concatenate([vector_norms, vector_update_norms], axis=1)]
        ).T
    )
    return tuple(results)


def solution(mesh):
    return jax.shard_map(
        local,
        mesh=mesh,
        in_specs=(
            P("dp", "mp", None),
            P("dp", "mp", None),
            P("dp"),
            P(),
            P(),
            P(None, None, "mp"),
            P("mp", None),
            P(None, "mp"),
            P("mp", None),
            P("mp"),
            P(None, "mp"),
            P(),
            P(None, "dp", None, "mp"),
            P(None, "mp", "dp"),
            P(None, "dp", "mp"),
            P(None, "mp", "dp"),
            P(None, "mp"),
            P(None, None, "mp"),
            P(),
        ),
        out_specs=(
            P("dp", "mp", None),
            P("dp", "mp", None),
            P("dp", None, "mp"),
            P(None, "dp", None, "mp"),
            P("mp", "dp"),
            P(None, "mp", "dp"),
            P("dp", "mp"),
            P(None, "dp", "mp"),
            P("mp", "dp"),
            P(None, "mp", "dp"),
            P("mp"),
            P(None, "mp"),
            P(None, "mp"),
            P(None, None, "mp"),
            P(),
            P(),
            P(),
        ),
        check_vma=False,
    )
```

```python
import jax
import jax.numpy as jnp
from jax import lax
from jax.experimental import pallas as pl
from jax.experimental.pallas import tpu as pltpu
from jax.sharding import PartitionSpec as P

HD = 64
f32 = jnp.float32
bf16 = jnp.bfloat16

norm_eps = 1e-05
adam_eps = 1e-06
learn_rate = 0.25
weight_decay = 0.1
masked_score = -1000000000.0
score_scale = HD ** (-0.5)
kernel_bytes = 16 << 20
back_bytes = 24 << 20

in_vmem = pl.BlockSpec(memory_space=pltpu.VMEM)
in_smem = pl.BlockSpec(memory_space=pltpu.SMEM)


def dot_nt(left, right):
    return lax.dot_general(left, right, (((1,), (1,)), ((), ())), preferred_element_type=f32)


def dot_nn(left, right):
    return lax.dot_general(left, right, (((1,), (0,)), ((), ())), preferred_element_type=f32)


def dot_tn(left, right):
    return lax.dot_general(left, right, (((0,), (0,)), ((), ())), preferred_element_type=f32)


def tile_of(rows):
    return min(256, rows)


def bias_tiles(line_ref, head, tiles, tile):
    causal = lax.broadcasted_iota(jnp.int32, (tile, tile), 0) <= lax.broadcasted_iota(
        jnp.int32, (tile, tile), 1
    )
    made = []
    for kk in range(tiles):
        line = line_ref[head : head + 1, kk * 2 * tile : (kk + 1) * 2 * tile]
        wide = jnp.broadcast_to(line, (tile, 2 * tile))
        made.append(pltpu.roll(wide, tile, 1, stride=1, stride_axis=0)[:, :tile])
    made[0] = jnp.where(causal, made[0], masked_score)
    return made


def scores_of(keys, query, toeplitz, block, tile, key_pos, length):
    count = (block + 1) * tile
    raw = dot_nt(keys[:count], query)
    raw = raw + jnp.concatenate([toeplitz[block - j] for j in range(block + 1)], axis=0)
    return jnp.where(key_pos[:count] < length, raw, masked_score)


def attend_kernel(heads, length_ref, qkv_ref, line_ref, ctx_ref, lse_ref):
    rows = qkv_ref.shape[0]
    tile = tile_of(rows)
    tiles = rows // tile
    width = heads * HD
    length = length_ref[0]
    key_pos = lax.broadcasted_iota(jnp.int32, (rows, tile), 0)
    for head in range(heads):
        toeplitz = bias_tiles(line_ref, head, tiles, tile)
        cols = slice(head * HD, (head + 1) * HD)
        keys = qkv_ref[:, width + head * HD : width + (head + 1) * HD]
        vals = qkv_ref[:, 2 * width + head * HD : 2 * width + (head + 1) * HD]
        for block in range(tiles):
            here = slice(block * tile, (block + 1) * tile)
            count = (block + 1) * tile
            query = qkv_ref[here, cols] * jnp.asarray(score_scale, bf16)
            raw = scores_of(keys, query, toeplitz, block, tile, key_pos, length)
            top = jnp.max(raw, axis=0, keepdims=True)
            grown = jnp.exp(raw - top)
            total = jnp.sum(grown, axis=0, keepdims=True)
            probs = (grown * (1.0 / total)).astype(bf16)
            ctx_ref[here, cols] = dot_tn(probs, vals[:count]).astype(bf16)
            lse_ref[head : head + 1, here] = top + jnp.log(total)


def attend_back_kernel(
    heads,
    length_ref,
    qkv_ref,
    line_ref,
    lse_ref,
    grad_ref,
    out_ref,
    dist_ref,
    key_acc,
    val_acc,
    diag_acc,
):
    rows = qkv_ref.shape[0]
    tile = tile_of(rows)
    tiles = rows // tile
    width = heads * HD
    length = length_ref[0]
    key_pos = lax.broadcasted_iota(jnp.int32, (rows, tile), 0)
    for head in range(heads):
        toeplitz = bias_tiles(line_ref, head, tiles, tile)
        cols = slice(head * HD, (head + 1) * HD)
        key_cols = slice(width + head * HD, width + (head + 1) * HD)
        val_cols = slice(2 * width + head * HD, 2 * width + (head + 1) * HD)
        keys = qkv_ref[:, key_cols]
        vals = qkv_ref[:, val_cols]
        key_acc[...] = jnp.zeros_like(key_acc)
        val_acc[...] = jnp.zeros_like(val_acc)
        diag_acc[...] = jnp.zeros_like(diag_acc)
        for block in range(tiles):
            here = slice(block * tile, (block + 1) * tile)
            count = (block + 1) * tile
            query = qkv_ref[here, cols] * jnp.asarray(score_scale, bf16)
            grad = grad_ref[here, cols]
            raw = scores_of(keys, query, toeplitz, block, tile, key_pos, length)
            probs = jnp.exp(raw - lse_ref[head : head + 1, here])
            pgrad = dot_nt(vals[:count], grad)
            drop = jnp.sum(probs * pgrad, axis=0, keepdims=True)
            sgrad = (probs * (pgrad - drop)).astype(bf16)
            val_acc[:count] += dot_nn(probs.astype(bf16), grad)
            key_acc[:count] += dot_nn(sgrad, query)
            out_ref[here, cols] = (dot_tn(sgrad, keys[:count]) * score_scale).astype(bf16)
            wide = sgrad.astype(f32)
            for j in range(block + 1):
                diag_acc[block - j] += wide[j * tile : (j + 1) * tile]
        out_ref[:, key_cols] = key_acc[...].astype(bf16)
        out_ref[:, val_cols] = val_acc[...].astype(bf16)
        for kk in range(tiles):
            held = jnp.concatenate([diag_acc[kk], jnp.zeros((tile, tile), f32)], axis=1)
            half = tile // 2
            while half >= 1:
                held = held[:half] + pltpu.roll(held[half : 2 * half], 2 * tile - half, 1)
                half //= 2
            dist_ref[head : head + 1, kk * 2 * tile : (kk + 1) * 2 * tile] = pltpu.roll(held, tile, 1)


def attend(length, qkv, line, heads):
    rows = qkv.shape[0]
    return pl.pallas_call(
        lambda *refs: attend_kernel(heads, *refs),
        out_shape=(
            jax.ShapeDtypeStruct((rows, heads * HD), bf16),
            jax.ShapeDtypeStruct((heads, rows), f32),
        ),
        in_specs=[in_smem, in_vmem, in_vmem],
        out_specs=(in_vmem, in_vmem),
        compiler_params=pltpu.CompilerParams(vmem_limit_bytes=kernel_bytes),
        cost_estimate=pl.CostEstimate(
            flops=heads * rows * rows * HD * 10,
            bytes_accessed=1 << 20,
            transcendentals=0,
        ),
        name="attend",
    )(length, qkv, line)


def attend_back(length, qkv, line, lse, grad, heads):
    rows = qkv.shape[0]
    tile = tile_of(rows)
    return pl.pallas_call(
        lambda *refs: attend_back_kernel(heads, *refs),
        out_shape=(
            jax.ShapeDtypeStruct((rows, 3 * heads * HD), bf16),
            jax.ShapeDtypeStruct((heads, 2 * rows), f32),
        ),
        in_specs=[in_smem, in_vmem, in_vmem, in_vmem, in_vmem],
        out_specs=(in_vmem, in_vmem),
        scratch_shapes=[
            pltpu.VMEM((rows, HD), f32),
            pltpu.VMEM((rows, HD), f32),
            pltpu.VMEM((rows // tile, tile, tile), f32),
        ],
        compiler_params=pltpu.CompilerParams(vmem_limit_bytes=back_bytes),
        cost_estimate=pl.CostEstimate(
            flops=heads * rows * rows * HD * 20,
            bytes_accessed=1 << 20,
            transcendentals=0,
        ),
        name="attend_back",
    )(length, qkv, line, lse, grad)


def tie(*values):
    return lax.optimization_barrier(values)


def after(values, *others):
    return lax.optimization_barrier((values, *others))[0]


class Places:
    def __init__(self, per):
        self.per = per
        self.dp_n = lax.axis_size("dp")
        self.mp_n = lax.axis_size("mp")
        self.q_n = self.dp_n // 2
        self.slots = 2 * per
        self.t_n = self.mp_n // self.slots
        assert self.dp_n % 2 == 0 and self.mp_n % self.slots == 0
        dp_i = lax.axis_index("dp")
        mp_i = lax.axis_index("mp")
        self.dp_i, self.mp_i = dp_i, mp_i
        self.q, self.c = dp_i // 2, lax.rem(dp_i, 2)
        self.s, self.t = mp_i // self.t_n, lax.rem(mp_i, self.t_n)
        assert per == 2
        self.home = self.s // per
        self.at_home = self.c == self.home
        self.q_bits = []
        while (1 << len(self.q_bits)) < self.q_n:
            self.q_bits.append(1 << len(self.q_bits))
        assert (1 << len(self.q_bits)) == self.q_n

    def move(self, values, target):
        pairs = []
        for q in range(self.q_n):
            for c in range(2):
                for s in range(self.slots):
                    for t in range(self.t_n):
                        found = target(q, c, s, t)
                        if found is not None:
                            nq, nc, ns, nt = found
                            pairs.append(
                                (
                                    (q * 2 + c) * self.mp_n + s * self.t_n + t,
                                    (nq * 2 + nc) * self.mp_n + ns * self.t_n + nt,
                                )
                            )
        return lax.ppermute(values, ("dp", "mp"), pairs)

    def to_core(self, values):
        return self.move(values, lambda q, c, s, t: (q, 1 - c, s, t))

    def to_slot(self, values, step):
        return self.move(values, lambda q, c, s, t: (q, c, s ^ step, t))

    def to_chip(self, values, bit):
        return self.move(values, lambda q, c, s, t: (q ^ bit, c, s, t))

    def to_team(self, values, step):
        return self.move(values, lambda q, c, s, t: (q, c, s, (t + step) % self.t_n))

    def relative(self, values, dim):
        size = values.shape[dim] // self.q_n
        return jnp.concatenate(
            [
                lax.dynamic_slice_in_dim(values, (self.q ^ k) * size, size, dim)
                for k in range(self.q_n)
            ],
            axis=dim,
        )

    def block_at(self, step):
        return lax.rem(self.s + step, self.slots) * self.t_n + self.t

    def collect_piece(self, local, step):
        piece = lax.dynamic_index_in_dim(local, (self.s ^ step) % 2, 0, keepdims=False)
        if step == 0:
            return piece
        return self.move(
            piece,
            lambda q, c, s, t: (
                (q, c, s ^ step, t) if (s ^ step) // self.per == c else None
            ),
        )

    def collect_end(self, pieces):
        count, width = pieces[0].shape
        whole = jnp.zeros((count * self.mp_n, width), pieces[0].dtype)
        for step, piece in enumerate(pieces):
            for turn in range(self.t_n):
                piece_t = self.to_team(piece, turn) if turn > 0 else piece
                from_t = lax.rem(self.t + self.t_n - turn, self.t_n)
                whole = lax.dynamic_update_slice_in_dim(
                    whole, piece_t, ((self.s ^ step) * self.t_n + from_t) * count, 0
                )
        return whole

    def collect_both(self, whole):
        other = self.move(
            whole, lambda q, c, s, t: (q, 1 - c, s, t) if c == s // self.per else None
        )
        return jnp.where(self.at_home, whole, other)

    def deliver_first(self, blocks):
        return self.move(
            blocks, lambda q, c, s, t: (q, 1 - c, s ^ 2, t) if c != s // 2 else None
        )

    def deliver_pair(self, blocks, got):
        return jnp.where(self.at_home, blocks, got)

    def deliver_last(self, pair):
        return self.to_slot(pair[pair.shape[0] // 2 :], 1)

    def delivered(self, pair, got):
        mine = pair[: pair.shape[0] // 2]
        even = self.s % 2 == 0
        return jnp.stack([jnp.where(even, mine, got), jnp.where(even, got, mine)])

    def share(self, values, length, flip, team):
        side = jnp.where(self.at_home, 0, 1) ^ flip
        parts = []
        for index in range(self.per):
            slot = self.s ^ (self.per * side + index)
            block = slot * self.t_n + lax.rem(self.t + team, self.t_n)
            parts.append(lax.dynamic_slice_in_dim(values, block * length, length, 0))
        return jnp.concatenate(parts, axis=0)

    def sum_share(self, partial, length):
        total = self.share(partial, length, 0, 0).astype(f32)
        for team in range(self.t_n):
            for flip in (0, 1):
                if (team, flip) != (0, 0):
                    sent = self.share(partial, length, flip, team).astype(bf16)
                    total = total + self.move(
                        sent, lambda q, c, s, t: (q, c ^ flip, s, (t + team) % self.t_n)
                    ).astype(f32)
        return total

    def sum_team(self, partial):
        total = partial.astype(f32)
        total = total + self.to_core(partial).astype(f32)
        if self.t_n > 1:
            low = total.astype(bf16)
            for team in range(1, self.t_n):
                total = total + self.to_team(low, team).astype(f32)
        return total

    def spread_inner(self, own, one):
        both = jnp.concatenate([own, one], axis=1)
        return self.move(both, lambda q, c, s, t: (q, c, s ^ 3, t) if s in (1, 2) else None)

    def spread_outer(self, inner):
        return self.move(inner, lambda q, c, s, t: (q, c, s ^ 1, t) if s in (1, 2) else None)

    def spread_pair(self, inner, outer):
        size = inner.shape[1] // 2
        turned = jnp.concatenate([inner[:, size:], inner[:, :size]], axis=1)
        return jnp.where((self.s == 1) | (self.s == 2), turned, outer)

    def fold_outer(self, far):
        return self.move(far, lambda q, c, s, t: (q, c, s ^ 1, t) if s in (0, 3) else None)

    def fold_add(self, far, got):
        size = far.shape[1] // 2
        turned = jnp.concatenate([got[:, size:], got[:, :size]], axis=1)
        return (far.astype(f32) + turned.astype(f32)).astype(bf16)

    def fold_inner(self, far):
        return self.move(far, lambda q, c, s, t: (q, c, s ^ 3, t) if s in (1, 2) else None)

    def bits_from(self, first):
        return self.q_bits[first:] + self.q_bits[:first]

    def gather_chips(self, piece, first):
        pieces = {0: piece}
        for bit in self.bits_from(first):
            for k in list(pieces):
                pieces[k | bit] = self.to_chip(pieces[k], bit)
        return [pieces[k] for k in range(self.q_n)]

    def gather_start(self, piece):
        return {bit: self.to_chip(piece, bit) for bit in self.q_bits}

    def gather_end(self, piece, near, first):
        pieces = {0: piece}
        for bit in self.bits_from(first):
            for k in list(pieces):
                pieces[k | bit] = near[bit] if k == 0 else self.to_chip(pieces[k], bit)
        return [pieces[k] for k in range(self.q_n)]

    def scatter_order(self, first):
        order = [0]
        for bit in reversed(self.bits_from(first)):
            order = order + [k | bit for k in order]
        return order

    def sum_plane(self, values):
        values = values + self.to_core(values)
        for low in range(0, len(self.q_bits), 2):
            bits = self.q_bits[low : low + 2]
            got = [self.to_chip(values, bit) for bit in bits]
            if len(bits) == 2:
                both = self.to_chip(values, bits[0] | bits[1])
                values = (values + got[0]) + (got[1] + both)
            else:
                values = values + got[0]
        return values

    def sum_column(self, values):
        bit, bits = 1, []
        while bit < self.mp_n:
            bits.append(bit)
            bit *= 2

        def flip(mask):
            def target(q, c, s, t):
                place = (s * self.t_n + t) ^ mask
                return (q, c, place // self.t_n, place % self.t_n)

            return self.move(values, target)

        for low in range(0, len(bits), 2):
            pair = bits[low : low + 2]
            if len(pair) == 2:
                one, two, both = flip(pair[0]), flip(pair[1]), flip(pair[0] | pair[1])
                values = (values + one) + (two + both)
            else:
                values = values + flip(pair[0])
        return values


class ChipSum:
    def __init__(self, at, halves, first):
        self.at = at
        self.bits = list(at.bits_from(first))
        self.parts, sent = [halves[0]], halves[1]
        self.exchange(sent)

    def exchange(self, sent):
        self.got = self.at.to_chip(sent, self.bits.pop(0))
        self.parts.append(self.got)

    def total(self, rows=None):
        total = self.parts[0][rows].astype(f32) if rows else self.parts[0].astype(f32)
        for part in self.parts[1:]:
            total = total + (part[rows] if rows else part).astype(f32)
        return total

    def step(self, *others):
        if not self.bits:
            return
        self.parts[-1] = after(self.parts[-1], *others)
        half = self.got.shape[0] // 2
        sent = self.total(slice(half, None)).astype(bf16)
        self.parts = [part[:half] for part in self.parts]
        self.exchange(sent)

    def rest(self, *others):
        while self.bits:
            self.step(*others)


def pack_attn_kernel(place_ref, qkv_ref, out_ref, qkv_full, out_full, piece_ref):
    size = qkv_ref.shape[2]
    for j in range(3):
        qkv_full[:, j * size : (j + 1) * size] = qkv_ref[j].astype(bf16)
    out_full[...] = out_ref[...].T.astype(bf16)

    @pl.when(pl.program_id(0) == 0)
    def _():
        piece_ref[:, : 3 * size] = qkv_full[...]
        piece_ref[:, 3 * size :] = out_full[...]


def pack_mlp_kernel(place_ref, up_ref, down_ref, up_full, down_full, up_piece, down_piece):
    up_full[...] = up_ref[...].astype(bf16)
    down_full[...] = down_ref[...].T.astype(bf16)

    @pl.when(pl.program_id(0) == 0)
    def _():
        up_piece[...] = up_full[...]
        down_piece[...] = down_full[...]


def packs_in_kernels(at, width, head_width):
    return (width // at.q_n) % 128 == 0 and head_width % 128 == 0


def pack_attn(at, qkv_weight, out_weight, head_width, after):
    width = qkv_weight.shape[0]
    part = width // at.q_n
    if packs_in_kernels(at, width, head_width):
        place = tie(jnp.stack([at.q, at.c]).astype(jnp.int32), after)[0]
        sizes = (3 * head_width, head_width)
        return pl.pallas_call(
            pack_attn_kernel,
            grid_spec=pltpu.PrefetchScalarGridSpec(
                num_scalar_prefetch=1,
                grid=(at.q_n,),
                in_specs=[
                    pl.BlockSpec((3, part, head_width), lambda k, p: (0, p[0] ^ k, p[1])),
                    pl.BlockSpec((head_width, part), lambda k, p: (p[1], p[0] ^ k)),
                ],
                out_specs=tuple(pl.BlockSpec((part, n), lambda k, p: (k, 0)) for n in sizes)
                + (pl.BlockSpec((part, sum(sizes)), lambda k, p: (0, 0)),),
            ),
            out_shape=tuple(jax.ShapeDtypeStruct((width, n), bf16) for n in sizes)
            + (jax.ShapeDtypeStruct((part, sum(sizes)), bf16),),
            name="pack_attn",
        )(place, jnp.transpose(qkv_weight, (1, 0, 2)), out_weight)
    qkv = lax.dynamic_slice_in_dim(qkv_weight, at.c * head_width, head_width, 2)
    out = lax.dynamic_slice_in_dim(out_weight, at.c * head_width, head_width, 0)
    qkv = at.relative(qkv.reshape(width, 3 * head_width).astype(bf16), 0)
    out = at.relative(out.astype(bf16).T, 0)
    return qkv, out, jnp.concatenate([qkv[:part], out[:part]], axis=1)


def pack_mlp(at, up_weight, down_weight, head_width, units, after):
    width = up_weight.shape[0]
    part = width // at.q_n
    if packs_in_kernels(at, width, head_width):
        place = tie(jnp.stack([at.q, at.c]).astype(jnp.int32), after)[0]
        return pl.pallas_call(
            pack_mlp_kernel,
            grid_spec=pltpu.PrefetchScalarGridSpec(
                num_scalar_prefetch=1,
                grid=(at.q_n,),
                in_specs=[
                    pl.BlockSpec((part, units), lambda k, p: (p[0] ^ k, p[1])),
                    pl.BlockSpec((units, part), lambda k, p: (p[1], p[0] ^ k)),
                ],
                out_specs=(
                    pl.BlockSpec((part, units), lambda k, p: (k, 0)),
                    pl.BlockSpec((part, units), lambda k, p: (k, 0)),
                    pl.BlockSpec((part, units), lambda k, p: (0, 0)),
                    pl.BlockSpec((part, units), lambda k, p: (0, 0)),
                ),
            ),
            out_shape=(jax.ShapeDtypeStruct((width, units), bf16),) * 2
            + (jax.ShapeDtypeStruct((part, units), bf16),) * 2,
            name="pack_mlp",
        )(place, up_weight, down_weight)
    up = lax.dynamic_slice_in_dim(up_weight, at.c * units, units, 1).astype(bf16)
    down = lax.dynamic_slice_in_dim(down_weight, at.c * units, units, 0).astype(bf16).T
    up, down = at.relative(up, 0), at.relative(down, 0)
    return up, down, up[:part], down[:part]


def join_kernel(plan, count, *refs):
    pieces, outs = refs[:count], refs[count:]
    for out_ref, (start_cols, rows) in zip(outs, plan):
        part = out_ref.shape[0] // len(rows)
        for k, chunks in enumerate(rows):
            col = 0
            for index, start, size in chunks:
                out_ref[k * part : (k + 1) * part, col : col + size] = pieces[index][
                    :part, start : start + size
                ]
                col += size


def join(pieces, part, plans):
    shapes = [
        jax.ShapeDtypeStruct((part * len(rows), sum(size for _, _, size in rows[0])), bf16)
        for rows in plans
    ]
    return pl.pallas_call(
        lambda *refs: join_kernel([(0, rows) for rows in plans], len(pieces), *refs),
        in_specs=[in_vmem] * len(pieces),
        out_specs=(in_vmem,) * len(plans),
        out_shape=tuple(shapes),
        compiler_params=pltpu.CompilerParams(vmem_limit_bytes=kernel_bytes),
        name="join",
    )(*pieces)


def gelu_parts(values):
    half = 0.5 * (1.0 + lax.erf(values * (0.5**0.5)))
    bell = jnp.exp(-0.5 * values * values) * 0.3989422804014327
    return (values * half, half + values * bell)


def row_tiles(rows, tile=256):
    tile = min(tile, rows)
    return [slice(start, start + tile) for start in range(0, rows, tile)]


def sum_nt_kernel(count, *refs):
    lefts, rights, out_ref = refs[:count], refs[count : 2 * count], refs[-1]
    for here in row_tiles(out_ref.shape[0]):
        total = dot_nt(lefts[0][here, :], rights[0][...])
        for left, right in zip(lefts[1:], rights[1:]):
            total = total + dot_nt(left[here, :], right[...])
        out_ref[here, :] = total.astype(bf16)


def cost_of(flops):
    return pl.CostEstimate(flops=flops // 2, bytes_accessed=1 << 20, transcendentals=0)


def sum_nt(lefts, rights):
    rows, width = lefts[0].shape[0], rights[0].shape[0]
    return pl.pallas_call(
        lambda *refs: sum_nt_kernel(len(lefts), *refs),
        in_specs=[in_vmem] * (2 * len(lefts)),
        out_specs=in_vmem,
        out_shape=jax.ShapeDtypeStruct((rows, width), bf16),
        compiler_params=pltpu.CompilerParams(vmem_limit_bytes=kernel_bytes),
        cost_estimate=cost_of(2 * rows * width * sum(v.shape[1] for v in lefts)),
        name="sum_nt",
    )(*lefts, *rights)


def up_kernel(normed_ref, weight_ref, bias_ref, act_ref, slope_ref):
    for here in row_tiles(act_ref.shape[0]):
        pre = dot_nn(normed_ref[here, :], weight_ref[...]) + bias_ref[...]
        act, slope = gelu_parts(pre)
        act_ref[here, :] = act.astype(bf16)
        slope_ref[here, :] = slope


def up_project(normed, weight, bias):
    rows, cols = normed.shape[0], weight.shape[1]
    return pl.pallas_call(
        up_kernel,
        in_specs=[in_vmem] * 3,
        out_specs=(in_vmem, in_vmem),
        out_shape=(
            jax.ShapeDtypeStruct((rows, cols), bf16),
            jax.ShapeDtypeStruct((rows, cols), f32),
        ),
        compiler_params=pltpu.CompilerParams(vmem_limit_bytes=kernel_bytes),
        cost_estimate=cost_of(2 * rows * cols * normed.shape[1]),
        name="up_project",
    )(normed, weight, bias[None, :])


def down_back_kernel(kept_ref, weight_ref, slope_ref, pre_ref, bias_ref):
    total = None
    for here in row_tiles(pre_ref.shape[0]):
        grad = (dot_nn(kept_ref[here, :], weight_ref[...]) * slope_ref[here, :]).astype(bf16)
        pre_ref[here, :] = grad
        part = jnp.sum(grad.astype(f32), axis=0, keepdims=True)
        total = part if total is None else total + part
    bias_ref[...] = total


def down_back(kept, weight, slope):
    rows, cols = slope.shape
    pre, bias = pl.pallas_call(
        down_back_kernel,
        in_specs=[in_vmem] * 3,
        out_specs=(in_vmem, in_vmem),
        out_shape=(
            jax.ShapeDtypeStruct((rows, cols), bf16),
            jax.ShapeDtypeStruct((1, cols), f32),
        ),
        compiler_params=pltpu.CompilerParams(vmem_limit_bytes=kernel_bytes),
        cost_estimate=cost_of(2 * rows * cols * kept.shape[1]),
        name="down_back",
    )(kept, weight, slope)
    return pre, bias[0]


def halves_kernel(order, shape, *refs):
    operands, (kept_ref, sent_ref) = refs[:-2], refs[-2:]
    part = operands[0].shape[1] // len(order)
    middle = len(order) // 2
    for index, block in enumerate(order):
        target = kept_ref if index < middle else sent_ref
        rows = slice(index % middle * part, (index % middle + 1) * part)
        col = 0
        number = 0
        for count in shape:
            left = operands[number][:, block * part : (block + 1) * part]
            number += 1
            for _ in range(count):
                right_ref = operands[number]
                number += 1
                size = right_ref.shape[1]
                target[rows, col : col + size] = dot_tn(left, right_ref[...]).astype(bf16)
                col += size


def grad_halves(at, pairs, first):
    rows, width = pairs[0][0].shape
    part = width // at.q_n
    order = at.scatter_order(first)
    middle = at.q_n // 2
    cols = sum(right.shape[1] for _, rights in pairs for right in rights)
    if part % 128 == 0:
        halves = jax.ShapeDtypeStruct((middle * part, cols), bf16)
        operands = [value for left, rights in pairs for value in (left, *rights)]
        return pl.pallas_call(
            lambda *refs: halves_kernel(order, [len(rights) for _, rights in pairs], *refs),
            in_specs=[in_vmem] * len(operands),
            out_specs=(in_vmem, in_vmem),
            out_shape=(halves, halves),
            compiler_params=pltpu.CompilerParams(vmem_limit_bytes=kernel_bytes),
            cost_estimate=pl.CostEstimate(
                flops=rows * width * cols, bytes_accessed=1 << 20, transcendentals=0
            ),
            name="grad_halves",
        )(*operands)
    return tuple(
        jnp.concatenate(
            [
                jnp.concatenate(
                    [
                        dot_tn(left[:, k * part : (k + 1) * part], right).astype(bf16)
                        for left, rights in pairs
                        for right in rights
                    ],
                    axis=1,
                )
                for k in side
            ],
            axis=0,
        )
        for side in (order[:middle], order[middle:])
    )


def adjust(weight, first, second, gradient, decay_rate, first_fix, second_fix):
    first_new = 0.9 * first + 0.1 * gradient
    second_new = 0.999 * second + 0.001 * gradient * gradient
    update = (
        first_new / first_fix / (jnp.sqrt(second_new / second_fix) + adam_eps) + decay_rate * weight
    )
    return (first_new, second_new, update)


def in_order(c, mine, other):
    return jnp.where(c == 0, mine, other), jnp.where(c == 0, other, mine)


def adjust_into(
    index, weight, moments_ref, gradient, fixes_ref, state_ref, update_ref, own_ref, sums_ref
):
    own_ref[...] = weight
    first_new, second_new, update = adjust(
        weight, moments_ref[0], moments_ref[1], gradient, weight_decay, fixes_ref[0], fixes_ref[1]
    )
    state_ref[0] = first_new
    state_ref[1] = second_new
    update_ref[...] = update
    sums_ref[2 * index] = jnp.sum(weight * weight)
    sums_ref[2 * index + 1] = jnp.sum(update * update)


def adjust_attn_kernel(
    place_ref, fixes_ref, mine_ref, other_ref, qkv_ref, out_ref, qkv_moments, out_moments,
    qkv_state, out_state, qkv_update, out_update, qkv_own, out_own, sums_ref,
):
    size = qkv_ref.shape[2] // 2
    one, two = in_order(place_ref[1], mine_ref[...], other_ref[...])
    parts = [
        jnp.concatenate([one[:, j * size : (j + 1) * size], two[:, j * size : (j + 1) * size]], 1)
        for j in range(4)
    ]
    adjust_into(
        0, qkv_ref[...], qkv_moments, jnp.stack(parts[:3]), fixes_ref,
        qkv_state, qkv_update, qkv_own, sums_ref,
    )
    adjust_into(
        1, out_ref[...], out_moments, parts[3].T, fixes_ref,
        out_state, out_update, out_own, sums_ref,
    )


def adjust_mlp_kernel(
    place_ref, fixes_ref, mine_ref, other_ref, up_ref, down_ref, up_moments, down_moments,
    up_state, down_state, up_update, down_update, up_own, down_own, sums_ref,
):
    size = up_ref.shape[1] // 2
    one, two = in_order(place_ref[1], mine_ref[...], other_ref[...])
    down_grad = jnp.concatenate([one[:, :size], two[:, :size]], axis=1)
    up_grad = jnp.concatenate([one[:, size:], two[:, size:]], axis=1)
    adjust_into(
        0, up_ref[...], up_moments, up_grad, fixes_ref, up_state, up_update, up_own, sums_ref
    )
    adjust_into(
        1, down_ref[...], down_moments, down_grad.T, fixes_ref,
        down_state, down_update, down_own, sums_ref,
    )


def own_spec(shape, dim, count):
    block = list(shape)
    block[dim] //= count
    return pl.BlockSpec(
        tuple(block), lambda i, p: tuple(p[0] if d == dim else 0 for d in range(len(shape)))
    )


def whole_spec(shape):
    return pl.BlockSpec(shape, lambda i, p: (0,) * len(shape))


def adjust_pair(at, kernel, place, fixes, mine, other, weights, dims, moments):
    parts = [m.shape[1:] for m in moments]
    shapes = [jax.ShapeDtypeStruct(m.shape, f32) for m in moments]
    shapes += [jax.ShapeDtypeStruct(p, f32) for p in parts] * 2
    return pl.pallas_call(
        kernel,
        grid_spec=pltpu.PrefetchScalarGridSpec(
            num_scalar_prefetch=1,
            grid=(1,),
            in_specs=[in_smem, whole_spec(mine.shape), whole_spec(other.shape)]
            + [own_spec(w.shape, d, at.dp_n) for w, d in zip(weights, dims)]
            + [whole_spec(m.shape) for m in moments],
            out_specs=tuple(whole_spec(s.shape) for s in shapes) + (in_smem,),
        ),
        out_shape=tuple(shapes) + (jax.ShapeDtypeStruct((4,), f32),),
        compiler_params=pltpu.CompilerParams(vmem_limit_bytes=back_bytes),
        name="adjust_pair",
    )(place, fixes, mine, other, *weights, *moments)


def adjust_small_kernel(
    fixes_ref, vec_grad, vec_moments, vec, bias_grad, bias_moments, bias, rel_grad, rel_moments,
    rel, vec_state, vec_new, weight_norms, update_norms, bias_state, bias_update, rel_state,
    rel_update, sums_ref,
):
    fixes = (fixes_ref[0], fixes_ref[1])
    first, second, update = adjust(
        vec[...], vec_moments[0], vec_moments[1], vec_grad[...], 0.0, *fixes
    )
    vec_state[0] = first
    vec_state[1] = second
    weight_norm = jnp.sqrt(jnp.sum(vec[...] * vec[...], axis=1, keepdims=True))
    update_norm = jnp.sqrt(jnp.sum(update * update, axis=1, keepdims=True))
    weight_norms[...] = weight_norm
    update_norms[...] = update_norm
    vec_new[...] = vec[...] - learn_rate * (weight_norm / (update_norm + adam_eps)) * update
    first, second, update = adjust(
        bias[...], bias_moments[0:1, :], bias_moments[1:2, :], bias_grad[...], 0.0, *fixes
    )
    bias_state[0:1, :] = first
    bias_state[1:2, :] = second
    bias_update[...] = update
    sums_ref[0] = jnp.sum(bias[...] * bias[...])
    sums_ref[1] = jnp.sum(update * update)
    first, second, update = adjust(
        rel[...], rel_moments[0], rel_moments[1], rel_grad[...], 0.0, *fixes
    )
    rel_state[0] = first
    rel_state[1] = second
    rel_update[...] = update
    sums_ref[2] = jnp.sum(rel[...] * rel[...])
    sums_ref[3] = jnp.sum(update * update)


def adjust_small(fixes, vec, bias, rel):
    shape = jax.ShapeDtypeStruct
    rows = vec[2].shape[0]
    return pl.pallas_call(
        adjust_small_kernel,
        in_specs=[in_smem] + [in_vmem] * 9,
        out_specs=(in_vmem,) * 8 + (in_smem,),
        out_shape=(
            shape(vec[1].shape, f32),
            shape(vec[2].shape, f32),
            shape((rows, 1), f32),
            shape((rows, 1), f32),
            shape(bias[1].shape, f32),
            shape(bias[2].shape, f32),
            shape(rel[1].shape, f32),
            shape(rel[2].shape, f32),
            shape((4,), f32),
        ),
        name="adjust_small",
    )(fixes, *vec, *bias, *rel)


def apply_kernel(rates_ref, *refs):
    count = len(refs) // 3
    for index in range(count):
        refs[2 * count + index][...] = (
            refs[index][...] - rates_ref[index] * refs[count + index][...]
        )


def apply_updates(rates, weights, updates):
    return pl.pallas_call(
        apply_kernel,
        in_specs=[in_smem] + [in_vmem] * (2 * len(updates)),
        out_specs=(in_vmem,) * len(updates),
        out_shape=tuple(jax.ShapeDtypeStruct(u.shape, f32) for u in updates),
        compiler_params=pltpu.CompilerParams(vmem_limit_bytes=kernel_bytes),
        name="apply_updates",
    )(rates, *weights, *updates)


def norm_parts(values):
    center = values - jnp.mean(values, axis=-1, keepdims=True)
    spread = jnp.mean(center * center, axis=-1, keepdims=True)
    inverse = lax.rsqrt(spread + norm_eps)
    return (center * inverse, inverse)


def norm_back(upstream, normed, inverse, gain_vec):
    scaled = upstream * gain_vec
    return inverse * (
        scaled
        - jnp.mean(scaled, axis=-1, keepdims=True)
        - normed * jnp.mean(scaled * normed, axis=-1, keepdims=True)
    )


def local(
    tokens,
    cotangent,
    lengths,
    buckets,
    step_count,
    qkv_weight,
    out_weight,
    up_weight,
    down_weight,
    up_bias,
    rel_bias,
    norm_vectors,
    qkv_moments,
    out_moments,
    up_moments,
    down_moments,
    bias_moments,
    rel_moments,
    vector_moments,
):
    per, length_rows, width = tokens.shape
    at = Places(per)
    seq_len = length_rows * at.mp_n
    blocks = at.slots
    q_n, c, q = at.q_n, at.c, at.q
    head_width = out_weight.shape[0] // 2
    heads = head_width // HD
    units = up_weight.shape[1] // 2
    bucket_count, local_heads = rel_bias.shape

    other_lengths = at.to_core(lengths)
    all_lengths = jnp.where(
        c == 0,
        jnp.concatenate([lengths, other_lengths]),
        jnp.concatenate([other_lengths, lengths]),
    )
    length = lax.dynamic_slice_in_dim(all_lengths, at.s, 1, 0)
    row_keep = jnp.arange(seq_len)[:, None] < length[0]
    row_mask = row_keep.astype(f32)
    vectors = at.relative(norm_vectors, 1)

    def half(values, dim, size):
        return lax.dynamic_slice_in_dim(values, c * size, size, dim)

    part = width // q_n
    small_own = jnp.concatenate(
        [half(up_bias, 0, units), half(rel_bias, 1, heads).T.reshape(-1)]
    )
    qkv_cols = 3 * head_width
    attn_cols = 4 * head_width
    high = lax.reduce_precision(small_own, 8, 7)
    rest = small_own - high
    mid = lax.reduce_precision(rest, 8, 7)
    three = jnp.concatenate([high, mid, rest - mid]).astype(bf16)
    small_rows = -(-three.size // (16 * attn_cols)) * 16
    three = jnp.pad(three, (0, small_rows * attn_cols - three.size)).reshape(small_rows, attn_cols)

    def small_of(rows_low):
        flat = rows_low.reshape(-1).astype(f32)
        count = small_own.size
        return (flat[:count] + flat[count : 2 * count]) + flat[2 * count : 3 * count]

    tokens_near = at.relative(tokens, 2)
    token_pieces = {step: at.collect_piece(tokens_near, step) for step in (0, 2, 3, 1)}
    qkv_own, out_own, attn_piece = pack_attn(
        at, qkv_weight, out_weight, head_width, tokens_near
    )
    attn_piece = jnp.concatenate([attn_piece, three], axis=0)
    attn_one = at.to_slot(attn_piece, 1)
    up_own, down_own, up_piece, down_piece = pack_mlp(
        at, up_weight, down_weight, head_width, units, attn_piece
    )
    mlp_piece = jnp.concatenate([up_piece, down_piece], axis=1)
    attn_one = after(attn_one, token_pieces[1], mlp_piece)
    attn_inner = at.spread_inner(attn_piece, attn_one)
    attn_near = at.gather_start(attn_one[:part])
    tokens_there = (after(token_pieces[2], attn_one), token_pieces[3])
    token_pieces[2] = tokens_there[0]
    mlp_one = at.to_slot(after(mlp_piece, *tokens_there), 1)
    inputs_home = at.collect_end([token_pieces[k] for k in range(blocks)])
    attn_pieces = at.gather_end(
        attn_one[:part], {b: after(v, *tokens_there) for b, v in attn_near.items()}, 0
    )
    inputs_low = at.collect_both(inputs_home)
    inputs_low = after(inputs_low, attn_inner, *attn_pieces)
    attn_outer = at.spread_outer(attn_inner)
    up_one, down_one = mlp_one[:, :units], mlp_one[:, units:]
    up_inner = at.spread_inner(up_piece, up_one)
    mlp_near = at.gather_start(mlp_one)
    turn = 1 % len(at.q_bits)
    attn_pair = at.spread_pair(attn_inner, attn_outer)
    pair_first = after(attn_pair[:part], *mlp_near.values(), up_inner)
    small = [
        small_own,
        small_of(attn_one[part:]),
        small_of(attn_pair[part:, :attn_cols]),
        small_of(attn_pair[part:, attn_cols:]),
    ]
    tile = tile_of(seq_len)
    tiles = seq_len // tile
    padded = jnp.concatenate([jnp.zeros((tile,), jnp.int32), buckets])
    spread = jnp.concatenate(
        [padded[kk * tile : (kk + 2) * tile] for kk in range(tiles)]
    )
    choose = (jnp.arange(bucket_count, dtype=jnp.int32)[:, None] == spread[None, :]).astype(f32)

    def lines_of(r):
        rel_rows = small[r][units:].reshape(heads, bucket_count)
        return jnp.dot(rel_rows, choose, precision=lax.Precision.HIGHEST)


    columns = range(q_n)
    qkv_one, out_one = join(
        attn_pieces,
        part,
        [
            [[(k, 0, qkv_cols)] for k in columns],
            [[(k, qkv_cols, head_width)] for k in columns],
        ],
    )
    qkv_w, out_w = [qkv_own, qkv_one], [out_own, out_one]

    first_parts = norm_parts(inputs_low.astype(f32))
    first_normed, first_inverse = first_parts
    first_low = (first_normed * vectors[0] + vectors[1]).astype(bf16)
    qkv, contexts, totals = [], [], []

    def attention(r, *others):
        qkv.append(after(dot_nn(first_low, qkv_w[r]).astype(bf16), *others))
        context, total = attend(length, qkv[r], lines_of(r), heads)
        contexts.append(context)
        totals.append(total)

    attention(0, mlp_one)
    pair_first = after(pair_first, contexts[0])
    pair_near = at.gather_start(pair_first)
    up_outer = at.spread_outer(after(up_inner, *mlp_near.values()))
    down_inner = at.spread_inner(after(down_piece, up_inner, *mlp_near.values()), down_one)
    attention(1, attn_outer)
    near_done = (*pair_near.values(), up_outer, down_inner)
    pair_near = {b: after(v, *near_done, contexts[1]) for b, v in pair_near.items()}
    pair_pieces = []
    for k in range(2):
        cols = slice(k * attn_cols, (k + 1) * attn_cols)
        pair_pieces.append(
            at.gather_end(
                pair_first[:, cols], {b: v[:, cols] for b, v in pair_near.items()}, k * turn
            )
        )
    down_outer = at.spread_outer(after(down_inner, *near_done))
    incoming_near = at.relative(after(cotangent, *near_done), 2)
    incoming_pieces = {step: at.collect_piece(incoming_near, step) for step in (2, 3)}
    pair_done = [v for pieces in pair_pieces for v in pieces[1:]]
    mlp_near = {b: after(v, *pair_done) for b, v in mlp_near.items()}
    up_one_pieces = at.gather_end(up_one, {b: v[:, :units] for b, v in mlp_near.items()}, 0)
    down_one_pieces = at.gather_end(
        down_one, {b: v[:, units:] for b, v in mlp_near.items()}, turn
    )
    one_done = (*up_one_pieces, *down_one_pieces, down_outer)
    up_pair = after(at.spread_pair(up_inner, up_outer), *one_done)
    up_near = at.gather_start(up_pair)
    incoming_near = after(incoming_near, *one_done)
    incoming_pieces.update({step: at.collect_piece(incoming_near, step) for step in (0, 1)})
    down_pair = after(at.spread_pair(down_inner, down_outer), *up_near.values())

    def pair_halves(piece, near):
        halves = []
        for k in range(2):
            cols = slice(k * units, (k + 1) * units)
            halves.append(
                at.gather_end(piece[:, cols], {b: v[:, cols] for b, v in near.items()}, k * turn)
            )
        return halves

    def pair_join(halves):
        return join(
            halves[0] + halves[1], part, [[[(k, 0, units), (k + q_n, 0, units)] for k in columns]]
        )[0]

    up_halves = pair_halves(up_pair, up_near)
    down_near = at.gather_start(down_pair)
    down_near = {b: after(v, up_halves[0][-1], up_halves[1][-1]) for b, v in down_near.items()}
    down_halves = pair_halves(down_pair, down_near)
    joined = join(
        pair_pieces[0] + pair_pieces[1],
        part,
        [
            [[(k + half_at, start, size)] for k in columns]
            for half_at in (0, q_n)
            for start, size in ((0, qkv_cols), (qkv_cols, head_width))
        ],
    )
    qkv_w += joined[0::2]
    out_w += joined[1::2]
    attention(2, *one_done)
    attention(3, *up_near.values())
    incoming_home = at.collect_end([incoming_pieces[k] for k in range(blocks)])
    rows_of = [[(k, 0, units)] for k in columns]
    up_w = [up_own, join(up_one_pieces, part, [rows_of])[0], pair_join(up_halves)]
    down_w = [down_own, join(down_one_pieces, part, [rows_of])[0], pair_join(down_halves)]

    inputs = inputs_low.astype(f32)
    mixed = at.sum_team(sum_nt(contexts, out_w))
    mixed = after(mixed, *up_near.values())
    middle = inputs + (mixed + vectors[4]) * row_mask
    second_normed, second_inverse = norm_parts(middle)
    second_low = (second_normed * vectors[2] + vectors[3]).astype(bf16)
    acts, slopes = [], []
    biases = [small[0][:units], small[1][:units], jnp.concatenate([small[2][:units], small[3][:units]])]
    for r in range(3):
        act, slope = up_project(second_low, up_w[r], biases[r])
        acts.append(act)
        slopes.append(slope)
    incoming_low = at.collect_both(incoming_home)
    kept = jnp.where(row_keep, incoming_low, jnp.zeros_like(incoming_low))
    fed_bias_grad = jnp.sum(kept.astype(f32), axis=0)
    bias_grads = [None] * blocks

    pre_pair, bias_pair = down_back(kept, down_w[2], slopes[2])
    bias_grads[2], bias_grads[3] = bias_pair[:units], bias_pair[units:]
    up_far_halves = grad_halves(at, [(second_low, [pre_pair])], 1)
    up_far = ChipSum(at, up_far_halves, 1)
    down_far_halves = grad_halves(at, [(after(kept, *up_far_halves), [acts[2]])], 0)
    down_far = ChipSum(at, down_far_halves, 0)
    down_near_halves = grad_halves(at, [(after(kept, *down_far_halves), acts[:2])], 0)
    fed_low = sum_nt([after(acts[0], *down_far_halves)] + acts[1:], down_w)
    fed_share = at.sum_share(fed_low, length_rows)
    middle_share = at.share(middle, length_rows, 0, 0)
    mask_share = at.share(row_mask, length_rows, 0, 0)
    out_share = (middle_share + (fed_share + vectors[5]) * mask_share).astype(bf16)
    out_got = at.deliver_first(out_share)
    kept_late = after(kept, fed_low, *down_far_halves)
    pre_own, bias_grads[0] = down_back(kept_late, down_w[0], slopes[0])
    pre_one, bias_grads[1] = down_back(kept_late, down_w[1], slopes[1])
    back_low = sum_nt([pre_own, pre_one, pre_pair], up_w)
    up_near_halves = grad_halves(at, [(after(second_low, back_low), [pre_own, pre_one])], 1)
    second_grad = at.sum_team(back_low)
    second_grad = after(second_grad, *up_near_halves)
    lead = jnp.where((c == 0) & (at.t == 0), 1.0, 0.0)
    gain_two = jnp.sum(second_grad * second_normed, axis=0)
    shift_two = jnp.sum(second_grad, axis=0)
    middle_grad = incoming_low.astype(f32) + norm_back(
        second_grad, second_normed, second_inverse, vectors[2]
    )
    branch = jnp.where(row_keep, middle_grad, 0.0).astype(bf16)
    mix_bias_grad = jnp.sum(branch.astype(f32), axis=0)
    rel_grads = [None] * blocks
    branch = after(branch, up_far.got, down_far.got)
    context_grads = [dot_nn(branch, out_w[r]).astype(bf16) for r in range(blocks)]
    own_cols = slice(0, units)
    far_cols = slice(units, 2 * units)
    attn_sums = [None] * blocks
    attn_halves = [None] * blocks
    proj_grads = [None] * blocks
    for r in reversed(range(blocks)):
        context_grad = context_grads[r]
        if r == 3:
            there = (up_far.got, down_far.got)
            up_far.rest(*there)
            down_far.rest(*there)
        if r == 2:
            far_done = (up_far.got, down_far.got)
            context_grad = after(context_grad, *far_done)
            down_near_sum = ChipSum(at, [after(v, *far_done) for v in down_near_halves], 0)
            up_near_sum = ChipSum(at, [after(v, *far_done) for v in up_near_halves], 1)
            far_sums = (down_far.total(), up_far.total())
            mlp_far = jnp.concatenate(
                [v[:, cols] for cols in (own_cols, far_cols) for v in far_sums], axis=1
            ).astype(bf16)
            far_got = at.fold_outer(mlp_far)
        if r == 1:
            context_grad = after(context_grad, out_got)
        if r == 0:
            near_firsts = (down_near_sum.got, up_near_sum.got)
            context_grad = after(context_grad, *near_firsts, far_got)
            mlp_far = at.fold_add(mlp_far, after(far_got, *near_firsts))
            down_near_sum.rest(*near_firsts)
            up_near_sum.rest(*near_firsts)
            near_done = (down_near_sum.got, up_near_sum.got)
        proj_grad, dist = attend_back(
            length, qkv[r], lines_of(r), totals[r], context_grad, heads
        )
        rel_grads[r] = dist
        if r == 0:
            proj_grad = after(proj_grad, *near_done)
        attn_halves[r] = grad_halves(
            at, [(first_low, [proj_grad]), (branch, [contexts[r]])], r % 2
        )
        proj_grads[r] = proj_grad
    back_low = sum_nt(proj_grads, qkv_w)
    inner_got = at.fold_inner(after(mlp_far, back_low))
    out_pair = at.deliver_pair(out_share, after(out_got, far_got, back_low))
    out_last = at.deliver_last(out_pair)
    for k in (3, 2):
        attn_sums[k] = ChipSum(at, [after(v, *near_done) for v in attn_halves[k]], k % 2)
    firsts = (attn_sums[3].got, attn_sums[2].got)
    first_grad = at.sum_share(back_low, length_rows)
    for k in (3, 2):
        attn_sums[k].rest(*firsts)
    attn_far = jnp.concatenate([attn_sums[2].total(), attn_sums[3].total()], axis=1).astype(bf16)
    mlp_size = 2 * units
    mlp_near = (down_near_sum.total(), up_near_sum.total())
    mlp_one = jnp.concatenate([v[:, far_cols] for v in mlp_near], axis=1)
    mlp_own = jnp.concatenate([v[:, own_cols] for v in mlp_near], axis=1)
    mlp_one = (mlp_one + inner_got[:, :mlp_size].astype(f32)).astype(bf16)
    rel_grad = lax.dot_general(
        jnp.concatenate(rel_grads, axis=0),
        choose,
        (((1,), (1,)), ((), ())),
        precision=lax.Precision.HIGHEST,
    )
    normed_share = at.share(first_normed, length_rows, 0, 0)
    inverse_share = at.share(first_inverse, length_rows, 0, 0)
    middle_grad_share = at.share(middle_grad, length_rows, 0, 0)
    gain_one = jnp.sum(first_grad * normed_share, axis=0)
    shift_one = jnp.sum(first_grad, axis=0)
    input_share = middle_grad_share + norm_back(
        first_grad, normed_share, inverse_share, vectors[0]
    )
    input_low = input_share.astype(bf16)
    def by_place(rows_of):
        around = jnp.stack(rows_of)
        moved = []
        for place in range(blocks):
            picked = around[0]
            for k in range(1, blocks):
                picked = jnp.where(at.s ^ k == place, around[k], picked)
            moved.append(picked)
        moved = jnp.stack(moved)[:, None, None, :]
        here = (jnp.arange(at.t_n)[:, None] == at.t) & (jnp.arange(2)[None, :] == c)
        return jnp.where(here[None, :, :, None], moved, 0.0).reshape(at.mp_n, 2, -1)

    vector_grad = jnp.concatenate(
        [
            jnp.stack([gain_one, shift_one]),
            lead * jnp.stack([gain_two, shift_two, mix_bias_grad, fed_bias_grad]),
        ]
    )
    small_grad = by_place(
        [
            jnp.concatenate([bias_grads[r], rel_grad[r * heads : (r + 1) * heads].reshape(-1)])
            for r in range(blocks)
        ]
    )
    last_got = at.to_slot(mlp_one, 1)
    plane = at.sum_plane(
        jnp.concatenate([at.relative(vector_grad, 1).reshape(-1), small_grad.reshape(-1)])
    )
    there = (attn_sums[3].got, attn_sums[2].got, plane)
    for k in (1, 0):
        attn_sums[k] = ChipSum(at, [after(v, *there) for v in attn_halves[k]], k % 2)
    there = (attn_sums[1].got, attn_sums[0].got)
    for k in (1, 0):
        attn_sums[k].rest(*there)
    joined = at.sum_column(after(plane, last_got))
    input_got = at.deliver_first(after(input_low, joined))
    attn_got = at.fold_outer(after(attn_far, joined))
    mlp_mine = mlp_own + inner_got[:, mlp_size:].astype(f32) + last_got.astype(f32)
    attn_got = after(attn_got, attn_sums[0].got, attn_sums[1].got, input_got)
    rows = part // 2

    def exchanged(mine):
        sent = lax.dynamic_slice_in_dim(mine, (1 - c) * rows, rows, 0)
        return lax.dynamic_slice_in_dim(mine, c * rows, rows, 0), at.to_core(sent)

    mlp_mine, mlp_other = exchanged(mlp_mine)
    steps_done = step_count[0].astype(f32)
    first_fix = 1.0 - jnp.power(jnp.float32(0.9), steps_done)
    second_fix = 1.0 - jnp.power(jnp.float32(0.999), steps_done)
    fixes = jnp.stack([first_fix, second_fix])
    qkv_view = jnp.transpose(qkv_weight, (1, 0, 2))
    qkv_mom = jnp.transpose(qkv_moments, (0, 2, 1, 3))
    weights = [qkv_view, out_weight, up_weight, down_weight]
    dims = [1, 1, 0, 1]
    in_kernels = rows % 128 == 0
    if in_kernels:
        place = jnp.stack([at.dp_i, c]).astype(jnp.int32)
        up_state, down_state, up_update, down_update, up_mine, down_mine, mlp_squares = adjust_pair(
            at, adjust_mlp_kernel, place, fixes, mlp_mine, mlp_other,
            weights[2:], dims[2:], [up_moments, down_moments],
        )
        attn_got = after(attn_got, mlp_squares)
    attn_inner_got = at.fold_inner(at.fold_add(attn_far, attn_got))
    attn_one_sum = attn_inner_got[:, :attn_cols].astype(f32) + attn_sums[1].total()
    attn_last_got = at.to_slot(attn_one_sum.astype(bf16), 1)
    attn_mine = (
        attn_sums[0].total()
        + attn_inner_got[:, attn_cols:].astype(f32)
        + attn_last_got.astype(f32)
    )
    input_pair = at.deliver_pair(input_low, input_got)
    input_last = at.deliver_last(input_pair)
    input_grad = at.relative(at.delivered(input_pair, input_last), 2).astype(f32)
    vector_grad = joined[: vector_grad.size].reshape(vector_grad.shape)
    small_sum = lax.dynamic_index_in_dim(
        joined[vector_grad.size :].reshape(small_grad.shape), at.mp_i, 0, keepdims=False
    )
    bias_sum = small_sum[:, :units].reshape(1, -1)
    rel_sum = small_sum[:, units:].reshape(2 * heads, bucket_count).T

    attn_mine, attn_other = exchanged(attn_mine)

    if in_kernels:
        qkv_state, out_state, qkv_update, out_update, qkv_mine, out_mine, attn_squares = adjust_pair(
            at, adjust_attn_kernel, place, fixes, attn_mine, attn_other,
            weights[:2], dims[:2], [qkv_mom, out_moments],
        )
        squares = jnp.concatenate([attn_squares, mlp_squares])
        updates = [qkv_update, out_update, up_update, down_update]
        states = [qkv_state, out_state, up_state, down_state]
        own_weights = [qkv_mine, out_mine, up_mine, down_mine]
    else:
        one, two = in_order(c, attn_mine, attn_other)
        parts = [
            jnp.concatenate(
                [v[:, j * head_width : (j + 1) * head_width] for v in (one, two)], axis=1
            )
            for j in range(4)
        ]
        one, two = in_order(c, mlp_mine, mlp_other)
        grads = [
            jnp.stack(parts[:3]),
            parts[3].T,
            jnp.concatenate([one[:, units:], two[:, units:]], axis=1),
            jnp.concatenate([one[:, :units], two[:, :units]], axis=1).T,
        ]
        own_weights, updates, states, squares = [], [], [], []
        for weight, dim, moments, grad in zip(
            weights, dims, [qkv_mom, out_moments, up_moments, down_moments], grads
        ):
            count = weight.shape[dim] // at.dp_n
            weight = lax.dynamic_slice_in_dim(weight, at.dp_i * count, count, dim)
            first_new, second_new, update = adjust(
                weight, moments[0], moments[1], grad, weight_decay, first_fix, second_fix
            )
            own_weights.append(weight)
            updates.append(update)
            states.append(jnp.stack([first_new, second_new]))
            squares += [jnp.sum(weight * weight), jnp.sum(update * update)]
        squares = jnp.stack(squares)
    (
        vector_state, vector_new, vector_norms, vector_update_norms,
        bias_state, bias_update, rel_state, rel_update, small_squares,
    ) = adjust_small(
        fixes,
        (vector_grad, vector_moments, norm_vectors),
        (bias_sum, bias_moments, up_bias[None, :]),
        (rel_sum, rel_moments, rel_bias),
    )
    lead_dp = (at.dp_i == 0).astype(f32)
    squares = jnp.concatenate([squares, lead_dp * small_squares])
    squares = after(at.sum_plane(squares), input_last)
    squares = at.sum_column(squares).reshape(6, 2)
    norms = jnp.sqrt(squares)
    rates = learn_rate * (norms[:, 0] / (norms[:, 1] + adam_eps))
    small_weights = [up_bias[None, :], rel_bias]
    small_updates = [bias_update, rel_update]
    if in_kernels:
        *new, bias_new, rel_new = apply_updates(
            rates, own_weights + small_weights, updates + small_updates
        )
    else:
        new = [own_weights[k] - rates[k] * updates[k] for k in range(4)]
        bias_new, rel_new = apply_updates(rates[4:], small_weights, small_updates)
    new, states = list(new), list(states)
    new[0] = jnp.transpose(new[0], (1, 0, 2))
    states[0] = jnp.transpose(states[0], (0, 2, 1, 3))
    block_out = at.relative(at.delivered(out_pair, out_last), 2)
    results = [block_out, input_grad]
    for k in range(4):
        results += [new[k], states[k]]
    results += [bias_new[0], bias_state, rel_new, rel_state, vector_new, vector_state]
    results.append(
        jnp.concatenate(
            [norms, jnp.concatenate([vector_norms, vector_update_norms], axis=1)]
        ).T
    )
    return tuple(results)


def solution(mesh):
    return jax.shard_map(
        local,
        mesh=mesh,
        in_specs=(
            P("dp", "mp", None),
            P("dp", "mp", None),
            P("dp"),
            P(),
            P(),
            P(None, None, "mp"),
            P("mp", None),
            P(None, "mp"),
            P("mp", None),
            P("mp"),
            P(None, "mp"),
            P(),
            P(None, "dp", None, "mp"),
            P(None, "mp", "dp"),
            P(None, "dp", "mp"),
            P(None, "mp", "dp"),
            P(None, "mp"),
            P(None, None, "mp"),
            P(),
        ),
        out_specs=(
            P("dp", "mp", None),
            P("dp", "mp", None),
            P("dp", None, "mp"),
            P(None, "dp", None, "mp"),
            P("mp", "dp"),
            P(None, "mp", "dp"),
            P("dp", "mp"),
            P(None, "dp", "mp"),
            P("mp", "dp"),
            P(None, "mp", "dp"),
            P("mp"),
            P(None, "mp"),
            P(None, "mp"),
            P(None, None, "mp"),
            P(),
            P(),
            P(),
        ),
        check_vma=False,
    )
```
